32 devices in a mesh: fsdp: 2 (over y), ctx: 4 (over z), tp: 4 (over x, core).
Axes of the slice: x: 2, y: 2, z: 4, core: 2. Of those that a mesh axis runs over, the one named last changes fastest.
Arguments:
- block_in: bfloat16 [8, 2048, 768], P('fsdp', ('ctx', 'tp')), may hold values from -6 to 6
- segments: int32 [8, 2048], P('fsdp'), may hold values from 0 to 10, as said below
- ln1_gain: bfloat16 [768], P('fsdp'), may hold values from 0.5 to 1.5
- ln1_shift: bfloat16 [768], P('fsdp'), may hold values from -1 to 1
- w_qkv: bfloat16 [3, 768, 768], P(None, ('tp', 'fsdp')), may hold values from -0.21875 to 0.21875
- b_qv: bfloat16 [12, 128], P('tp', 'fsdp'), may hold values from -1.796875 to 1.796875
- w_out: bfloat16 [768, 768], P(('tp', 'fsdp')), may hold values from -0.875 to 0.875
- b_out: bfloat16 [768], P('fsdp'), may hold values from -1 to 1
- ln2_gain: bfloat16 [768], P('fsdp'), may hold values from 0.5 to 1.5
- ln2_shift: bfloat16 [768], P('fsdp'), may hold values from -1 to 1
- w_up: bfloat16 [768, 3072], P('fsdp', 'tp'), may hold values from -0.21875 to 0.21875
- b_up: bfloat16 [12, 256], P('tp', 'fsdp'), may hold values from -1.796875 to 1.796875
- w_down: bfloat16 [3072, 768], P(('tp', 'fsdp')), may hold values from -0.109375 to 0.109375
- b_down: bfloat16 [768], P('fsdp'), may hold values from -1 to 1
- cotangent: bfloat16 [8, 2048, 768], P('fsdp', ('ctx', 'tp')), may hold values from -6 to 6
Outputs:
- block_out: bfloat16 [8, 2048, 768], P('fsdp', ('ctx', 'tp'))
- grad_x: bfloat16 [8, 2048, 768], P('fsdp', ('ctx', 'tp'))
- grad_ln1_gain: float32 [768], P('fsdp')
- grad_ln1_shift: float32 [768], P('fsdp')
- grad_w_qkv: float32 [3, 768, 768], P(None, ('tp', 'fsdp'))
- grad_b_qv: float32 [12, 128], P('tp', 'fsdp')
- grad_w_out: float32 [768, 768], P(('tp', 'fsdp'))
- grad_b_out: float32 [768], P('fsdp')
- grad_ln2_gain: float32 [768], P('fsdp')
- grad_ln2_shift: float32 [768], P('fsdp')
- grad_w_up: float32 [768, 3072], P('fsdp', 'tp')
- grad_b_up: float32 [12, 256], P('tp', 'fsdp')
- grad_w_down: float32 [3072, 768], P(('tp', 'fsdp'))
- grad_b_down: float32 [768], P('fsdp')
The draws below stay inside these ranges and needn't reach their ends.
Inputs may be any that keep to these rules, and one draw needn't show every extreme that they name: `segments`: within each sequence the numbers start at 0 and never fall; positions with one number form one document. In each aligned block of 4 sequences, one sequence's first document covers at least its first 1793 positions; other documents are at least 204 long except a sequence's last one.
All inputs are finite; a program needn't handle non-finite values.
Results may differ from the reference program's by a relative error of at most 0.02.
Values may be sent and summed in bfloat16 or wider, within the bound.
No kernel may reach another device: no remote copies, remote signals or barrier semaphores. Data moves between devices by JAX's collectives and lax.ppermute only.
A program may use at most 256 MiB of HBM per device.

```python
import jax
import jax.numpy as jnp
from jax import lax

H = 12
HD = 64
D = 768
FF = 3072
SEQ_DEV = 512
SEQS = 4
SEQ_LEN = 2048
SEQ_COUNT = 8


def draw_segments(key, part):
    key = jax.random.fold_in(key, 11)
    gap_key, pick_key, long_key = jax.random.split(key, 3)
    pieces = 12
    least_gap = SEQ_LEN // 10
    gaps = jax.random.randint(gap_key, (SEQ_COUNT, pieces), least_gap, SEQ_LEN + 1)
    chosen = jax.random.randint(pick_key, (SEQ_COUNT // SEQS, 1), 0, SEQS)
    within = jnp.arange(SEQ_COUNT).reshape(SEQ_COUNT // SEQS, SEQS) % SEQS
    is_long = (within == chosen).reshape(SEQ_COUNT)
    is_dense = (within == (chosen + 1) % SEQS).reshape(SEQ_COUNT)
    gaps = jnp.where(is_dense[:, None], least_gap, gaps)
    first_gap = SEQ_LEN - jax.random.randint(long_key, (SEQ_COUNT,), 0, max(SEQ_DEV // 2, 1))
    gaps = gaps.at[:, 0].set(jnp.where(is_long, first_gap, gaps[:, 0]))
    bounds = jnp.cumsum(gaps, axis=1)
    places = jnp.arange(SEQ_LEN)
    return jnp.sum((bounds[:, None, :] <= places[None, :, None]).astype(jnp.int32), axis=2)


def shard_levels(rng, dims, cuts, smallest, top_value):
    def one(position, shards_of):
        steps = jax.random.uniform(jax.random.fold_in(jax.random.fold_in(rng, 6), position), (shards_of,), jnp.float32, smallest / len(cuts), top_value / len(cuts))
        return jnp.repeat(jnp.exp(steps), dims[position] // shards_of).reshape((-1,) + (1,) * (len(dims) - position - 1))

    loudness = one(*cuts[0])
    for cut in cuts[1:]:
        loudness = loudness * one(*cut)
    return loudness


def scatter_about(own_key, shape, scale, limit, shards=(), kind=jnp.bfloat16):
    gain = shard_levels(own_key, shape, shards, -0.22, 0.18) if shards else 1.0
    values = jax.random.normal(own_key, shape, jnp.float32) * scale * gain
    return jnp.minimum(jnp.maximum(values, -limit), limit).astype(kind)


def setup_inputs(seed: int = 0) -> dict:
    splits = jax.random.split(jax.random.key(seed), 16)
    return {
        "block_in": scatter_about(splits[0], (SEQ_COUNT, SEQ_LEN, D), 1.0, 6.0, ((0, 2), (1, 16))),
        "segments": draw_segments(jax.random.fold_in(splits[15], 71), 0),
        "ln1_gain": jnp.clip(1.0 + 0.1 * jax.random.normal(splits[2], (D,), jnp.float32), 0.5, 1.5).astype(jnp.bfloat16),
        "ln1_shift": scatter_about(splits[3], (D,), 0.2, 1.0, ((0, 2),)),
        "w_qkv": scatter_about(splits[4], (3, D, D), D ** -0.5, 0.21875, ((1, 8),)),
        "b_qv": scatter_about(splits[5], (H, 2 * HD), 0.3, 1.796875, ((0, 4), (1, 2))),
        "w_out": scatter_about(splits[6], (D, D), (D // 16) ** -0.5, 0.875, ((0, 8),)),
        "b_out": scatter_about(splits[7], (D,), 0.2, 1.0, ((0, 2),)),
        "ln2_gain": jnp.clip(1.0 + 0.1 * jax.random.normal(splits[8], (D,), jnp.float32), 0.5, 1.5).astype(jnp.bfloat16),
        "ln2_shift": scatter_about(splits[9], (D,), 0.2, 1.0, ((0, 2),)),
        "w_up": scatter_about(splits[10], (D, FF), D ** -0.5, 0.21875, ((0, 2), (1, 4))),
        "b_up": scatter_about(splits[11], (H, FF // H), 0.3, 1.796875, ((0, 4), (1, 2))),
        "w_down": scatter_about(splits[12], (FF, D), FF ** -0.5, 0.109375, ((0, 8),)),
        "b_down": scatter_about(splits[13], (D,), 0.2, 1.0, ((0, 2),)),
        "cotangent": scatter_about(splits[14], (SEQ_COUNT, SEQ_LEN, D), 1.0, 6.0, ((0, 2), (1, 16))),
    }


EPS = 1e-05
HIGH = lax.Precision.HIGHEST

@jax.custom_vjp
def low(v):
    return lax.optimization_barrier(v.astype(jnp.bfloat16)).astype(jnp.float32)

@jax.custom_vjp
def low_back(v):
    return v

def low_keep(v):
    return (low(v), None)

def low_pass(kept, grad):
    return (grad,)

def back_keep(v):
    return (v, None)

def back_low(kept, grad):
    return (low(grad),)
low.defvjp(low_keep, low_pass)
low_back.defvjp(back_keep, back_low)

def layer_norm(values, ln_gain, ln_shift):
    center = values - lax.optimization_barrier(jnp.mean(values, axis=-1, keepdims=True))
    spread = lax.optimization_barrier(jnp.mean(center * center, axis=-1, keepdims=True))
    return center * lax.rsqrt(spread + EPS) * ln_gain + ln_shift

def matmul_high(left, right):
    return jnp.dot(left, right, precision=HIGH, preferred_element_type=jnp.float32)

def forward(tokens, seg_ids, weights):
    gain_one, shift_one, qkv_mat, qv_bias, out_mat, out_bias, gain_two, shift_two, up_mat, up_bias, down_mat, down_bias = weights
    length = tokens.shape[0]
    normed_one = low(layer_norm(tokens, gain_one, shift_one))
    projected = matmul_high(normed_one, qkv_mat.reshape(3 * D, D).T).reshape(length, 3, H, HD)
    queries = low_back(low(projected[:, 0] + qv_bias[:, :HD]))
    keys_all = low_back(low(projected[:, 1]))
    values_all = low_back(low(projected[:, 2] + qv_bias[:, HD:]))
    places = jnp.arange(length)
    allowed = (seg_ids[:, None] == seg_ids[None, :]) & (places[None, :] <= places[:, None])

    def one_head(blocks):
        query_head, key_head, value_head = blocks
        scores = low_back(matmul_high(query_head, key_head.T) * HD ** (-0.5))
        scores = jnp.where(allowed, scores, -1e+30)
        peak_score = lax.optimization_barrier(jnp.max(scores, axis=-1, keepdims=True))
        exponent = jnp.exp(scores - peak_score)
        probs = exponent / lax.optimization_barrier(jnp.sum(exponent, axis=-1, keepdims=True))
        return matmul_high(low(probs), value_head)
    head_outs = lax.map(jax.checkpoint(one_head), (queries.transpose(1, 0, 2), keys_all.transpose(1, 0, 2), values_all.transpose(1, 0, 2)))
    merged = low_back(low(head_outs.transpose(1, 0, 2).reshape(length, D)))
    hidden = tokens + low_back(matmul_high(merged, out_mat)) + out_bias
    normed_two = low(layer_norm(hidden, gain_two, shift_two))
    pre_act = low_back(matmul_high(normed_two, up_mat) + up_bias.reshape(FF))
    activ = low(jax.nn.gelu(pre_act, approximate=True))
    return hidden + matmul_high(activ, down_mat) + down_bias

def reference(block_in, segments, ln1_gain, ln1_shift, w_qkv, b_qv, w_out, b_out, ln2_gain, ln2_shift, w_up, b_up, w_down, b_down, cotangent):
    params = tuple((argument.astype(jnp.float32) for argument in (ln1_gain, ln1_shift, w_qkv, b_qv, w_out, b_out, ln2_gain, ln2_shift, w_up, b_up, w_down, b_down)))

    def one_sequence(totals, inputs):
        tokens, seg_ids, grad_seq = inputs
        result, pull_back = jax.vjp(lambda tokens_in, weights_in: forward(tokens_in, seg_ids, weights_in), tokens.astype(jnp.float32), params)
        grad_tokens, grad_weights = pull_back(grad_seq.astype(jnp.float32))
        totals = jax.tree.map(jnp.add, totals, grad_weights)
        return (totals, (result.astype(jnp.bfloat16), grad_tokens.astype(jnp.bfloat16)))
    zeros_init = jax.tree.map(jnp.zeros_like, params)
    totals, (outputs, grad_inputs) = lax.scan(one_sequence, zeros_init, (block_in, segments, cotangent))
    return (outputs, grad_inputs) + tuple(totals)
```

```python
import functools

import jax
import jax.numpy as jnp
from jax import lax
from jax.experimental import pallas as pl
from jax.experimental.pallas import tpu as pltpu
from jax.sharding import PartitionSpec as P

EPS = 1e-05
NEG = -1e30
BF = jnp.bfloat16
F32 = jnp.float32
LANES = 128
HEAD_PAD = 256
BQ = 256
BK = 256
VMEM_BYTES = 48 * 1024 * 1024


def dot_nn(left, right):
    return lax.dot_general(left, right, (((1,), (0,)), ((), ())), preferred_element_type=F32)


def dot_nt(left, right):
    return lax.dot_general(left, right, (((1,), (1,)), ((), ())), preferred_element_type=F32)


def dot_tn(left, right):
    return lax.dot_general(left, right, (((0,), (0,)), ((), ())), preferred_element_type=F32)


def swap(value, axis, bit):
    size = lax.axis_size(axis)
    return lax.ppermute(value, axis, [(i, i ^ bit) for i in range(size)])


def tree_sum(items):
    items = [item.astype(F32) for item in items]
    while len(items) > 1:
        items = [items[i] + items[i + 1] for i in range(0, len(items), 2)]
    return items[0]


def butterfly(value, axis):
    size = lax.axis_size(axis)
    if size & (size - 1):
        return lax.psum(value, axis)
    return tree_sum([value] + [swap(value, axis, bit) for bit in range(1, size)])


def gather_fsdp(value):
    if lax.axis_size("fsdp") != 2:
        return lax.all_gather(value, "fsdp", axis=0, tiled=False)
    other = swap(value, "fsdp", 1)
    first = lax.axis_index("fsdp") == 0
    return jnp.stack([jnp.where(first, value, other), jnp.where(first, other, value)])


def scatter_fsdp(value):
    if lax.axis_size("fsdp") != 2:
        return lax.psum_scatter(value, "fsdp", scatter_dimension=0, tiled=False)
    rank = lax.axis_index("fsdp")
    mine = lax.dynamic_index_in_dim(value, rank, 0, keepdims=False)
    theirs = lax.dynamic_index_in_dim(value, 1 - rank, 0, keepdims=False)
    return (mine.astype(F32) + swap(theirs, "fsdp", 1).astype(F32)).astype(value.dtype)


def sum_ctx(value):
    size = lax.axis_size("ctx")
    rows = value.shape[0]
    if size != 4 or rows % (8 * size):
        return lax.psum(value, "ctx").astype(F32)
    rank = lax.axis_index("ctx")
    parts = value.reshape((size, rows // size) + value.shape[1:])

    def part(index):
        return lax.dynamic_index_in_dim(parts, index, 0, keepdims=False)

    got = [part(rank)] + [
        lax.ppermute(part(rank ^ s), "ctx", [(i, i ^ s) for i in range(size)])
        for s in range(1, size)
    ]
    mine = tree_sum(got).astype(value.dtype)
    slots = jnp.stack([mine] + [swap(mine, "ctx", s) for s in range(1, size)])
    out = [lax.dynamic_index_in_dim(slots, rank ^ i, 0, keepdims=False) for i in range(size)]
    return jnp.concatenate(out, axis=0).astype(F32)


def gather_tp(value):
    far = swap(value, "tp", 2)
    return [value, swap(value, "tp", 1), far, swap(far, "tp", 1)]


def scatter_tp(slots):
    near = [slots[0].astype(F32) + swap(slots[1], "tp", 1).astype(F32)]
    far = slots[2].astype(F32) + swap(slots[3], "tp", 1).astype(F32)
    return near[0] + swap(far.astype(BF), "tp", 2).astype(F32)


def seq_steps(seqs):
    size = lax.axis_size("ctx")
    groups = size // seqs
    return [
        [(src, ((src % seqs + step) % seqs) * groups + src // seqs) for src in range(size)]
        for step in range(seqs)
    ]


def send(value, pairs):
    if all(src == dst for src, dst in pairs):
        return value
    return lax.ppermute(value, "ctx", pairs)


def to_sequence(value):
    seqs = value.shape[0]
    base = lax.axis_index("ctx") % seqs
    return [
        send(lax.dynamic_index_in_dim(value, (base + step) % seqs, 0, keepdims=False), pairs)
        for step, pairs in enumerate(seq_steps(seqs))
    ]


def from_sequence(blocks):
    seqs = len(blocks)
    base = lax.axis_index("ctx") % seqs
    got = [
        send(block, [(dst, src) for src, dst in pairs])
        for block, pairs in zip(blocks, seq_steps(seqs))
    ]
    twice = jnp.stack(got + got)
    return lax.dynamic_slice_in_dim(twice, (seqs - base) % seqs, seqs, 0)


def lane_is_low(rows):
    return lax.broadcasted_iota(jnp.int32, (rows, LANES), 1) < LANES // 2


def pieces(dims):
    ranks, steps = dims
    return [(j * ranks + rank, j, rank) for j in range(steps) for rank in range(ranks)]


def allowed_block(seg_row, seg_col, q_axis, q_start, k_start, shape):
    q_at = q_start + lax.broadcasted_iota(jnp.int32, shape, q_axis)
    k_at = k_start + lax.broadcasted_iota(jnp.int32, shape, 1 - q_axis)
    return (seg_row == seg_col) & (k_at <= q_at)


def attend_kernel(where_ref, low_ref, full_ref, seg_q_ref, seg_k_ref, q_ref, kv_ref, o_ref, lse_ref, qs, ks, vs):
    ranks, steps, sub, _ = q_ref.shape
    parts = kv_ref.shape[0]
    tp_rank, seq_rank, part = where_ref[0], where_ref[1], where_ref[2]
    q_len = ranks * steps * sub
    scale = 64 ** (-0.5)
    low = lane_is_low(sub)
    for block, j, rank in pieces((ranks, steps)):
        slot, step = tp_rank ^ rank, lax.rem(seq_rank - j + steps, steps)
        rows = slice(block * sub, (block + 1) * sub)
        tile = q_ref[slot, step]
        tile = (tile.astype(F32) * scale).astype(BF)
        head_pair = tile[:, :LANES]
        zero = jnp.zeros_like(head_pair)
        qs[rows, 0:128] = jnp.where(low, head_pair, zero)
        qs[rows, 128:256] = jnp.where(low, zero, head_pair)
        qs[rows, 256:384] = tile[:, LANES:]
        for p in range(parts):
            at = slice(p * q_len + block * sub, p * q_len + (block + 1) * sub)
            ks[at, :] = kv_ref[p, slot, step, :, :HEAD_PAD]
            vs[at, :] = kv_ref[p, slot, step, :, HEAD_PAD:]

    def q_block(i, _):
        q_row = pl.multiple_of(i * BQ, BQ)
        q_first = part * q_len + q_row
        seg_q = seg_q_ref[pl.ds(q_row, BQ), :]

        def step(masked, kk, carry):
            k_row = pl.multiple_of(kk * BK, BK)
            keys = ks[pl.ds(k_row, BK), :]
            vals = vs[pl.ds(k_row, BK), :]
            if masked:
                ok = allowed_block(seg_q, seg_k_ref[:, pl.ds(k_row, BK)], 0, q_first, k_row, (BQ, BK))
            out = []
            for h in range(3):
                top, total, acc = carry[h]
                lanes = slice((h // 2) * LANES, (h // 2 + 1) * LANES)
                scores = dot_nt(qs[pl.ds(q_row, BQ), h * LANES : (h + 1) * LANES], keys[:, lanes])
                if masked:
                    scores = jnp.where(ok, scores, NEG)
                new_top = jnp.maximum(top, jnp.max(scores, axis=1, keepdims=True))
                probs = jnp.exp(scores - new_top)
                shrink = jnp.exp(top - new_top)
                total = total * shrink + jnp.sum(probs, axis=1, keepdims=True)
                acc = acc * shrink + dot_nn(probs.astype(BF), vals[:, lanes])
                out.append((new_top, total, acc))
            return tuple(out)

        start = tuple(
            (jnp.full((BQ, 1), NEG, F32), jnp.zeros((BQ, 1), F32), jnp.zeros((BQ, LANES), F32))
            for _ in range(3)
        )
        first, full = low_ref[i], full_ref[i]
        last = q_first // BK
        carry = lax.fori_loop(first, full, functools.partial(step, True), start)
        carry = lax.fori_loop(full, last, functools.partial(step, False), carry)
        carry = lax.fori_loop(last, last + BQ // BK, functools.partial(step, True), carry)
        heads = [acc / total for _, total, acc in carry]
        pair = jnp.where(lane_is_low(BQ), heads[0], heads[1]).astype(BF)
        third = heads[2].astype(BF)
        for n in range(BQ // sub):
            block = i * (BQ // sub) + n
            j, rank = block // ranks, lax.rem(block, ranks)
            slot, at = tp_rank ^ rank, lax.rem(seq_rank - j + steps, steps)
            o_ref[slot, at, :, 0:128] = pair[n * sub : (n + 1) * sub]
            o_ref[slot, at, :, 128:256] = third[n * sub : (n + 1) * sub]
        for h in range(3):
            top, total, _ = carry[h]
            column = jnp.broadcast_to(top + jnp.log(total), (BQ, LANES))
            lse_ref[h : h + 1, pl.ds(q_row, BQ)] = column.T[0:1]
        return 0

    lax.fori_loop(0, q_len // BQ, q_block, 0)


def attend_back_kernel(
    where_ref, full_ref, high_ref, seg_q_ref, seg_k_ref, q_ref, kv_ref, o_ref, do_ref, lse_ref, dq_ref, dkv_ref, qs, ks, vs, dos, dqs, delta
):
    ranks, steps, sub, _ = q_ref.shape
    parts = kv_ref.shape[0]
    tp_rank, seq_rank, part = where_ref[0], where_ref[1], where_ref[2]
    q_len = ranks * steps * sub
    scale = 64 ** (-0.5)
    low = lane_is_low(sub)

    def place(rank, j):
        return tp_rank ^ rank, lax.rem(seq_rank - j + steps, steps)

    for block, j, rank in pieces((ranks, steps)):
        slot, step = place(rank, j)
        rows = slice(block * sub, (block + 1) * sub)
        tile = (q_ref[slot, step].astype(F32) * scale).astype(BF)
        grad = do_ref[slot, step]
        for source, target in ((tile, qs), (grad, dos)):
            head_pair = source[:, :LANES]
            zero = jnp.zeros_like(head_pair)
            target[rows, 0:128] = jnp.where(low, head_pair, zero)
            target[rows, 128:256] = jnp.where(low, zero, head_pair)
            target[rows, 256:384] = source[:, LANES:]
        product = grad.astype(F32) * o_ref[slot, step].astype(F32)
        pair = product[:, :LANES].T
        third = product[:, LANES:].T
        delta[0:1, rows] = jnp.sum(pair[:64], axis=0, keepdims=True)
        delta[1:2, rows] = jnp.sum(pair[64:], axis=0, keepdims=True)
        delta[2:3, rows] = jnp.sum(third[:64], axis=0, keepdims=True)
        for p in range(parts):
            at = slice(p * q_len + block * sub, p * q_len + (block + 1) * sub)
            ks[at, :] = kv_ref[p, slot, step, :, :HEAD_PAD]
            vs[at, :] = kv_ref[p, slot, step, :, HEAD_PAD:]
    dqs[...] = jnp.zeros_like(dqs)
    q_count = q_len // BQ
    low_q = lane_is_low(BQ)

    def k_block(kk, _):
        k_row = pl.multiple_of(kk * BK, BK)
        keys = ks[pl.ds(k_row, BK), :]
        vals = vs[pl.ds(k_row, BK), :]
        seg_k = seg_k_ref[pl.ds(k_row, BK), :]

        def step(masked, i, carry):
            q_row = pl.multiple_of(i * BQ, BQ)
            at = pl.ds(q_row, BQ)
            if masked:
                ok = allowed_block(
                    seg_q_ref[:, at], seg_k, 1, part * q_len + q_row, k_row, (BK, BQ)
                )
            dk, dv = list(carry[0]), list(carry[1])
            dq = []
            for h in range(3):
                t = h // 2
                lanes = slice(t * LANES, (t + 1) * LANES)
                mine = slice(h * LANES, (h + 1) * LANES)
                q_head, do_head = qs[at, mine], dos[at, mine]
                scores = dot_nt(keys[:, lanes], q_head)
                probs = jnp.exp(scores - lse_ref[h : h + 1, at])
                if masked:
                    probs = jnp.where(ok, probs, 0.0)
                grad_probs = dot_nt(vals[:, lanes], do_head)
                grad_scores = (probs * (grad_probs - delta[h : h + 1, at])).astype(BF)
                dv[t] = dv[t] + dot_nn(probs.astype(BF), do_head)
                dk[t] = dk[t] + dot_nn(grad_scores, q_head)
                dq.append(dot_tn(grad_scores, keys[:, lanes]))
            dqs[at, 0:128] += jnp.where(low_q, dq[0], dq[1])
            dqs[at, 128:256] += dq[2]
            return tuple(dk), tuple(dv)

        zero = jnp.zeros((BK, LANES), F32)
        carry = ((zero, zero), (zero, zero))
        first = jnp.maximum(kk * BK // BQ - part * q_count, 0)
        diagonal = jnp.where(kk * BK >= part * q_len, first + 1, first)
        diagonal = jnp.where(kk * BK >= (part + 1) * q_len, first, diagonal)
        first = jnp.minimum(first, q_count)
        diagonal = jnp.minimum(diagonal, q_count)
        full = jnp.maximum(full_ref[kk], diagonal)
        high = jnp.maximum(high_ref[kk], full)
        carry = lax.fori_loop(first, diagonal, functools.partial(step, True), carry)
        carry = lax.fori_loop(diagonal, full, functools.partial(step, False), carry)
        carry = lax.fori_loop(full, high, functools.partial(step, True), carry)
        dk, dv = carry
        p = kk // (q_len // BK)
        for n in range(BK // sub):
            block = lax.rem(kk, q_len // BK) * (BK // sub) + n
            slot, step_at = place(lax.rem(block, ranks), block // ranks)
            rows = slice(n * sub, (n + 1) * sub)
            for t in range(2):
                dkv_ref[p, slot, step_at, :, t * 128 : (t + 1) * 128] = dk[t][rows].astype(BF)
                dkv_ref[p, slot, step_at, :, 256 + t * 128 : 256 + (t + 1) * 128] = dv[t][rows].astype(BF)
        return 0

    lax.fori_loop(0, parts * q_len // BK, k_block, 0)
    for block, j, rank in pieces((ranks, steps)):
        slot, step = place(rank, j)
        dq_ref[slot, step] = (dqs[block * sub : (block + 1) * sub, :] * scale).astype(BF)


SMEM = pl.BlockSpec(memory_space=pltpu.SMEM)
VMEM = pl.BlockSpec(memory_space=pltpu.VMEM)
PARAMS = pltpu.CompilerParams(vmem_limit_bytes=VMEM_BYTES)


def attend(where, seg_q, seg_k, queries, keyvals):
    ranks, steps, sub, _ = queries.shape
    q_len, k_len = ranks * steps * sub, keyvals.shape[0] * ranks * steps * sub
    q_first, q_last = seg_q[::BQ], seg_q[BQ - 1 :: BQ]
    k_first, k_last = seg_k[::BK], seg_k[BK - 1 :: BK]
    k_index = jnp.arange(k_len // BK)
    bound = where[2] * (q_len // BK) + jnp.arange(q_len // BQ) * (BQ // BK)
    before = k_index[None, :] < bound[:, None]
    first = jnp.sum(before & (k_last[None, :] < q_first[:, None]), axis=1).astype(jnp.int32)
    full = jnp.sum(before & (k_first[None, :] != q_last[:, None]), axis=1).astype(jnp.int32)
    return pl.pallas_call(
        attend_kernel,
        out_shape=(
            jax.ShapeDtypeStruct((ranks, steps, sub, HEAD_PAD), BF),
            jax.ShapeDtypeStruct((8, q_len), F32),
        ),
        in_specs=[SMEM, SMEM, SMEM, VMEM, VMEM, VMEM, VMEM],
        out_specs=(VMEM, VMEM),
        scratch_shapes=[
            pltpu.VMEM((q_len, 3 * LANES), BF),
            pltpu.VMEM((k_len, HEAD_PAD), BF),
            pltpu.VMEM((k_len, HEAD_PAD), BF),
        ],
        compiler_params=PARAMS,
        cost_estimate=pl.CostEstimate(
            flops=6 * q_len * k_len * 256, bytes_accessed=8 * q_len * 1024, transcendentals=3 * q_len * k_len // 2
        ),
        name="attend",
    )(where, first, jnp.maximum(full, first), seg_q[:, None], seg_k[None, :], queries, keyvals)


def attend_back(where, seg_q, seg_k, queries, keyvals, attended, grad, lse):
    ranks, steps, sub, _ = queries.shape
    q_len, k_len = ranks * steps * sub, keyvals.shape[0] * ranks * steps * sub
    q_first, q_last = seg_q[::BQ], seg_q[BQ - 1 :: BQ]
    k_first, k_last = seg_k[::BK], seg_k[BK - 1 :: BK]
    full = jnp.sum(q_last[None, :] <= k_first[:, None], axis=1).astype(jnp.int32)
    high = jnp.sum(q_first[None, :] <= k_last[:, None], axis=1).astype(jnp.int32)
    return pl.pallas_call(
        attend_back_kernel,
        out_shape=(
            jax.ShapeDtypeStruct(queries.shape, BF),
            jax.ShapeDtypeStruct(keyvals.shape, BF),
        ),
        in_specs=[SMEM, SMEM, SMEM] + [VMEM] * 7,
        out_specs=(VMEM, VMEM),
        scratch_shapes=[
            pltpu.VMEM((q_len, 3 * LANES), BF),
            pltpu.VMEM((k_len, HEAD_PAD), BF),
            pltpu.VMEM((k_len, HEAD_PAD), BF),
            pltpu.VMEM((q_len, 3 * LANES), BF),
            pltpu.VMEM((q_len, HEAD_PAD), F32),
            pltpu.VMEM((8, q_len), F32),
        ],
        compiler_params=PARAMS,
        cost_estimate=pl.CostEstimate(
            flops=15 * q_len * k_len * 256, bytes_accessed=16 * q_len * 1024, transcendentals=3 * q_len * k_len // 2
        ),
        name="attend_back",
    )(where, full, high, seg_q[None, :], seg_k[:, None], queries, keyvals, attended, grad, lse)


def norm_parts(values):
    center = values - jnp.mean(values, axis=-1, keepdims=True)
    rstd = lax.rsqrt(jnp.mean(center * center, axis=-1, keepdims=True) + EPS)
    return center * rstd, rstd


def norm_back(xhat, rstd, gain, grad):
    gg = grad * gain
    inner = gg - jnp.mean(gg, axis=-1, keepdims=True)
    return rstd * (inner - xhat * jnp.mean(gg * xhat, axis=-1, keepdims=True))


def gelu_tanh(inputs):
    return jax.nn.gelu(inputs, approximate=True)


def on_device(
    block_in, segments, ln1_gain, ln1_shift, w_qkv, b_qv, w_out, b_out, ln2_gain, ln2_shift, w_up, b_up, w_down, b_down, cotangent
):
    seqs, sub, width = block_in.shape
    ranks = lax.axis_size("tp")
    ctx_size = lax.axis_size("ctx")
    parts = ctx_size // seqs
    tp_rank, ctx_rank = lax.axis_index("tp"), lax.axis_index("ctx")
    heads = b_qv.shape[0]
    head_width = heads * 64
    own = seqs * sub
    tokens = ranks * own

    x_own = jnp.concatenate(to_sequence(block_in), axis=0)

    small = [ln1_gain, ln1_shift, b_out, ln2_gain, ln2_shift, b_down]
    flat = jnp.concatenate([*small, b_qv.reshape(-1), b_up.reshape(-1)])
    packed = gather_fsdp(flat)
    shard = ln1_gain.shape[0]
    gain_one, shift_one, out_bias, gain_two, shift_two, down_bias = (
        packed[:, n * shard : (n + 1) * shard].reshape(-1).astype(F32) for n in range(6)
    )
    rest = packed[:, 6 * shard :]
    qv_bias = rest[:, : b_qv.size].reshape((-1,) + b_qv.shape).transpose(1, 0, 2).reshape(heads, -1)
    up_bias = rest[:, b_qv.size :].reshape((-1,) + b_up.shape).transpose(1, 0, 2).reshape(-1)

    qkv_mat = gather_fsdp(w_qkv).transpose(1, 0, 2, 3).reshape(3, head_width, width)
    qkv_pad = jnp.pad(qkv_mat, ((0, 0), (0, HEAD_PAD - head_width), (0, 0)))
    q_mat, kv_mat = qkv_pad[0], qkv_pad[1:].reshape(2 * HEAD_PAD, width)
    bias_float = qv_bias.astype(F32)

    def pad_bias(bias):
        return jnp.pad(bias.reshape(-1), (0, HEAD_PAD - head_width))

    q_bias = pad_bias(bias_float[:, :64])
    kv_bias = jnp.concatenate([jnp.zeros((HEAD_PAD,), F32), pad_bias(bias_float[:, 64:])])

    x_float = x_own.astype(F32)
    xhat_one, rstd_one = norm_parts(x_float)
    normed_own = (xhat_one * gain_one + shift_one).astype(BF)
    normed_one = jnp.concatenate(gather_tp(normed_own), axis=0)

    queries = (dot_nt(normed_one, q_mat) + q_bias).astype(BF).reshape(ranks, seqs, sub, HEAD_PAD)
    keyvals = (dot_nt(normed_one, kv_mat) + kv_bias).astype(BF)
    keyvals = keyvals.reshape(1, ranks, seqs, sub, 2 * HEAD_PAD)
    groups = [[g * parts + p for p in range(parts)] for g in range(ctx_size // parts)]
    if parts > 1:
        keyvals = lax.all_gather(keyvals, "ctx", axis=0, tiled=True, axis_index_groups=groups)
    seq_rank, part = ctx_rank // parts, ctx_rank % parts
    where = jnp.stack([tp_rank, seq_rank, part]).astype(jnp.int32)
    seg_k = lax.dynamic_index_in_dim(segments, seq_rank, 0, keepdims=False)
    seg_q = lax.dynamic_slice_in_dim(seg_k, part * tokens, tokens, 0)
    attended, lse = attend(where, seg_q, seg_k, queries, keyvals)

    out_mats = gather_tp(gather_fsdp(w_out).reshape(head_width, width))
    up_mats = gather_tp(gather_fsdp(w_up).reshape(width, -1))
    down_far = gather_fsdp(jnp.stack([w_down, swap(w_down, "tp", 2)]))
    down_far = down_far.transpose(1, 0, 2, 3).reshape(2, -1, width)
    down_mats = [down_far[0], swap(down_far[0], "tp", 1), down_far[1], swap(down_far[1], "tp", 1)]
    up_biases = [up_bias] + [swap(up_bias, "tp", s) for s in range(1, ranks)]
    blank = jnp.zeros((HEAD_PAD - head_width, width), BF)
    out_mat = jnp.concatenate([piece for mat in out_mats for piece in (mat, blank)], axis=0)

    attended_slots = attended.reshape(ranks, own, HEAD_PAD)
    merged = jnp.concatenate(
        [attended_slots[0]] + [swap(attended_slots[s], "tp", s) for s in range(1, ranks)], axis=1
    )
    hidden = x_float + dot_nn(merged, out_mat) + out_bias
    xhat_two, rstd_two = norm_parts(hidden)
    normed_two = (xhat_two * gain_two + shift_two).astype(BF)

    cot_rows = jnp.concatenate(to_sequence(cotangent), axis=0)
    cot_float = cot_rows.astype(F32)

    mlp_out = down_bias
    grad_normed_two = 0.0
    grad_up, grad_down, grad_up_bias = [], [], []
    for s in range(ranks):
        pre = dot_nn(normed_two, up_mats[s]) + up_biases[s].astype(F32)
        activ, pull = jax.vjp(gelu_tanh, pre)
        activ = activ.astype(BF)
        mlp_out = mlp_out + dot_nn(activ, down_mats[s])
        grad_pre = pull(dot_nt(cot_rows, down_mats[s]))[0].astype(BF)
        grad_normed_two = grad_normed_two + dot_nt(grad_pre, up_mats[s])
        grad_down.append(dot_tn(activ, cot_rows).astype(BF))
        grad_up.append(dot_tn(normed_two, grad_pre).astype(BF))
        grad_up_bias.append(jnp.sum(grad_pre.astype(F32), axis=0))
    block_out = (hidden + mlp_out).astype(BF)
    out_blocks = from_sequence([block_out[n * sub : (n + 1) * sub] for n in range(seqs)])

    grad_hidden = cot_float + norm_back(xhat_two, rstd_two, gain_two, grad_normed_two)
    grad_branch = grad_hidden.astype(BF)
    grad_merged = dot_nt(grad_branch, out_mat).astype(BF)
    grad_slots = [grad_merged[:, s * HEAD_PAD : (s + 1) * HEAD_PAD] for s in range(ranks)]
    grad_slots = [grad_slots[0]] + [swap(grad_slots[s], "tp", s) for s in range(1, ranks)]
    grad_attended = jnp.stack(grad_slots).reshape(ranks, seqs, sub, HEAD_PAD)
    grad_out = dot_tn(merged, grad_branch).astype(BF)

    fsdp = lax.axis_size("fsdp")
    near_down = [
        (grad_down[n].astype(F32) + swap(grad_down[n + 1], "tp", 1).astype(F32)).astype(BF)
        for n in (0, 2)
    ]
    near_down = jnp.stack(near_down, axis=0).reshape(2, fsdp, -1, width).transpose(1, 0, 2, 3)
    near_down = scatter_fsdp(near_down)
    down_shard = near_down[0].astype(F32) + swap(near_down[1], "tp", 2).astype(F32)
    sum_down = sum_ctx(down_shard.astype(BF))
    up_shard = scatter_tp(grad_up).astype(BF).reshape(fsdp, -1, grad_up[0].shape[1])
    sum_up = sum_ctx(scatter_fsdp(up_shard))
    out_shard = scatter_tp(
        [grad_out[s * HEAD_PAD : s * HEAD_PAD + head_width] for s in range(ranks)]
    )
    sum_out = sum_ctx(scatter_fsdp(out_shard.astype(BF).reshape(fsdp, -1, width)))

    early = [
        jnp.sum(grad_normed_two * xhat_two, axis=0),
        jnp.sum(grad_normed_two, axis=0),
        jnp.sum(grad_hidden, axis=0),
        jnp.sum(cot_float, axis=0),
    ]
    up_bias_all = jnp.take(jnp.stack(grad_up_bias), tp_rank ^ jnp.arange(ranks), axis=0)
    early = jnp.concatenate(early + [up_bias_all.reshape(-1)]).reshape(-1, LANES)
    early = lax.psum(early, ("fsdp", "ctx", "tp")).reshape(-1)

    dq, dkv = attend_back(where, seg_q, seg_k, queries, keyvals, attended, grad_attended, lse)
    if parts > 1:
        dkv = lax.psum_scatter(
            dkv, "ctx", scatter_dimension=0, tiled=True, axis_index_groups=groups
        )
    dq = dq.reshape(tokens, HEAD_PAD)
    dkv = dkv.reshape(tokens, 2 * HEAD_PAD)
    grad_normed = (dot_nn(dq, q_mat) + dot_nn(dkv, kv_mat)).astype(BF).reshape(ranks, own, width)
    grad_normed_one = scatter_tp([grad_normed[s] for s in range(ranks)])
    grad_x = grad_hidden + norm_back(xhat_one, rstd_one, gain_one, grad_normed_one)
    grad_x = grad_x.astype(BF)
    grad_blocks = from_sequence([grad_x[n * sub : (n + 1) * sub] for n in range(seqs)])

    grad_qkv = jnp.concatenate(
        [
            dot_tn(dq, normed_one)[:head_width],
            dot_tn(dkv, normed_one).reshape(2, HEAD_PAD, width)[:, :head_width].reshape(-1, width),
        ]
    ).astype(BF)
    grad_qkv = grad_qkv.reshape(3, fsdp, -1, width).transpose(1, 0, 2, 3)
    qkv_shard = scatter_fsdp(grad_qkv)
    sum_qkv = sum_ctx(qkv_shard.reshape(-1, width)).reshape(w_qkv.shape)

    bias_q = jnp.sum(dq.astype(F32), axis=0)[:head_width].reshape(heads, 64)
    bias_v = jnp.sum(dkv[:, HEAD_PAD:].astype(F32), axis=0)[:head_width].reshape(heads, 64)
    bias_rows = jnp.concatenate([bias_q, bias_v], axis=1)
    bias_all = lax.dynamic_update_slice(
        jnp.zeros((ranks * heads, 128), F32), bias_rows, (tp_rank * heads, 0)
    )
    late = [jnp.sum(grad_normed_one * xhat_one, axis=0), jnp.sum(grad_normed_one, axis=0)]
    late = jnp.concatenate(late + [bias_all.reshape(-1)]).reshape(-1, LANES)
    for axis in ("tp", "ctx", "fsdp"):
        late = butterfly(late, axis)
    late = late.reshape(-1)

    fsdp_rank = lax.axis_index("fsdp")

    def mine(vector):
        return lax.dynamic_slice_in_dim(vector, fsdp_rank * shard, shard, 0)

    def mine_bias(rows, like):
        rows = lax.dynamic_slice_in_dim(rows, tp_rank * like.shape[0], like.shape[0], 0)
        return lax.dynamic_slice_in_dim(rows, fsdp_rank * like.shape[1], like.shape[1], 1)

    sum_qv_bias = mine_bias(late[2 * width :].reshape(ranks * heads, 128), b_qv)
    sum_up_bias = mine_bias(early[4 * width :].reshape(ranks * b_up.shape[0], -1), b_up)
    return (
        out_blocks,
        grad_blocks,
        mine(late[:width]),
        mine(late[width : 2 * width]),
        sum_qkv,
        sum_qv_bias,
        sum_out,
        mine(early[2 * width : 3 * width]),
        mine(early[:width]),
        mine(early[width : 2 * width]),
        sum_up,
        sum_up_bias,
        sum_down,
        mine(early[3 * width : 4 * width]),
    )


def solution(mesh):
    rows = P("fsdp", ("ctx", "tp"), None)
    vector = P("fsdp")
    out_rows = P(("tp", "fsdp"), None)
    qkv_rows = P(None, ("tp", "fsdp"), None)
    bias = P("tp", "fsdp")
    weights = (
        vector, vector, qkv_rows, bias, out_rows, vector, vector, vector, P("fsdp", "tp"), bias, out_rows, vector,
    )
    return jax.shard_map(
        on_device,
        mesh=mesh,
        in_specs=(rows, P("fsdp", None)) + weights + (rows,),
        out_specs=(rows, rows) + weights,
        check_vma=False,
    )
```

```python
import functools

import jax
import jax.numpy as jnp
from jax import lax
from jax.experimental import pallas as pl
from jax.experimental.pallas import tpu as pltpu
from jax.sharding import PartitionSpec as P

EPS = 1e-05
NEG = -1e30
BF = jnp.bfloat16
F32 = jnp.float32
LANES = 128
HEAD_PAD = 256
BQ = 512
BK = 512
VMEM_BYTES = 48 * 1024 * 1024


def dot_nn(left, right):
    return lax.dot_general(left, right, (((1,), (0,)), ((), ())), preferred_element_type=F32)


def dot_nt(left, right):
    return lax.dot_general(left, right, (((1,), (1,)), ((), ())), preferred_element_type=F32)


def dot_tn(left, right):
    return lax.dot_general(left, right, (((0,), (0,)), ((), ())), preferred_element_type=F32)


def swap(value, axis, bit):
    size = lax.axis_size(axis)
    return lax.ppermute(value, axis, [(i, i ^ bit) for i in range(size)])


def tree_sum(items):
    items = [item.astype(F32) for item in items]
    while len(items) > 1:
        items = [items[i] + items[i + 1] for i in range(0, len(items), 2)]
    return items[0]


def butterfly(value, axis):
    size = lax.axis_size(axis)
    if size & (size - 1):
        return lax.psum(value, axis)
    return tree_sum([value] + [swap(value, axis, bit) for bit in range(1, size)])


def gather_fsdp(values, axis):
    if lax.axis_size("fsdp") != 2:
        return [lax.all_gather(value, "fsdp", axis=axis, tiled=True) for value in values]
    whole = values[0] if len(values) == 1 else jnp.concatenate(values, axis=axis)
    other = swap(whole, "fsdp", 1)
    first = lax.axis_index("fsdp") == 0
    out, start = [], 0
    for value in values:
        size = value.shape[axis]
        theirs = lax.slice_in_dim(other, start, start + size, axis=axis)
        start += size
        pair = [jnp.where(first, value, theirs), jnp.where(first, theirs, value)]
        out.append(jnp.concatenate(pair, axis=axis))
    return out


def scatter_fsdp(value):
    if lax.axis_size("fsdp") != 2:
        return lax.psum_scatter(value, "fsdp", scatter_dimension=0, tiled=False)
    rank = lax.axis_index("fsdp")
    mine = lax.dynamic_index_in_dim(value, rank, 0, keepdims=False)
    theirs = lax.dynamic_index_in_dim(value, 1 - rank, 0, keepdims=False)
    return (mine.astype(F32) + swap(theirs, "fsdp", 1).astype(F32)).astype(value.dtype)


def sum_ctx(value):
    size = lax.axis_size("ctx")
    rows = value.shape[0]
    if size != 4 or rows % (8 * size):
        return lax.psum(value, "ctx").astype(F32)
    rank = lax.axis_index("ctx")
    near, far = rank % 2, rank // 2
    parts = value.reshape((2, 2, rows // size) + value.shape[1:])

    def halve(array, axis, bit, side):
        mine = lax.dynamic_index_in_dim(array, side, axis, keepdims=False)
        theirs = lax.dynamic_index_in_dim(array, 1 - side, axis, keepdims=False)
        return (mine.astype(F32) + swap(theirs, "ctx", bit).astype(F32)).astype(value.dtype)

    def double(array, axis, bit, side):
        other = swap(array, "ctx", bit)
        first = side == 0
        return jnp.stack(
            [jnp.where(first, array, other), jnp.where(first, other, array)], axis=axis
        )

    total = halve(halve(parts, 1, 1, near), 0, 2, far)
    total = double(double(total, 0, 2, far), 1, 1, near)
    return total.reshape(value.shape).astype(F32)


def gather_tp(value):
    far = swap(value, "tp", 2)
    return [value, swap(value, "tp", 1), far, swap(far, "tp", 1)]


def add_low(left, right):
    return (left.astype(F32) + right.astype(F32)).astype(BF)


def near_sums(slots):
    return [add_low(slots[n], swap(slots[n + 1], "tp", 1)) for n in (0, 2)]


def far_sum(near, far):
    return near.astype(F32) + swap(far, "tp", 2).astype(F32)


def seq_steps(seqs):
    size = lax.axis_size("ctx")
    groups = size // seqs
    return [
        [(src, ((src % seqs + step) % seqs) * groups + src // seqs) for src in range(size)]
        for step in range(seqs)
    ]


def send(value, pairs):
    if all(src == dst for src, dst in pairs):
        return value
    return lax.ppermute(value, "ctx", pairs)


def to_sequence(value):
    seqs = value.shape[0]
    size = lax.axis_size("ctx")
    base = lax.axis_index("ctx") % seqs
    owner = lax.axis_index("ctx") // (size // seqs)
    out = jnp.zeros_like(value)
    for step, pairs in enumerate(seq_steps(seqs)):
        block = lax.dynamic_index_in_dim(value, (base + step) % seqs, 0, keepdims=True)
        place = (owner - step + seqs) % seqs
        out = lax.dynamic_update_slice_in_dim(out, send(block, pairs), place, 0)
    return out


def from_sequence(value):
    seqs = value.shape[0]
    size = lax.axis_size("ctx")
    base = lax.axis_index("ctx") % seqs
    owner = lax.axis_index("ctx") // (size // seqs)
    out = jnp.zeros_like(value)
    for step, pairs in enumerate(seq_steps(seqs)):
        block = lax.dynamic_index_in_dim(value, (owner - step + seqs) % seqs, 0, keepdims=True)
        block = send(block, [(dst, src) for src, dst in pairs])
        out = lax.dynamic_update_slice_in_dim(out, block, (base + step) % seqs, 0)
    return out


def lane_is_low(rows):
    return lax.broadcasted_iota(jnp.int32, (rows, LANES), 1) < LANES // 2


def pieces(dims):
    ranks, steps = dims
    return [(j * ranks + rank, j, rank) for j in range(steps) for rank in range(ranks)]


def allowed_block(seg_row, seg_col, q_axis, q_start, k_start, shape):
    q_at = q_start + lax.broadcasted_iota(jnp.int32, shape, q_axis)
    k_at = k_start + lax.broadcasted_iota(jnp.int32, shape, 1 - q_axis)
    return (seg_row == seg_col) & (k_at <= q_at)


def split_heads(tile, target, rows, low):
    head_pair = tile[:, :LANES]
    zero = jnp.zeros_like(head_pair)
    target[rows, 0:128] = jnp.where(low, head_pair, zero)
    target[rows, 128:256] = jnp.where(low, zero, head_pair)
    target[rows, 256:384] = tile[:, LANES:]


def attend_kernel(gathered, where_ref, low_ref, full_ref, seg_q_ref, seg_k_ref, proj_ref, *refs):
    kv_ref = refs[0] if gathered else None
    o_ref, lse_ref, qs, ks, vs = refs[1:] if gathered else refs
    ranks, steps, sub, _ = proj_ref.shape
    parts = kv_ref.shape[0] if gathered else 1
    tp_rank, part = where_ref[0], where_ref[1]
    q_len = ranks * steps * sub
    scale = 64 ** (-0.5)
    low = lane_is_low(sub)
    for block, j, rank in pieces((ranks, steps)):
        slot = tp_rank ^ rank
        rows = slice(block * sub, (block + 1) * sub)
        tile = (proj_ref[slot, j, :, :HEAD_PAD].astype(F32) * scale).astype(BF)
        split_heads(tile, qs, rows, low)
        for p in range(parts):
            at = slice(p * q_len + block * sub, p * q_len + (block + 1) * sub)
            both = kv_ref[p, slot, j] if gathered else proj_ref[slot, j, :, HEAD_PAD:]
            ks[at, :] = both[:, :HEAD_PAD]
            vs[at, :] = both[:, HEAD_PAD:]

    def q_block(i, _):
        q_row = pl.multiple_of(i * BQ, BQ)
        q_first = part * q_len + q_row
        seg_q = seg_q_ref[pl.ds(q_row, BQ), :]

        def step(masked, kk, carry):
            k_row = pl.multiple_of(kk * BK, BK)
            keys = ks[pl.ds(k_row, BK), :]
            vals = vs[pl.ds(k_row, BK), :]
            if masked:
                ok = allowed_block(seg_q, seg_k_ref[:, pl.ds(k_row, BK)], 0, q_first, k_row, (BQ, BK))
            out = []
            for h in range(3):
                top, total, acc = carry[h]
                lanes = slice((h // 2) * LANES, (h // 2 + 1) * LANES)
                scores = dot_nt(qs[pl.ds(q_row, BQ), h * LANES : (h + 1) * LANES], keys[:, lanes])
                if masked:
                    scores = jnp.where(ok, scores, NEG)
                new_top = jnp.maximum(top, jnp.max(scores, axis=1, keepdims=True))
                probs = jnp.exp(scores - new_top)
                shrink = jnp.exp(top - new_top)
                total = total * shrink + jnp.sum(probs, axis=1, keepdims=True)
                acc = acc * shrink + dot_nn(probs.astype(BF), vals[:, lanes])
                out.append((new_top, total, acc))
            return tuple(out)

        start = tuple(
            (jnp.full((BQ, 1), NEG, F32), jnp.zeros((BQ, 1), F32), jnp.zeros((BQ, LANES), F32))
            for _ in range(3)
        )
        first, full = low_ref[i], full_ref[i]
        last = q_first // BK
        carry = lax.fori_loop(first, full, functools.partial(step, True), start)
        carry = lax.fori_loop(full, last, functools.partial(step, False), carry)
        carry = lax.fori_loop(last, last + BQ // BK, functools.partial(step, True), carry)
        heads = [acc / total for _, total, acc in carry]
        pair = jnp.where(lane_is_low(BQ), heads[0], heads[1]).astype(BF)
        third = heads[2].astype(BF)
        for n in range(BQ // sub):
            block = i * (BQ // sub) + n
            slot, j = tp_rank ^ lax.rem(block, ranks), block // ranks
            o_ref[slot, j, :, 0:128] = pair[n * sub : (n + 1) * sub]
            o_ref[slot, j, :, 128:256] = third[n * sub : (n + 1) * sub]
        for h in range(3):
            top, total, _ = carry[h]
            column = jnp.broadcast_to(top + jnp.log(total), (BQ, LANES))
            lse_ref[i, h] = column.T[0:8]
        return 0

    lax.fori_loop(0, q_len // BQ, q_block, 0)


def attend_back_kernel(
    gathered, q_range, k_range, k_done, more, where_ref, full_ref, high_ref, seg_q_ref, seg_k_ref, o_ref, do_ref, lse_ref, proj_ref, *refs
):
    refs = list(refs)
    kv_ref = refs.pop(0) if gathered else None
    sum_ref = refs.pop(0) if more else None
    dproj_ref = refs.pop(0)
    dkv_ref = refs.pop(0) if gathered else None
    rest_ref = refs.pop(0) if k_done > k_range[0] else None
    qs, ks, vs, kt, dos, dqs, delta = refs
    ranks, steps, sub, _ = proj_ref.shape
    parts = kv_ref.shape[0] if gathered else 1
    tp_rank, part = where_ref[0], where_ref[1]
    q_len = ranks * steps * sub
    scale = 64 ** (-0.5)
    low = lane_is_low(sub)
    q_first, q_end = q_range
    per_q = BQ // sub

    for block, j, rank in pieces((ranks, steps)):
        slot = tp_rank ^ rank
        rows = slice(block * sub, (block + 1) * sub)
        if q_first * per_q <= block < q_end * per_q:
            split_heads((proj_ref[slot, j, :, :HEAD_PAD].astype(F32) * scale).astype(BF), qs, rows, low)
            grad = do_ref[slot, j]
            split_heads(grad, dos, rows, low)
            product = grad.astype(F32) * o_ref[slot, j].astype(F32)
            pair, third = product[:, :LANES].T, product[:, LANES:].T
            lanes = slice(rows.start % BQ, rows.start % BQ + sub)
            for h, part_of in enumerate((pair[:64], pair[64:], third[:64])):
                delta[block // per_q, h : h + 1, lanes] = jnp.sum(part_of, axis=0, keepdims=True)
        for p in range(parts):
            if not k_range[0] * BK <= p * q_len + block * sub < k_range[1] * BK:
                continue
            at = slice(p * q_len + block * sub, p * q_len + (block + 1) * sub)
            both = kv_ref[p, slot, j] if gathered else proj_ref[slot, j, :, HEAD_PAD:]
            ks[at, :] = both[:, :HEAD_PAD]
            vs[at, :] = both[:, HEAD_PAD:]
            kt[at.start // BK, :, at.start % BK : at.start % BK + sub] = both[:, :HEAD_PAD].T
    dqs[...] = jnp.zeros_like(dqs)

    def k_block(kk, _):
        k_row = pl.multiple_of(kk * BK, BK)
        keys = ks[pl.ds(k_row, BK), :]
        vals = vs[pl.ds(k_row, BK), :]
        seg_k = seg_k_ref[pl.ds(k_row, BK), :]

        def step(masked, i, carry):
            q_row = pl.multiple_of(i * BQ, BQ)
            at = pl.ds(q_row, BQ)
            if masked:
                ok = allowed_block(seg_q_ref[i], seg_k, 1, part * q_len + q_row, k_row, (BK, BQ))
            dk, dv = list(carry[0]), list(carry[1])
            for h in range(3):
                t = h // 2
                lanes = slice(t * LANES, (t + 1) * LANES)
                mine = slice(h * LANES, (h + 1) * LANES)
                q_head, do_head = qs[at, mine], dos[at, mine]
                scores = dot_nt(keys[:, lanes], q_head)
                probs = jnp.exp(scores - lse_ref[i, h, 0:1, :])
                if masked:
                    probs = jnp.where(ok, probs, 0.0)
                grad_probs = dot_nt(vals[:, lanes], do_head)
                grad_scores = (probs * (grad_probs - delta[i, h : h + 1, :])).astype(BF)
                dv[t] = dv[t] + dot_nn(probs.astype(BF), do_head)
                dk[t] = dk[t] + dot_nn(grad_scores, q_head)
                rows = slice(h * 64, (h + 1) * 64)
                dqs[i, rows, :] += dot_nn(kt[kk, rows, :], grad_scores)
            return tuple(dk), tuple(dv)

        zero = jnp.zeros((BK, LANES), F32)
        carry = ((zero, zero), (zero, zero))
        if more:
            pieces_in = [sum_ref[pl.ds(k_row, BK), t * LANES : (t + 1) * LANES] for t in range(4)]
            carry = (tuple(pieces_in[:2]), tuple(pieces_in[2:]))
        ahead = kk - part * (q_len // BQ)
        inside = lambda value: jnp.clip(value, q_first, q_end)
        first = inside(ahead)
        diagonal = jnp.where(ahead >= 0, inside(ahead + 1), first)
        full = jnp.maximum(inside(full_ref[kk]), diagonal)
        high = jnp.maximum(inside(high_ref[kk]), full)
        carry = lax.fori_loop(first, diagonal, functools.partial(step, True), carry)
        carry = lax.fori_loop(diagonal, full, functools.partial(step, False), carry)
        carry = lax.fori_loop(full, high, functools.partial(step, True), carry)
        return carry[0] + carry[1]

    def finish(kk, _):
        sums = k_block(kk, 0)
        for n in range(BK // sub):
            block = lax.rem(kk, q_len // BK) * (BK // sub) + n
            slot, j = tp_rank ^ lax.rem(block, ranks), block // ranks
            for t in range(4):
                piece = sums[t][n * sub : (n + 1) * sub].astype(BF)
                lanes = slice(t * LANES, (t + 1) * LANES)
                if gathered:
                    dkv_ref[kk // (q_len // BK), slot, j, :, lanes] = piece
                else:
                    start = HEAD_PAD + t * LANES
                    dproj_ref[slot, j - k_done * BK // (ranks * sub), :, start : start + LANES] = piece
        return 0

    def keep(kk, _):
        sums = k_block(kk, 0)
        for t in range(4):
            rest_ref[pl.ds(pl.multiple_of(kk * BK, BK), BK), t * LANES : (t + 1) * LANES] = sums[t]
        return 0

    if rest_ref is not None:
        lax.fori_loop(k_range[0], k_done, keep, 0)
    lax.fori_loop(k_done, k_range[1], finish, 0)
    for block, j, rank in pieces((ranks, steps)):
        if q_first * per_q <= block < q_end * per_q:
            lanes = slice(block % per_q * sub, (block % per_q + 1) * sub)
            grad = (dqs[block // per_q, :, lanes] * scale).T.astype(BF)
            dproj_ref[tp_rank ^ rank, j - q_first * per_q // ranks, :, :HEAD_PAD] = grad


SMEM = pl.BlockSpec(memory_space=pltpu.SMEM)
VMEM = pl.BlockSpec(memory_space=pltpu.VMEM)
PARAMS = pltpu.CompilerParams(vmem_limit_bytes=VMEM_BYTES)


def attend(where, seg_q, seg_k, proj, keyvals):
    ranks, steps, sub, _ = proj.shape
    gathered = keyvals is not None
    q_len = ranks * steps * sub
    k_len = q_len * (keyvals.shape[0] if gathered else 1)
    q_first, q_last = seg_q[::BQ], seg_q[BQ - 1 :: BQ]
    k_first, k_last = seg_k[::BK], seg_k[BK - 1 :: BK]
    k_index = jnp.arange(k_len // BK)
    bound = where[1] * (q_len // BK) + jnp.arange(q_len // BQ) * (BQ // BK)
    before = k_index[None, :] < bound[:, None]
    first = jnp.sum(before & (k_last[None, :] < q_first[:, None]), axis=1).astype(jnp.int32)
    full = jnp.sum(before & (k_first[None, :] != q_last[:, None]), axis=1).astype(jnp.int32)
    inputs = (proj, keyvals) if gathered else (proj,)
    return pl.pallas_call(
        functools.partial(attend_kernel, gathered),
        out_shape=(
            jax.ShapeDtypeStruct((ranks, steps, sub, HEAD_PAD), BF),
            jax.ShapeDtypeStruct((q_len // BQ, 3, 8, BQ), F32),
        ),
        in_specs=[SMEM] * 3 + [VMEM] * (2 + len(inputs)),
        out_specs=(VMEM, VMEM),
        scratch_shapes=[
            pltpu.VMEM((q_len, 3 * LANES), BF),
            pltpu.VMEM((k_len, HEAD_PAD), BF),
            pltpu.VMEM((k_len, HEAD_PAD), BF),
        ],
        compiler_params=PARAMS,
        cost_estimate=pl.CostEstimate(
            flops=16 * q_len * k_len * 256, bytes_accessed=8 * q_len * 1024, transcendentals=3 * q_len * k_len // 2
        ),
        name="attend",
    )(where, first, jnp.maximum(full, first), seg_q[:, None], seg_k[None, :], *inputs)


def attend_back(where, seg_q, seg_k, proj, keyvals, attended, grad, lse, q_range, k_range, k_done, before=None):
    ranks, steps, sub, _ = proj.shape
    gathered = keyvals is not None
    q_len = ranks * steps * sub
    k_len = q_len * (keyvals.shape[0] if gathered else 1)
    q_first, q_last = seg_q[::BQ], seg_q[BQ - 1 :: BQ]
    k_first, k_last = seg_k[::BK], seg_k[BK - 1 :: BK]
    full = jnp.sum(q_last[None, :] <= k_first[:, None], axis=1).astype(jnp.int32)
    high = jnp.sum(q_first[None, :] <= k_last[:, None], axis=1).astype(jnp.int32)
    inputs = [attended, grad, lse, proj] + ([keyvals] if gathered else []) + ([before] if before is not None else [])
    part_steps = (q_range[1] - q_range[0]) * BQ // (ranks * sub)
    outs = [jax.ShapeDtypeStruct((ranks, part_steps, sub, proj.shape[3] if not gathered else HEAD_PAD), BF)]
    if gathered:
        outs.append(jax.ShapeDtypeStruct(keyvals.shape, BF))
    if k_done > k_range[0]:
        outs.append(jax.ShapeDtypeStruct((k_done * BK, 2 * HEAD_PAD), F32))
    return pl.pallas_call(
        functools.partial(attend_back_kernel, gathered, q_range, k_range, k_done, before is not None),
        out_shape=outs,
        in_specs=[SMEM] * 3 + [VMEM] * (2 + len(inputs)),
        out_specs=[VMEM] * len(outs),
        scratch_shapes=[
            pltpu.VMEM((q_len, 3 * LANES), BF),
            pltpu.VMEM((k_len, HEAD_PAD), BF),
            pltpu.VMEM((k_len, HEAD_PAD), BF),
            pltpu.VMEM((k_len // BK, HEAD_PAD, BK), BF),
            pltpu.VMEM((q_len, 3 * LANES), BF),
            pltpu.VMEM((q_len // BQ, HEAD_PAD, BQ), F32),
            pltpu.VMEM((q_len // BQ, 8, BQ), F32),
        ],
        compiler_params=PARAMS,
        cost_estimate=pl.CostEstimate(
            flops=12 * q_len * k_len * 256, bytes_accessed=16 * q_len * 1024, transcendentals=3 * q_len * k_len // 2
        ),
        name=f"attend_back_{q_range[0]}_{q_range[1]}",
    )(where, full, high, seg_q.reshape(-1, 1, BQ), seg_k[:, None], *inputs)


GELU_A, GELU_B = 0.7978845608028654, 0.044715
ORDER = (0, 2, 1, 3)


def row_mean(values):
    return jnp.mean(values, axis=-1, keepdims=True)


def middle_kernel(
    head_width, x_ref, m0, m1, m2, m3, cot_ref, vec_ref, up0, up1, up2, up3, down_even, down_odd,
    out_ref, gh_ref, do_ref, up_even_ref, up_odd_ref, down_even_ref, down_odd_ref, wout_even_ref, wout_odd_ref, small_ref,
    wu, wd, xhat, rstd, n2, act, gpre, mlp, dn2,
):
    at = pl.program_id(0)
    tokens, width = x_ref.shape
    units = wd.shape[0]
    chunk = 256
    merged = (m0, m1, m2, m3)
    ups = (up0, up1, up2, up3)
    downs = ((down_even, 0), (down_odd, 0), (down_even, 1), (down_odd, 1))
    bias_row = up0.shape[0] - 16

    @pl.when(at == 0)
    def _():
        gain, shift = vec_ref[0:1, :], vec_ref[1:2, :]
        for t in range(tokens // chunk):
            rows = slice(t * chunk, (t + 1) * chunk)
            hidden = x_ref[rows, :].astype(F32) + vec_ref[2:3, :]
            for s in range(4):
                hidden = hidden + dot_nn(merged[s][rows, :head_width], ups[s][units : units + head_width, :])
            center = hidden - row_mean(hidden)
            scale = lax.rsqrt(row_mean(center * center) + EPS)
            norm = center * scale
            xhat[rows, :] = norm
            rstd[rows, :] = jnp.broadcast_to(scale, (chunk, LANES))
            n2[rows, :] = (norm * gain + shift).astype(BF)
            mlp[rows, :] = hidden + vec_ref[3:4, :]
        dn2[...] = jnp.zeros_like(dn2)
        small_ref[...] = jnp.zeros_like(small_ref)

    for n, s in enumerate(ORDER):

        @pl.when(at == n)
        def _():
            wu[...] = ups[s][...]
            wd[...] = downs[s][0][downs[s][1]]

    slot = (at % 2) * 2 + at // 2
    bias = wu[bias_row : bias_row + 16, :][0:1].astype(F32)

    def tokens_step(t, total):
        rows = pl.ds(pl.multiple_of(t * chunk, chunk), chunk)
        pre = dot_nn(n2[rows, :], wu[:units, :]) + bias
        square = pre * pre
        tanh = jnp.tanh(GELU_A * pre * (1.0 + GELU_B * square))
        half = 0.5 * (1.0 + tanh)
        activ = (pre * half).astype(BF)
        act[rows, :] = activ
        mlp[rows, :] += dot_nn(activ, wd[...])
        slope = half + (0.5 * GELU_A) * pre * (1.0 - tanh * tanh) * (1.0 + (3.0 * GELU_B) * square)
        grad = (dot_nt(cot_ref[rows, :], wd[...]) * slope).astype(BF)
        gpre[rows, :] = grad
        dn2[rows, :] += dot_nt(grad, wu[:units, :])
        return total + jnp.sum(grad.astype(F32), axis=0, keepdims=True)

    total = lax.fori_loop(0, tokens // chunk, tokens_step, jnp.zeros((1, units), F32))
    for s in range(4):

        @pl.when(slot == s)
        def _():
            small_ref[4 + s : 5 + s, :] = total

    def weight_grads(up_out, down_out):
        for c in range(units // chunk):
            rows = slice(c * chunk, (c + 1) * chunk)
            down_out[0, rows, :] = dot_tn(act[:, rows], cot_ref[...]).astype(BF)
        for c in range(width // chunk):
            rows = slice(c * chunk, (c + 1) * chunk)
            up_out[0, rows, :] = dot_tn(n2[:, rows], gpre[...]).astype(BF)

    @pl.when(at < 2)
    def _():
        weight_grads(up_even_ref, down_even_ref)

    @pl.when(at >= 2)
    def _():
        weight_grads(up_odd_ref, down_odd_ref)

    @pl.when(at == 3)
    def _():
        gain = vec_ref[0:1, :]
        for t in range(tokens // chunk):
            rows = slice(t * chunk, (t + 1) * chunk)
            out_ref[rows, :] = mlp[rows, :].astype(BF)
            grad, norm, cot = dn2[rows, :], xhat[rows, :], cot_ref[rows, :].astype(F32)
            gg = grad * gain
            inner = gg - row_mean(gg) - norm * row_mean(gg * norm)
            hidden = cot + rstd[rows, 0:1] * inner
            gh_ref[rows, :] = hidden
            small_ref[0:1, :] += jnp.sum(grad * norm, axis=0, keepdims=True)
            small_ref[1:2, :] += jnp.sum(grad, axis=0, keepdims=True)
            small_ref[2:3, :] += jnp.sum(hidden, axis=0, keepdims=True)
            small_ref[3:4, :] += jnp.sum(cot, axis=0, keepdims=True)
            branch = hidden.astype(BF)
            gpre[rows, :width] = branch
            for s in range(4):
                back = dot_nt(branch, ups[s][units : units + head_width, :]).astype(BF)
                do_ref[s, rows, :head_width] = back
                do_ref[s, rows, head_width:] = jnp.zeros((chunk, HEAD_PAD - head_width), BF)
        for s in range(4):
            target = (wout_even_ref, wout_odd_ref)[s % 2]
            target[s // 2] = dot_tn(merged[s][...], gpre[:, :width])[:head_width].astype(BF)


def middle(head_width, x_rows, merged, cot_rows, vectors, ups, down_even, down_odd):
    tokens, width = x_rows.shape
    units = down_even.shape[1]
    whole = lambda shape: pl.BlockSpec(shape, lambda at: (0,) * len(shape))
    early = lambda at: (jnp.minimum(at, 1), 0, 0)
    late = lambda at: (jnp.maximum(at - 2, 0), 0, 0)
    once = lambda value: pl.BlockSpec(value.shape, lambda at: (0,) * value.ndim, pipeline_mode=pl.Buffered(1))
    struct = jax.ShapeDtypeStruct
    return pl.pallas_call(
        functools.partial(middle_kernel, head_width),
        grid=(4,),
        out_shape=(
            struct((tokens, width), BF),
            struct((tokens, width), F32),
            struct((4, tokens, HEAD_PAD), BF),
            struct((2, width, units), BF),
            struct((2, width, units), BF),
            struct((2, units, width), BF),
            struct((2, units, width), BF),
            struct((2, head_width, width), BF),
            struct((2, head_width, width), BF),
            struct((8, width), F32),
        ),
        in_specs=[whole((tokens, width))]
        + [whole((tokens, HEAD_PAD))] * 4
        + [whole((tokens, width)), whole(vectors.shape)]
        + [once(value) for value in (*ups, down_even, down_odd)],
        out_specs=(
            whole((tokens, width)),
            whole((tokens, width)),
            whole((4, tokens, HEAD_PAD)),
            pl.BlockSpec((1, width, units), early),
            pl.BlockSpec((1, width, units), late),
            pl.BlockSpec((1, units, width), early),
            pl.BlockSpec((1, units, width), late),
            whole((2, head_width, width)),
            whole((2, head_width, width)),
            whole((8, width)),
        ),
        scratch_shapes=[
            pltpu.VMEM(ups[0].shape, BF),
            pltpu.VMEM((units, width), BF),
            pltpu.VMEM((tokens, width), F32),
            pltpu.VMEM((tokens, LANES), F32),
            pltpu.VMEM((tokens, width), BF),
            pltpu.VMEM((tokens, units), BF),
            pltpu.VMEM((tokens, units), BF),
            pltpu.VMEM((tokens, width), F32),
            pltpu.VMEM((tokens, width), F32),
        ],
        compiler_params=PARAMS,
        cost_estimate=pl.CostEstimate(
            flops=60 * tokens * width * units, bytes_accessed=12 * units * width, transcendentals=4 * tokens * units
        ),
        name="middle",
    )(x_rows, *merged, cot_rows, vectors, *ups, down_even, down_odd)


def norm_parts(values):
    center = values - row_mean(values)
    rstd = lax.rsqrt(row_mean(center * center) + EPS)
    return center * rstd, rstd


def norm_back(xhat, rstd, gain, grad):
    gg = grad * gain
    return rstd * (gg - row_mean(gg) - xhat * row_mean(gg * xhat))


def pick(array, index, axis):
    return lax.dynamic_index_in_dim(array, index, axis, keepdims=False)


def on_device(
    block_in, segments, ln1_gain, ln1_shift, w_qkv, b_qv, w_out, b_out, ln2_gain, ln2_shift, w_up, b_up, w_down, b_down, cotangent
):
    seqs, sub, width = block_in.shape
    ranks, fsdp, ctx_size = lax.axis_size("tp"), lax.axis_size("fsdp"), lax.axis_size("ctx")
    parts = ctx_size // seqs
    tp_rank, ctx_rank, fsdp_rank = lax.axis_index("tp"), lax.axis_index("ctx"), lax.axis_index("fsdp")
    heads = b_qv.shape[0]
    head_width = heads * 64
    own = seqs * sub
    tokens = ranks * own
    shard = ln1_gain.shape[0]

    x_blocks = to_sequence(block_in)
    down_far = swap(w_down, "tp", 2)
    x_blocks, down_far = lax.optimization_barrier((x_blocks, down_far))
    x_own = x_blocks.reshape(own, width)

    vectors = [ln1_gain, ln1_shift, b_out, ln2_gain, ln2_shift, b_down, b_qv.reshape(-1), b_up.reshape(-1)]
    rows = jnp.stack([jnp.pad(v, (0, shard - v.shape[0])) for v in vectors])
    (small,) = gather_fsdp([rows[None]], 0)
    (qkv_mat,) = gather_fsdp([w_qkv], 1)
    gain_one, shift_one, out_bias, gain_two, shift_two, down_bias = (
        small[:, n].reshape(-1).astype(F32) for n in range(6)
    )
    qv_bias = small[:, 6, : b_qv.size].reshape((fsdp,) + b_qv.shape)
    qv_bias = qv_bias.transpose(1, 0, 2).reshape(heads, -1).astype(F32)
    up_bias = small[:, 7, : b_up.size].reshape((fsdp,) + b_up.shape).transpose(1, 0, 2).reshape(1, -1)
    extra = HEAD_PAD - head_width
    qkv_pad = jnp.pad(qkv_mat, ((0, 0), (0, extra), (0, 0))).reshape(3 * HEAD_PAD, width)
    bias_rows = jnp.stack(
        [qv_bias[:, :64].reshape(-1), jnp.zeros((head_width,), F32), qv_bias[:, 64:].reshape(-1)]
    )
    qkv_bias = jnp.pad(bias_rows, ((0, 0), (0, extra))).reshape(-1)

    up_rows, out_rows = gather_fsdp([w_up, w_out], 0)
    up_own = jnp.concatenate([up_rows, out_rows, jnp.pad(up_bias, ((0, 15), (0, 0)))], axis=0)
    down_pair = jnp.stack([w_down, down_far])

    x_float = x_own.astype(F32)
    xhat_one, rstd_one = norm_parts(x_float)
    normed_own = (xhat_one * gain_one + shift_one).astype(BF)
    normed_own, cotangent = lax.optimization_barrier((normed_own, cotangent))
    cot_rows = to_sequence(cotangent)
    normed_one = jnp.concatenate(gather_tp(normed_own), axis=0)
    normed_one, up_own, down_pair, cot_rows = lax.optimization_barrier(
        (normed_one, up_own, down_pair, cot_rows)
    )
    cot_rows = cot_rows.reshape(own, width)
    proj = (dot_nt(normed_one, qkv_pad) + qkv_bias).astype(BF).reshape(ranks, seqs, sub, 3 * HEAD_PAD)
    up_side = swap(up_own, "tp", 1)
    keyvals = None
    groups = [[g * parts + p for p in range(parts)] for g in range(ctx_size // parts)]
    if parts > 1:
        keyvals = lax.all_gather(
            proj[None, ..., HEAD_PAD:], "ctx", axis=0, tiled=True, axis_index_groups=groups
        )
    seq_rank, part = ctx_rank // parts, ctx_rank % parts
    where = jnp.stack([tp_rank, part]).astype(jnp.int32)
    seg_k = pick(segments, seq_rank, 0)
    seg_q = lax.dynamic_slice_in_dim(seg_k, part * tokens, tokens, 0)
    attended, lse = attend(where, seg_q, seg_k, proj, keyvals)

    up_far = swap(up_own, "tp", 2)
    (down_even,) = gather_fsdp([down_pair], 1)
    attended, up_far, up_side, down_even = lax.optimization_barrier(
        (attended, up_far, up_side, down_even)
    )
    ups = [up_own, up_side, up_far, swap(up_far, "tp", 1)]
    down_odd = swap(down_even, "tp", 1)

    slots = attended.reshape(ranks, own, HEAD_PAD)
    merged = [slots[0]] + [swap(slots[s], "tp", s) for s in range(1, ranks)]
    vecs = jnp.stack([gain_two, shift_two, out_bias, down_bias])
    vecs = jnp.pad(vecs, ((0, 4), (0, 0)))
    (
        block_out, grad_hidden, grad_slots, up_even, up_odd, down_even_g, down_odd_g, out_even, out_odd, sums,
    ) = middle(head_width, x_own, merged, cot_rows, vecs, ups, down_even, down_odd)
    grad_slots = [grad_slots[0]] + [swap(grad_slots[s], "tp", s) for s in range(1, ranks)]
    grad_attended = jnp.stack(grad_slots).reshape(ranks, seqs, sub, HEAD_PAD)

    up_near = add_low(up_even, swap(up_odd, "tp", 1))
    down_near = add_low(down_even_g, swap(down_odd_g, "tp", 1))
    grad_attended, up_near, down_near, block_out, out_even, out_odd = lax.optimization_barrier(
        (grad_attended, up_near, down_near, block_out, out_even, out_odd)
    )
    out_blocks = from_sequence(block_out.reshape(seqs, sub, width))

    up_mid = add_low(up_near[0], swap(up_near[1], "tp", 2))
    down_mid = scatter_fsdp(down_near.reshape(2, fsdp, -1, width).transpose(1, 0, 2, 3))

    q_blocks = tokens // BQ
    back = functools.partial(attend_back, where, seg_q, seg_k, proj, keyvals, attended)
    if parts > 1:
        dq, dkv = back(grad_attended, lse, (0, q_blocks), (0, parts * q_blocks), 0)
        dkv = lax.psum_scatter(
            dkv, "ctx", scatter_dimension=0, tiled=True, axis_index_groups=groups
        )
        halves = [jnp.concatenate([dq, dkv.reshape(ranks, seqs, sub, 2 * HEAD_PAD)], axis=-1)]
        edges = [0, seqs]
    else:
        mid = q_blocks // 2
        high, rest = back(grad_attended, lse, (mid, q_blocks), (0, q_blocks), mid)
        rest, high, up_mid, down_mid, out_even, out_odd, out_blocks = lax.optimization_barrier(
            (rest, high, up_mid, down_mid, out_even, out_odd, out_blocks)
        )
        (low,) = back(grad_attended, lse, (0, mid), (0, mid), 0, rest)
        halves = [low, high]
        edges = [0, mid * BQ // (ranks * sub), seqs]

    up_last = scatter_fsdp(up_mid.reshape(fsdp, -1, up_mid.shape[1]))
    down_last = add_low(down_mid[0], swap(down_mid[1], "tp", 2))
    out_near = add_low(out_even, swap(out_odd, "tp", 1))
    grad_rows = [None] * len(halves)

    def back_rows(half):
        rows = dot_nn(half.reshape(-1, 3 * HEAD_PAD), qkv_pad).astype(BF).reshape(ranks, -1, width)
        return near_sums([rows[s] for s in range(ranks)])

    if parts == 1:
        grad_rows[1] = back_rows(halves[1])
        halves[0], grad_rows[1], up_last, down_last, out_near = lax.optimization_barrier(
            (halves[0], grad_rows[1], up_last, down_last, out_near)
        )
    grad_rows[0] = back_rows(halves[0])
    out_mid = add_low(out_near[0], swap(out_near[1], "tp", 2))
    total = sum_ctx(jnp.concatenate([up_last, down_last], axis=0))
    sum_up, sum_down = total[: w_up.shape[0]], total[w_up.shape[0] :]

    normed_all = normed_one.reshape(ranks, seqs, sub, width)
    grad_qkv, grad_normed, bias_sum = 0.0, [], 0.0
    for n in reversed(range(len(halves))):
        rows = halves[n].reshape(-1, 3 * HEAD_PAD)
        grad_normed.insert(0, far_sum(*grad_rows[n]))
        seen = normed_all[:, edges[n] : edges[n + 1]].reshape(-1, width)
        grad_qkv = grad_qkv + dot_tn(rows, seen)
        bias_sum = bias_sum + jnp.sum(rows.astype(F32), axis=0)
    grad_normed_one = jnp.concatenate(grad_normed, axis=0)
    grad_x = grad_hidden + norm_back(xhat_one, rstd_one, gain_one, grad_normed_one)
    grad_blocks = from_sequence(grad_x.astype(BF).reshape(seqs, sub, width))

    grad_qkv = grad_qkv.reshape(3, HEAD_PAD, width)[:, :head_width].astype(BF)
    both = jnp.concatenate([grad_qkv, out_mid[None]]).reshape(4, fsdp, -1, width).transpose(1, 0, 2, 3)
    total = sum_ctx(scatter_fsdp(both).reshape(-1, width))
    sum_qkv, sum_out = total[: -w_out.shape[0]].reshape(w_qkv.shape), total[-w_out.shape[0] :]

    bias_sum = bias_sum.reshape(3, HEAD_PAD)[:, :head_width].reshape(3, heads, 64)
    bias_rows = jnp.concatenate([bias_sum[0], bias_sum[2]], axis=1)
    bias_all = lax.dynamic_update_slice(
        jnp.zeros((ranks * heads, 128), F32), bias_rows, (tp_rank * heads, 0)
    )
    up_bias_all = jnp.zeros((ranks, width), F32)
    for s in range(ranks):
        up_bias_all = lax.dynamic_update_slice(up_bias_all, sums[4 + s : 5 + s], (tp_rank ^ s, 0))
    ln1_sums = jnp.stack([jnp.sum(grad_normed_one * xhat_one, axis=0), jnp.sum(grad_normed_one, axis=0)])
    late = jnp.concatenate(
        [sums[:4].reshape(-1, LANES), up_bias_all.reshape(-1, LANES), ln1_sums.reshape(-1, LANES), bias_all]
    )
    for axis in ("tp", "ctx", "fsdp"):
        late = butterfly(late, axis)
    late_rows = late[: 10 * width // LANES].reshape(10, fsdp, shard)

    def mine_bias(rows, like):
        rows = lax.dynamic_slice_in_dim(rows, tp_rank * like.shape[0], like.shape[0], 0)
        return lax.dynamic_slice_in_dim(rows, fsdp_rank * like.shape[1], like.shape[1], 1)

    vector_sums = pick(late_rows, fsdp_rank, 1)
    sum_qv_bias = mine_bias(late[10 * width // LANES :], b_qv)
    up_bias_rows = late[4 * width // LANES : 8 * width // LANES]
    sum_up_bias = mine_bias(up_bias_rows.reshape(ranks * b_up.shape[0], -1), b_up)
    return (
        out_blocks, grad_blocks, vector_sums[8], vector_sums[9], sum_qkv, sum_qv_bias, sum_out, vector_sums[2],
        vector_sums[0], vector_sums[1], sum_up, sum_up_bias, sum_down, vector_sums[3],
    )


def solution(mesh):
    rows = P("fsdp", ("ctx", "tp"), None)
    vector = P("fsdp")
    out_rows = P(("tp", "fsdp"), None)
    qkv_rows = P(None, ("tp", "fsdp"), None)
    bias = P("tp", "fsdp")
    weights = (
        vector, vector, qkv_rows, bias, out_rows, vector, vector, vector, P("fsdp", "tp"), bias, out_rows, vector,
    )
    return jax.shard_map(
        on_device,
        mesh=mesh,
        in_specs=(rows, P("fsdp", None)) + weights + (rows,),
        out_specs=(rows, rows) + weights,
        check_vma=False,
    )
```

```python
import functools

import jax
import jax.numpy as jnp
from jax import lax
from jax.experimental import pallas as pl
from jax.experimental.pallas import tpu as pltpu
from jax.sharding import PartitionSpec as P

EPS = 1e-05
NEG = -1e30
BF = jnp.bfloat16
F32 = jnp.float32
LANES = 128
HEAD_PAD = 256
BQ = 512
BK = 512
VMEM_BYTES = 48 * 1024 * 1024


def dot_nn(left, right):
    return lax.dot_general(left, right, (((1,), (0,)), ((), ())), preferred_element_type=F32)


def dot_nt(left, right):
    return lax.dot_general(left, right, (((1,), (1,)), ((), ())), preferred_element_type=F32)


def dot_tn(left, right):
    return lax.dot_general(left, right, (((0,), (0,)), ((), ())), preferred_element_type=F32)


def swap(value, axis, bit):
    size = lax.axis_size(axis)
    return lax.ppermute(value, axis, [(i, i ^ bit) for i in range(size)])


def tree_sum(items):
    items = [item.astype(F32) for item in items]
    while len(items) > 1:
        items = [items[i] + items[i + 1] for i in range(0, len(items), 2)]
    return items[0]


def butterfly(value, axis):
    size = lax.axis_size(axis)
    if size & (size - 1):
        return lax.psum(value, axis)
    return tree_sum([value] + [swap(value, axis, bit) for bit in range(1, size)])


def gather_fsdp(values, axis):
    if lax.axis_size("fsdp") != 2:
        return [lax.all_gather(value, "fsdp", axis=axis, tiled=True) for value in values]
    whole = values[0] if len(values) == 1 else jnp.concatenate(values, axis=axis)
    other = swap(whole, "fsdp", 1)
    first = lax.axis_index("fsdp") == 0
    out, start = [], 0
    for value in values:
        size = value.shape[axis]
        theirs = lax.slice_in_dim(other, start, start + size, axis=axis)
        start += size
        pair = [jnp.where(first, value, theirs), jnp.where(first, theirs, value)]
        out.append(jnp.concatenate(pair, axis=axis))
    return out


def scatter_fsdp(value):
    if lax.axis_size("fsdp") != 2:
        return lax.psum_scatter(value, "fsdp", scatter_dimension=0, tiled=False)
    rank = lax.axis_index("fsdp")
    mine = lax.dynamic_index_in_dim(value, rank, 0, keepdims=False)
    theirs = lax.dynamic_index_in_dim(value, 1 - rank, 0, keepdims=False)
    return (mine.astype(F32) + swap(theirs, "fsdp", 1).astype(F32)).astype(value.dtype)


def scatter_pair(value, split):
    size = lax.axis_size("fsdp")
    pieces = [part.reshape((size, -1) + part.shape[1:]) for part in (value[:split], value[split:])]
    if size != 2:
        return jnp.concatenate([scatter_fsdp(piece) for piece in pieces], axis=0)
    rank = lax.axis_index("fsdp")

    def cut(index):
        both = [lax.dynamic_index_in_dim(piece, index, 0, keepdims=False) for piece in pieces]
        return jnp.concatenate(both, axis=0)

    return (cut(rank).astype(F32) + swap(cut(1 - rank), "fsdp", 1).astype(F32)).astype(value.dtype)


def ctx_plan(rows):
    size = lax.axis_size("ctx")
    return size == 4 and rows % (8 * size) == 0


def ctx_reduce(value):
    if not ctx_plan(value.shape[0]):
        return lax.psum(value, "ctx")
    rank = lax.axis_index("ctx")

    def halve(array, axis, bit, side):
        mine = lax.dynamic_index_in_dim(array, side, axis, keepdims=False)
        theirs = lax.dynamic_index_in_dim(array, 1 - side, axis, keepdims=False)
        return (mine.astype(F32) + swap(theirs, "ctx", bit).astype(F32)).astype(value.dtype)

    parts = value.reshape((2, 2, value.shape[0] // 4) + value.shape[1:])
    return halve(halve(parts, 1, 1, rank % 2), 0, 2, rank // 2)


def ctx_spread(total, rows):
    if not ctx_plan(rows):
        return total.astype(F32)
    rank = lax.axis_index("ctx")

    def double(array, axis, bit, side):
        other = swap(array, "ctx", bit)
        first = side == 0
        return jnp.stack(
            [jnp.where(first, array, other), jnp.where(first, other, array)], axis=axis
        )

    total = double(double(total, 0, 2, rank // 2), 1, 1, rank % 2)
    return total.reshape((rows,) + total.shape[3:]).astype(F32)


def gather_tp(value):
    far = swap(value, "tp", 2)
    return [value, swap(value, "tp", 1), far, swap(far, "tp", 1)]


def add_low(left, right):
    return (left.astype(F32) + right.astype(F32)).astype(BF)


def near_sums(slots):
    return [add_low(slots[n], swap(slots[n + 1], "tp", 1)) for n in (0, 2)]


def far_sum(near, far):
    return near.astype(F32) + swap(far, "tp", 2).astype(F32)


def seq_steps(seqs):
    size = lax.axis_size("ctx")
    groups = size // seqs
    return [
        [(src, ((src % seqs + step) % seqs) * groups + src // seqs) for src in range(size)]
        for step in range(seqs)
    ]


def send(value, pairs):
    if all(src == dst for src, dst in pairs):
        return value
    return lax.ppermute(value, "ctx", pairs)


def to_sequence(value):
    seqs = value.shape[0]
    size = lax.axis_size("ctx")
    base = lax.axis_index("ctx") % seqs
    owner = lax.axis_index("ctx") // (size // seqs)
    out = jnp.zeros_like(value)
    for step, pairs in enumerate(seq_steps(seqs)):
        block = lax.dynamic_index_in_dim(value, (base + step) % seqs, 0, keepdims=True)
        place = (owner - step + seqs) % seqs
        out = lax.dynamic_update_slice_in_dim(out, send(block, pairs), place, 0)
    return out


def from_sequence(value):
    seqs = value.shape[0]
    size = lax.axis_size("ctx")
    base = lax.axis_index("ctx") % seqs
    owner = lax.axis_index("ctx") // (size // seqs)
    out = jnp.zeros_like(value)
    for step, pairs in enumerate(seq_steps(seqs)):
        block = lax.dynamic_index_in_dim(value, (owner - step + seqs) % seqs, 0, keepdims=True)
        block = send(block, [(dst, src) for src, dst in pairs])
        out = lax.dynamic_update_slice_in_dim(out, block, (base + step) % seqs, 0)
    return out


def lane_is_low(rows):
    return lax.broadcasted_iota(jnp.int32, (rows, LANES), 1) < LANES // 2


def pieces(dims):
    ranks, steps = dims
    return [(j * ranks + rank, j, rank) for j in range(steps) for rank in range(ranks)]


def allowed_block(seg_row, seg_col, q_axis, q_start, k_start, shape):
    q_at = q_start + lax.broadcasted_iota(jnp.int32, shape, q_axis)
    k_at = k_start + lax.broadcasted_iota(jnp.int32, shape, 1 - q_axis)
    return (seg_row == seg_col) & (k_at <= q_at)


def split_heads(tile, target, rows, low):
    head_pair = tile[:, :LANES]
    zero = jnp.zeros_like(head_pair)
    target[rows, 0:128] = jnp.where(low, head_pair, zero)
    target[rows, 128:256] = jnp.where(low, zero, head_pair)
    target[rows, 256:384] = tile[:, LANES:]


def attend_kernel(gathered, where_ref, low_ref, full_ref, seg_q_ref, seg_k_ref, proj_ref, *refs):
    kv_ref = refs[0] if gathered else None
    o_ref, lse_ref, qs, ks, vs = refs[1:] if gathered else refs
    ranks, steps, sub, _ = proj_ref.shape
    parts = kv_ref.shape[0] if gathered else 1
    tp_rank, part = where_ref[0], where_ref[1]
    q_len = ranks * steps * sub
    scale = 64 ** (-0.5)
    low = lane_is_low(sub)
    for block, j, rank in pieces((ranks, steps)):
        slot = tp_rank ^ rank
        rows = slice(block * sub, (block + 1) * sub)
        tile = (proj_ref[slot, j, :, :HEAD_PAD].astype(F32) * scale).astype(BF)
        split_heads(tile, qs, rows, low)
        for p in range(parts):
            at = slice(p * q_len + block * sub, p * q_len + (block + 1) * sub)
            both = kv_ref[p, slot, j] if gathered else proj_ref[slot, j, :, HEAD_PAD:]
            ks[at, :] = both[:, :HEAD_PAD]
            vs[at, :] = both[:, HEAD_PAD:]

    def q_block(i, _):
        q_row = pl.multiple_of(i * BQ, BQ)
        q_first = part * q_len + q_row
        seg_q = seg_q_ref[pl.ds(q_row, BQ), :]

        def step(masked, kk, carry):
            k_row = pl.multiple_of(kk * BK, BK)
            keys = ks[pl.ds(k_row, BK), :]
            vals = vs[pl.ds(k_row, BK), :]
            if masked:
                ok = allowed_block(seg_q, seg_k_ref[:, pl.ds(k_row, BK)], 0, q_first, k_row, (BQ, BK))
            out = []
            for h in range(3):
                top, total, acc = carry[h]
                lanes = slice((h // 2) * LANES, (h // 2 + 1) * LANES)
                scores = dot_nt(qs[pl.ds(q_row, BQ), h * LANES : (h + 1) * LANES], keys[:, lanes])
                if masked:
                    scores = jnp.where(ok, scores, NEG)
                new_top = jnp.maximum(top, jnp.max(scores, axis=1, keepdims=True))
                probs = jnp.exp(scores - new_top)
                shrink = jnp.exp(top - new_top)
                total = total * shrink + jnp.sum(probs, axis=1, keepdims=True)
                acc = acc * shrink + dot_nn(probs.astype(BF), vals[:, lanes])
                out.append((new_top, total, acc))
            return tuple(out)

        start = tuple(
            (jnp.full((BQ, 1), NEG, F32), jnp.zeros((BQ, 1), F32), jnp.zeros((BQ, LANES), F32))
            for _ in range(3)
        )
        first, full = low_ref[i], full_ref[i]
        last = q_first // BK
        carry = lax.fori_loop(first, full, functools.partial(step, True), start)
        carry = lax.fori_loop(full, last, functools.partial(step, False), carry)
        carry = lax.fori_loop(last, last + BQ // BK, functools.partial(step, True), carry)
        heads = [acc / total for _, total, acc in carry]
        pair = jnp.where(lane_is_low(BQ), heads[0], heads[1]).astype(BF)
        third = heads[2].astype(BF)
        for n in range(BQ // sub):
            block = i * (BQ // sub) + n
            slot, j = tp_rank ^ lax.rem(block, ranks), block // ranks
            o_ref[slot, j, :, 0:128] = pair[n * sub : (n + 1) * sub]
            o_ref[slot, j, :, 128:256] = third[n * sub : (n + 1) * sub]
        for h in range(3):
            top, total, _ = carry[h]
            column = jnp.broadcast_to(top + jnp.log(total), (BQ, LANES))
            lse_ref[i, h] = column.T[0:8]
        return 0

    lax.fori_loop(0, q_len // BQ, q_block, 0)


def attend_back_kernel(
    gathered, q_range, k_range, k_done, more, where_ref, full_ref, high_ref, seg_q_ref, seg_k_ref, o_ref, do_ref, lse_ref, proj_ref, *refs
):
    refs = list(refs)
    kv_ref = refs.pop(0) if gathered else None
    sum_ref = refs.pop(0) if more else None
    dproj_ref = refs.pop(0)
    dkv_ref = refs.pop(0) if gathered else None
    rest_ref = refs.pop(0) if k_done > k_range[0] else None
    qs, ks, vs, kt, dos, dqs, delta = refs
    ranks, steps, sub, _ = proj_ref.shape
    parts = kv_ref.shape[0] if gathered else 1
    tp_rank, part = where_ref[0], where_ref[1]
    q_len = ranks * steps * sub
    scale = 64 ** (-0.5)
    low = lane_is_low(sub)
    q_first, q_end = q_range
    per_q = BQ // sub

    for block, j, rank in pieces((ranks, steps)):
        slot = tp_rank ^ rank
        rows = slice(block * sub, (block + 1) * sub)
        if q_first * per_q <= block < q_end * per_q:
            split_heads((proj_ref[slot, j, :, :HEAD_PAD].astype(F32) * scale).astype(BF), qs, rows, low)
            grad = do_ref[slot, j]
            split_heads(grad, dos, rows, low)
            product = grad.astype(F32) * o_ref[slot, j].astype(F32)
            pair, third = product[:, :LANES].T, product[:, LANES:].T
            lanes = slice(rows.start % BQ, rows.start % BQ + sub)
            for h, part_of in enumerate((pair[:64], pair[64:], third[:64])):
                delta[block // per_q, h : h + 1, lanes] = jnp.sum(part_of, axis=0, keepdims=True)
        for p in range(parts):
            if not k_range[0] * BK <= p * q_len + block * sub < k_range[1] * BK:
                continue
            at = slice(p * q_len + block * sub, p * q_len + (block + 1) * sub)
            both = kv_ref[p, slot, j] if gathered else proj_ref[slot, j, :, HEAD_PAD:]
            ks[at, :] = both[:, :HEAD_PAD]
            vs[at, :] = both[:, HEAD_PAD:]
            kt[at.start // BK, :, at.start % BK : at.start % BK + sub] = both[:, :HEAD_PAD].T
    dqs[...] = jnp.zeros_like(dqs)

    def k_block(kk, _):
        k_row = pl.multiple_of(kk * BK, BK)
        keys = ks[pl.ds(k_row, BK), :]
        vals = vs[pl.ds(k_row, BK), :]
        seg_k = seg_k_ref[pl.ds(k_row, BK), :]

        def step(masked, i, carry):
            q_row = pl.multiple_of(i * BQ, BQ)
            at = pl.ds(q_row, BQ)
            if masked:
                ok = allowed_block(seg_q_ref[i], seg_k, 1, part * q_len + q_row, k_row, (BK, BQ))
            dk, dv = list(carry[0]), list(carry[1])
            for h in range(3):
                t = h // 2
                lanes = slice(t * LANES, (t + 1) * LANES)
                mine = slice(h * LANES, (h + 1) * LANES)
                q_head, do_head = qs[at, mine], dos[at, mine]
                scores = dot_nt(keys[:, lanes], q_head)
                probs = jnp.exp(scores - lse_ref[i, h, 0:1, :])
                if masked:
                    probs = jnp.where(ok, probs, 0.0)
                grad_probs = dot_nt(vals[:, lanes], do_head)
                grad_scores = (probs * (grad_probs - delta[i, h : h + 1, :])).astype(BF)
                dv[t] = dv[t] + dot_nn(probs.astype(BF), do_head)
                dk[t] = dk[t] + dot_nn(grad_scores, q_head)
                rows = slice(h * 64, (h + 1) * 64)
                dqs[i, rows, :] += dot_nn(kt[kk, rows, :], grad_scores)
            return tuple(dk), tuple(dv)

        zero = jnp.zeros((BK, LANES), F32)
        carry = ((zero, zero), (zero, zero))
        if more:
            pieces_in = [sum_ref[pl.ds(k_row, BK), t * LANES : (t + 1) * LANES] for t in range(4)]
            carry = (tuple(pieces_in[:2]), tuple(pieces_in[2:]))
        ahead = kk - part * (q_len // BQ)
        inside = lambda value: jnp.clip(value, q_first, q_end)
        first = inside(ahead)
        diagonal = jnp.where(ahead >= 0, inside(ahead + 1), first)
        full = jnp.maximum(inside(full_ref[kk]), diagonal)
        high = jnp.maximum(inside(high_ref[kk]), full)
        carry = lax.fori_loop(first, diagonal, functools.partial(step, True), carry)
        carry = lax.fori_loop(diagonal, full, functools.partial(step, False), carry)
        carry = lax.fori_loop(full, high, functools.partial(step, True), carry)
        return carry[0] + carry[1]

    def finish(kk, _):
        sums = k_block(kk, 0)
        for n in range(BK // sub):
            block = lax.rem(kk, q_len // BK) * (BK // sub) + n
            slot, j = tp_rank ^ lax.rem(block, ranks), block // ranks
            for t in range(4):
                piece = sums[t][n * sub : (n + 1) * sub].astype(BF)
                lanes = slice(t * LANES, (t + 1) * LANES)
                if gathered:
                    dkv_ref[kk // (q_len // BK), slot, j, :, lanes] = piece
                else:
                    start = HEAD_PAD + t * LANES
                    dproj_ref[slot, j - k_done * BK // (ranks * sub), :, start : start + LANES] = piece
        return 0

    def keep(kk, _):
        sums = k_block(kk, 0)
        for t in range(4):
            rest_ref[pl.ds(pl.multiple_of(kk * BK, BK), BK), t * LANES : (t + 1) * LANES] = sums[t]
        return 0

    if rest_ref is not None:
        lax.fori_loop(k_range[0], k_done, keep, 0)
    lax.fori_loop(k_done, k_range[1], finish, 0)
    for block, j, rank in pieces((ranks, steps)):
        if q_first * per_q <= block < q_end * per_q:
            lanes = slice(block % per_q * sub, (block % per_q + 1) * sub)
            grad = (dqs[block // per_q, :, lanes] * scale).T.astype(BF)
            dproj_ref[tp_rank ^ rank, j - q_first * per_q // ranks, :, :HEAD_PAD] = grad


SMEM = pl.BlockSpec(memory_space=pltpu.SMEM)
VMEM = pl.BlockSpec(memory_space=pltpu.VMEM)
PARAMS = pltpu.CompilerParams(vmem_limit_bytes=VMEM_BYTES)


def attend(where, seg_q, seg_k, proj, keyvals):
    ranks, steps, sub, _ = proj.shape
    gathered = keyvals is not None
    q_len = ranks * steps * sub
    k_len = q_len * (keyvals.shape[0] if gathered else 1)
    q_first, q_last = seg_q[::BQ], seg_q[BQ - 1 :: BQ]
    k_first, k_last = seg_k[::BK], seg_k[BK - 1 :: BK]
    k_index = jnp.arange(k_len // BK)
    bound = where[1] * (q_len // BK) + jnp.arange(q_len // BQ) * (BQ // BK)
    before = k_index[None, :] < bound[:, None]
    first = jnp.sum(before & (k_last[None, :] < q_first[:, None]), axis=1).astype(jnp.int32)
    full = jnp.sum(before & (k_first[None, :] != q_last[:, None]), axis=1).astype(jnp.int32)
    inputs = (proj, keyvals) if gathered else (proj,)
    return pl.pallas_call(
        functools.partial(attend_kernel, gathered),
        out_shape=(
            jax.ShapeDtypeStruct((ranks, steps, sub, HEAD_PAD), BF),
            jax.ShapeDtypeStruct((q_len // BQ, 3, 8, BQ), F32),
        ),
        in_specs=[SMEM] * 3 + [VMEM] * (2 + len(inputs)),
        out_specs=(VMEM, VMEM),
        scratch_shapes=[
            pltpu.VMEM((q_len, 3 * LANES), BF),
            pltpu.VMEM((k_len, HEAD_PAD), BF),
            pltpu.VMEM((k_len, HEAD_PAD), BF),
        ],
        compiler_params=PARAMS,
        cost_estimate=pl.CostEstimate(
            flops=16 * q_len * k_len * 256, bytes_accessed=8 * q_len * 1024, transcendentals=3 * q_len * k_len // 2
        ),
        name="attend",
    )(where, first, jnp.maximum(full, first), seg_q[:, None], seg_k[None, :], *inputs)


def attend_back(where, seg_q, seg_k, proj, keyvals, attended, grad, lse, q_range, k_range, k_done, before=None):
    ranks, steps, sub, _ = proj.shape
    gathered = keyvals is not None
    q_len = ranks * steps * sub
    k_len = q_len * (keyvals.shape[0] if gathered else 1)
    q_first, q_last = seg_q[::BQ], seg_q[BQ - 1 :: BQ]
    k_first, k_last = seg_k[::BK], seg_k[BK - 1 :: BK]
    full = jnp.sum(q_last[None, :] <= k_first[:, None], axis=1).astype(jnp.int32)
    high = jnp.sum(q_first[None, :] <= k_last[:, None], axis=1).astype(jnp.int32)
    inputs = [attended, grad, lse, proj] + ([keyvals] if gathered else []) + ([before] if before is not None else [])
    part_steps = (q_range[1] - q_range[0]) * BQ // (ranks * sub)
    outs = [jax.ShapeDtypeStruct((ranks, part_steps, sub, proj.shape[3] if not gathered else HEAD_PAD), BF)]
    if gathered:
        outs.append(jax.ShapeDtypeStruct(keyvals.shape, BF))
    if k_done > k_range[0]:
        outs.append(jax.ShapeDtypeStruct((k_done * BK, 2 * HEAD_PAD), F32))
    return pl.pallas_call(
        functools.partial(attend_back_kernel, gathered, q_range, k_range, k_done, before is not None),
        out_shape=outs,
        in_specs=[SMEM] * 3 + [VMEM] * (2 + len(inputs)),
        out_specs=[VMEM] * len(outs),
        scratch_shapes=[
            pltpu.VMEM((q_len, 3 * LANES), BF),
            pltpu.VMEM((k_len, HEAD_PAD), BF),
            pltpu.VMEM((k_len, HEAD_PAD), BF),
            pltpu.VMEM((k_len // BK, HEAD_PAD, BK), BF),
            pltpu.VMEM((q_len, 3 * LANES), BF),
            pltpu.VMEM((q_len // BQ, HEAD_PAD, BQ), F32),
            pltpu.VMEM((q_len // BQ, 8, BQ), F32),
        ],
        compiler_params=PARAMS,
        cost_estimate=pl.CostEstimate(
            flops=12 * q_len * k_len * 256, bytes_accessed=16 * q_len * 1024, transcendentals=3 * q_len * k_len // 2
        ),
        name=f"attend_back_{q_range[0]}_{q_range[1]}",
    )(where, full, high, seg_q.reshape(-1, 1, BQ), seg_k[:, None], *inputs)


GELU_A, GELU_B = 0.7978845608028654, 0.044715
ORDER = (0, 2, 1, 3)


def row_mean(values):
    return jnp.mean(values, axis=-1, keepdims=True)


def middle_kernel(
    head_width, x_ref, m0, m1, m2, m3, cot_ref, vec_ref, up0, up1, up2, up3, down_even, down_odd,
    out_ref, gh_ref, do_ref, up_even_ref, up_odd_ref, down_even_ref, down_odd_ref, wout_even_ref, wout_odd_ref, small_ref,
    wu, wd, xhat, rstd, n2, act, gpre, mlp, dn2,
):
    at = pl.program_id(0)
    tokens, width = x_ref.shape
    units = wd.shape[0]
    chunk, wide = tokens, 256
    merged = (m0, m1, m2, m3)
    ups = (up0, up1, up2, up3)
    downs = ((down_even, 0), (down_odd, 0), (down_even, 1), (down_odd, 1))
    bias_row = up0.shape[0] - 16

    @pl.when(at == 0)
    def _():
        gain, shift = vec_ref[0:1, :], vec_ref[1:2, :]
        for t in range(tokens // chunk):
            rows = slice(t * chunk, (t + 1) * chunk)
            hidden = x_ref[rows, :].astype(F32) + vec_ref[2:3, :]
            for s in range(4):
                hidden = hidden + dot_nn(merged[s][rows, :head_width], ups[s][units : units + head_width, :])
            center = hidden - row_mean(hidden)
            scale = lax.rsqrt(row_mean(center * center) + EPS)
            norm = center * scale
            xhat[rows, :] = norm
            rstd[rows, :] = jnp.broadcast_to(scale, (chunk, LANES))
            n2[rows, :] = (norm * gain + shift).astype(BF)
            mlp[rows, :] = hidden + vec_ref[3:4, :]
        dn2[...] = jnp.zeros_like(dn2)
        small_ref[...] = jnp.zeros_like(small_ref)

    for n, s in enumerate(ORDER):

        @pl.when(at == n)
        def _():
            wu[...] = ups[s][...]
            wd[...] = downs[s][0][downs[s][1]]

    slot = (at % 2) * 2 + at // 2
    bias = wu[bias_row : bias_row + 16, :][0:1].astype(F32)

    def tokens_step(t, total):
        rows = pl.ds(pl.multiple_of(t * chunk, chunk), chunk)
        pre = dot_nn(n2[rows, :], wu[:units, :]) + bias
        square = pre * pre
        tanh = jnp.tanh(GELU_A * pre * (1.0 + GELU_B * square))
        half = 0.5 * (1.0 + tanh)
        activ = (pre * half).astype(BF)
        act[rows, :] = activ
        mlp[rows, :] += dot_nn(activ, wd[...])
        slope = half + (0.5 * GELU_A) * pre * (1.0 - tanh * tanh) * (1.0 + (3.0 * GELU_B) * square)
        grad = (dot_nt(cot_ref[rows, :], wd[...]) * slope).astype(BF)
        gpre[rows, :] = grad
        dn2[rows, :] += dot_nt(grad, wu[:units, :])
        return total + jnp.sum(grad.astype(F32), axis=0, keepdims=True)

    total = lax.fori_loop(0, tokens // chunk, tokens_step, jnp.zeros((1, units), F32))
    for s in range(4):

        @pl.when(slot == s)
        def _():
            small_ref[4 + s : 5 + s, :] = total

    def weight_grads(up_out, down_out):
        for c in range(units // wide):
            rows = slice(c * wide, (c + 1) * wide)
            down_out[0, rows, :] = dot_tn(act[:, rows], cot_ref[...]).astype(BF)
        for c in range(width // wide):
            rows = slice(c * wide, (c + 1) * wide)
            up_out[0, rows, :] = dot_tn(n2[:, rows], gpre[...]).astype(BF)

    @pl.when(at < 2)
    def _():
        weight_grads(up_even_ref, down_even_ref)

    @pl.when(at >= 2)
    def _():
        weight_grads(up_odd_ref, down_odd_ref)

    @pl.when(at == 3)
    def _():
        gain = vec_ref[0:1, :]
        for t in range(tokens // chunk):
            rows = slice(t * chunk, (t + 1) * chunk)
            out_ref[rows, :] = mlp[rows, :].astype(BF)
            grad, norm, cot = dn2[rows, :], xhat[rows, :], cot_ref[rows, :].astype(F32)
            gg = grad * gain
            inner = gg - row_mean(gg) - norm * row_mean(gg * norm)
            hidden = cot + rstd[rows, 0:1] * inner
            gh_ref[rows, :] = hidden
            small_ref[0:1, :] += jnp.sum(grad * norm, axis=0, keepdims=True)
            small_ref[1:2, :] += jnp.sum(grad, axis=0, keepdims=True)
            small_ref[2:3, :] += jnp.sum(hidden, axis=0, keepdims=True)
            small_ref[3:4, :] += jnp.sum(cot, axis=0, keepdims=True)
            branch = hidden.astype(BF)
            gpre[rows, :width] = branch
            for s in range(4):
                back = dot_nt(branch, ups[s][units : units + head_width, :]).astype(BF)
                do_ref[s, rows, :head_width] = back
                do_ref[s, rows, head_width:] = jnp.zeros((chunk, HEAD_PAD - head_width), BF)
        for s in range(4):
            target = (wout_even_ref, wout_odd_ref)[s % 2]
            target[s // 2] = dot_tn(merged[s][...], gpre[:, :width])[:head_width].astype(BF)


def middle(head_width, x_rows, merged, cot_rows, vectors, ups, down_even, down_odd):
    tokens, width = x_rows.shape
    units = down_even.shape[1]
    whole = lambda shape: pl.BlockSpec(shape, lambda at: (0,) * len(shape))
    early = lambda at: (jnp.minimum(at, 1), 0, 0)
    late = lambda at: (jnp.maximum(at - 2, 0), 0, 0)
    once = lambda value: pl.BlockSpec(value.shape, lambda at: (0,) * value.ndim, pipeline_mode=pl.Buffered(1))
    struct = jax.ShapeDtypeStruct
    return pl.pallas_call(
        functools.partial(middle_kernel, head_width),
        grid=(4,),
        out_shape=(
            struct((tokens, width), BF),
            struct((tokens, width), F32),
            struct((4, tokens, HEAD_PAD), BF),
            struct((2, width, units), BF),
            struct((2, width, units), BF),
            struct((2, units, width), BF),
            struct((2, units, width), BF),
            struct((2, head_width, width), BF),
            struct((2, head_width, width), BF),
            struct((8, width), F32),
        ),
        in_specs=[whole((tokens, width))]
        + [whole((tokens, HEAD_PAD))] * 4
        + [whole((tokens, width)), whole(vectors.shape)]
        + [once(value) for value in (*ups, down_even, down_odd)],
        out_specs=(
            whole((tokens, width)),
            whole((tokens, width)),
            whole((4, tokens, HEAD_PAD)),
            pl.BlockSpec((1, width, units), early),
            pl.BlockSpec((1, width, units), late),
            pl.BlockSpec((1, units, width), early),
            pl.BlockSpec((1, units, width), late),
            whole((2, head_width, width)),
            whole((2, head_width, width)),
            whole((8, width)),
        ),
        scratch_shapes=[
            pltpu.VMEM(ups[0].shape, BF),
            pltpu.VMEM((units, width), BF),
            pltpu.VMEM((tokens, width), F32),
            pltpu.VMEM((tokens, LANES), F32),
            pltpu.VMEM((tokens, width), BF),
            pltpu.VMEM((tokens, units), BF),
            pltpu.VMEM((tokens, units), BF),
            pltpu.VMEM((tokens, width), F32),
            pltpu.VMEM((tokens, width), F32),
        ],
        compiler_params=PARAMS,
        cost_estimate=pl.CostEstimate(
            flops=60 * tokens * width * units, bytes_accessed=12 * units * width, transcendentals=4 * tokens * units
        ),
        name="middle",
    )(x_rows, *merged, cot_rows, vectors, *ups, down_even, down_odd)


def norm_parts(values):
    center = values - row_mean(values)
    rstd = lax.rsqrt(row_mean(center * center) + EPS)
    return center * rstd, rstd


def norm_back(xhat, rstd, gain, grad):
    gg = grad * gain
    return rstd * (gg - row_mean(gg) - xhat * row_mean(gg * xhat))


def pick(array, index, axis):
    return lax.dynamic_index_in_dim(array, index, axis, keepdims=False)


def on_device(
    block_in, segments, ln1_gain, ln1_shift, w_qkv, b_qv, w_out, b_out, ln2_gain, ln2_shift, w_up, b_up, w_down, b_down, cotangent
):
    seqs, sub, width = block_in.shape
    ranks, fsdp, ctx_size = lax.axis_size("tp"), lax.axis_size("fsdp"), lax.axis_size("ctx")
    parts = ctx_size // seqs
    tp_rank, ctx_rank, fsdp_rank = lax.axis_index("tp"), lax.axis_index("ctx"), lax.axis_index("fsdp")
    heads = b_qv.shape[0]
    head_width = heads * 64
    own = seqs * sub
    tokens = ranks * own
    shard = ln1_gain.shape[0]

    x_blocks = to_sequence(block_in)
    down_far = swap(w_down, "tp", 2)
    x_blocks, down_far = lax.optimization_barrier((x_blocks, down_far))
    x_own = x_blocks.reshape(own, width)

    vectors = [ln1_gain, ln1_shift, b_out, ln2_gain, ln2_shift, b_down, b_qv.reshape(-1), b_up.reshape(-1)]
    rows = jnp.stack([jnp.pad(v, (0, shard - v.shape[0])) for v in vectors])
    (small,) = gather_fsdp([rows[None]], 0)
    (qkv_mat,) = gather_fsdp([w_qkv], 1)
    gain_one, shift_one, out_bias, gain_two, shift_two, down_bias = (
        small[:, n].reshape(-1).astype(F32) for n in range(6)
    )
    qv_bias = small[:, 6, : b_qv.size].reshape((fsdp,) + b_qv.shape)
    qv_bias = qv_bias.transpose(1, 0, 2).reshape(heads, -1).astype(F32)
    up_bias = small[:, 7, : b_up.size].reshape((fsdp,) + b_up.shape).transpose(1, 0, 2).reshape(1, -1)
    extra = HEAD_PAD - head_width
    qkv_pad = jnp.pad(qkv_mat, ((0, 0), (0, extra), (0, 0))).reshape(3 * HEAD_PAD, width)
    bias_rows = jnp.stack(
        [qv_bias[:, :64].reshape(-1), jnp.zeros((head_width,), F32), qv_bias[:, 64:].reshape(-1)]
    )
    qkv_bias = jnp.pad(bias_rows, ((0, 0), (0, extra))).reshape(-1)

    up_rows, out_rows = gather_fsdp([w_up, w_out], 0)
    up_own = jnp.concatenate([up_rows, out_rows, jnp.pad(up_bias, ((0, 15), (0, 0)))], axis=0)
    down_pair = jnp.stack([w_down, down_far])

    x_float = x_own.astype(F32)
    xhat_one, rstd_one = norm_parts(x_float)
    normed_own = (xhat_one * gain_one + shift_one).astype(BF)
    normed_own, cotangent = lax.optimization_barrier((normed_own, cotangent))
    cot_rows = to_sequence(cotangent)
    normed_one = jnp.concatenate(gather_tp(normed_own), axis=0)
    normed_one, up_own, down_pair, cot_rows = lax.optimization_barrier(
        (normed_one, up_own, down_pair, cot_rows)
    )
    cot_rows = cot_rows.reshape(own, width)
    proj = (dot_nt(normed_one, qkv_pad) + qkv_bias).astype(BF).reshape(ranks, seqs, sub, 3 * HEAD_PAD)
    up_side = swap(up_own, "tp", 1)
    keyvals = None
    groups = [[g * parts + p for p in range(parts)] for g in range(ctx_size // parts)]
    if parts > 1:
        keyvals = lax.all_gather(
            proj[None, ..., HEAD_PAD:], "ctx", axis=0, tiled=True, axis_index_groups=groups
        )
    seq_rank, part = ctx_rank // parts, ctx_rank % parts
    where = jnp.stack([tp_rank, part]).astype(jnp.int32)
    seg_k = pick(segments, seq_rank, 0)
    seg_q = lax.dynamic_slice_in_dim(seg_k, part * tokens, tokens, 0)
    attended, lse = attend(where, seg_q, seg_k, proj, keyvals)

    up_far = swap(up_own, "tp", 2)
    (down_even,) = gather_fsdp([down_pair], 1)
    attended, up_far, up_side, down_even = lax.optimization_barrier(
        (attended, up_far, up_side, down_even)
    )
    ups = [up_own, up_side, up_far, swap(up_far, "tp", 1)]
    down_odd = swap(down_even, "tp", 1)

    slots = attended.reshape(ranks, own, HEAD_PAD)
    merged = [slots[0]] + [swap(slots[s], "tp", s) for s in range(1, ranks)]
    vecs = jnp.stack([gain_two, shift_two, out_bias, down_bias])
    vecs = jnp.pad(vecs, ((0, 4), (0, 0)))
    (
        block_out, grad_hidden, grad_slots, up_even, up_odd, down_even_g, down_odd_g, out_even, out_odd, sums,
    ) = middle(head_width, x_own, merged, cot_rows, vecs, ups, down_even, down_odd)

    up_near = jnp.concatenate(
        [add_low(up_even, swap(up_odd, "tp", 1)), add_low(out_even, swap(out_odd, "tp", 1))], axis=1
    )
    down_near = add_low(down_even_g, swap(down_odd_g, "tp", 1))
    grad_slots = [grad_slots[s] for s in range(ranks)]
    grad_slots[1], up_near, down_near = lax.optimization_barrier((grad_slots[1], up_near, down_near))
    grad_slots = [grad_slots[0]] + [swap(grad_slots[s], "tp", s) for s in range(1, ranks)]
    grad_attended = jnp.stack(grad_slots).reshape(ranks, seqs, sub, HEAD_PAD)
    grad_attended, up_near, down_near, block_out = lax.optimization_barrier(
        (grad_attended, up_near, down_near, block_out)
    )
    out_blocks = from_sequence(block_out.reshape(seqs, sub, width))

    up_mid = add_low(up_near[0], swap(up_near[1], "tp", 2))
    down_mid = scatter_fsdp(down_near.reshape(2, fsdp, -1, width).transpose(1, 0, 2, 3))

    def project_back(half):
        return dot_nn(half.reshape(-1, 3 * HEAD_PAD), qkv_pad).astype(BF).reshape(ranks, -1, width)

    q_blocks = tokens // BQ
    back = functools.partial(attend_back, where, seg_q, seg_k, proj, keyvals, attended)
    if parts > 1:
        dq, dkv = back(grad_attended, lse, (0, q_blocks), (0, parts * q_blocks), 0)
        dkv = lax.psum_scatter(
            dkv, "ctx", scatter_dimension=0, tiled=True, axis_index_groups=groups
        )
        halves = [jnp.concatenate([dq, dkv.reshape(ranks, seqs, sub, 2 * HEAD_PAD)], axis=-1)]
        edges = [0, seqs]
    else:
        mid = q_blocks // 2
        high, rest = back(grad_attended, lse, (mid, q_blocks), (0, q_blocks), mid)
        rest, high, up_mid, down_mid, out_blocks = lax.optimization_barrier(
            (rest, high, up_mid, down_mid, out_blocks)
        )
        high_rows = project_back(high)
        rest, high_rows = lax.optimization_barrier((rest, high_rows))
        (low,) = back(grad_attended, lse, (0, mid), (0, mid), 0, rest)
        halves = [low, high]
        edges = [0, mid * BQ // (ranks * sub), seqs]

    up_last = scatter_pair(up_mid, width)
    down_last = add_low(down_mid[0], swap(down_mid[1], "tp", 2))
    if parts == 1:
        halves[0], high_rows, up_last, down_last = lax.optimization_barrier(
            (halves[0], high_rows, up_last, down_last)
        )
        slots = [project_back(halves[0]), high_rows]
    else:
        slots = [project_back(halves[0])]
    grad_rows = [near_sums([rows[s] for s in range(ranks)]) for rows in reversed(slots)][::-1]
    quarter = ctx_reduce(jnp.concatenate([up_last, down_last], axis=0))
    cuts = [0, w_up.shape[0], w_up.shape[0] + w_out.shape[0], w_up.shape[0] + w_out.shape[0] + w_down.shape[0]]
    halves, grad_rows = lax.optimization_barrier((halves, grad_rows))

    normed_all = normed_one.reshape(ranks, seqs, sub, width)
    grad_qkv, grad_normed, bias_sum = 0.0, [], 0.0
    for n in reversed(range(len(halves))):
        rows = halves[n].reshape(-1, 3 * HEAD_PAD)
        grad_normed.insert(0, far_sum(*grad_rows[n]))
        seen = normed_all[:, edges[n] : edges[n + 1]].reshape(-1, width)
        grad_qkv = grad_qkv + dot_tn(rows, seen)
        bias_sum = bias_sum + jnp.sum(rows.astype(F32), axis=0)
    grad_normed_one = jnp.concatenate(grad_normed, axis=0)
    grad_x = grad_hidden + norm_back(xhat_one, rstd_one, gain_one, grad_normed_one)
    grad_x = grad_x.astype(BF)
    ln1_sums = jnp.stack([jnp.sum(grad_normed_one * xhat_one, axis=0), jnp.sum(grad_normed_one, axis=0)])
    grad_x, ln1_sums, quarter = lax.optimization_barrier((grad_x, ln1_sums, quarter))
    grad_blocks = from_sequence(grad_x.reshape(seqs, sub, width))
    total = ctx_spread(quarter, cuts[3])
    sum_up, sum_out, sum_down = (total[cuts[n] : cuts[n + 1]] for n in range(3))

    grad_qkv = grad_qkv.reshape(3, HEAD_PAD, width)[:, :head_width].astype(BF)
    qkv_shard = scatter_fsdp(grad_qkv.reshape(3, fsdp, -1, width).transpose(1, 0, 2, 3))
    qkv_rows = qkv_shard.reshape(-1, width)
    sum_qkv = ctx_spread(ctx_reduce(qkv_rows), qkv_rows.shape[0]).reshape(w_qkv.shape)

    bias_sum = bias_sum.reshape(3, HEAD_PAD)[:, :head_width].reshape(3, heads, 64)
    bias_rows = jnp.concatenate([bias_sum[0], bias_sum[2]], axis=1)
    bias_all = lax.dynamic_update_slice(
        jnp.zeros((ranks * heads, 128), F32), bias_rows, (tp_rank * heads, 0)
    )
    up_bias_all = jnp.zeros((ranks, width), F32)
    for s in range(ranks):
        up_bias_all = lax.dynamic_update_slice(up_bias_all, sums[4 + s : 5 + s], (tp_rank ^ s, 0))
    late = jnp.concatenate(
        [sums[:4].reshape(-1, LANES), up_bias_all.reshape(-1, LANES), ln1_sums.reshape(-1, LANES), bias_all]
    )
    late, grad_blocks = lax.optimization_barrier((late, grad_blocks))
    for axis in ("tp", "ctx", "fsdp"):
        late = butterfly(late, axis)
    late_rows = late[: 10 * width // LANES].reshape(10, fsdp, shard)

    def mine_bias(rows, like):
        rows = lax.dynamic_slice_in_dim(rows, tp_rank * like.shape[0], like.shape[0], 0)
        return lax.dynamic_slice_in_dim(rows, fsdp_rank * like.shape[1], like.shape[1], 1)

    vector_sums = pick(late_rows, fsdp_rank, 1)
    sum_qv_bias = mine_bias(late[10 * width // LANES :], b_qv)
    up_bias_rows = late[4 * width // LANES : 8 * width // LANES]
    sum_up_bias = mine_bias(up_bias_rows.reshape(ranks * b_up.shape[0], -1), b_up)
    return (
        out_blocks, grad_blocks, vector_sums[8], vector_sums[9], sum_qkv, sum_qv_bias, sum_out, vector_sums[2],
        vector_sums[0], vector_sums[1], sum_up, sum_up_bias, sum_down, vector_sums[3],
    )


def solution(mesh):
    rows = P("fsdp", ("ctx", "tp"), None)
    vector = P("fsdp")
    out_rows = P(("tp", "fsdp"), None)
    qkv_rows = P(None, ("tp", "fsdp"), None)
    bias = P("tp", "fsdp")
    weights = (
        vector, vector, qkv_rows, bias, out_rows, vector, vector, vector, P("fsdp", "tp"), bias, out_rows, vector,
    )
    return jax.shard_map(
        on_device,
        mesh=mesh,
        in_specs=(rows, P("fsdp", None)) + weights + (rows,),
        out_specs=(rows, rows) + weights,
        check_vma=False,
    )
```

```python
import functools

import jax
import jax.numpy as jnp
from jax import lax
from jax.experimental import pallas as pl
from jax.experimental.pallas import tpu as pltpu
from jax.sharding import PartitionSpec as P

EPS = 1e-05
NEG = -1e30
BF = jnp.bfloat16
F32 = jnp.float32
LANES = 128
HEAD_PAD = 256
BQ = 512
BK = 512
VMEM_BYTES = 48 * 1024 * 1024


def dot_nn(left, right):
    return lax.dot_general(left, right, (((1,), (0,)), ((), ())), preferred_element_type=F32)


def dot_nt(left, right):
    return lax.dot_general(left, right, (((1,), (1,)), ((), ())), preferred_element_type=F32)


def dot_tn(left, right):
    return lax.dot_general(left, right, (((0,), (0,)), ((), ())), preferred_element_type=F32)


def swap(value, axis, bit):
    size = lax.axis_size(axis)
    return lax.ppermute(value, axis, [(i, i ^ bit) for i in range(size)])


def tree_sum(items):
    items = [item.astype(F32) for item in items]
    while len(items) > 1:
        items = [items[i] + items[i + 1] for i in range(0, len(items), 2)]
    return items[0]


def butterfly(value, axis):
    size = lax.axis_size(axis)
    if size & (size - 1):
        return lax.psum(value, axis)
    return tree_sum([value] + [swap(value, axis, bit) for bit in range(1, size)])


def gather_fsdp(values, axis):
    if lax.axis_size("fsdp") != 2:
        return [lax.all_gather(value, "fsdp", axis=axis, tiled=True) for value in values]
    whole = values[0] if len(values) == 1 else jnp.concatenate(values, axis=axis)
    other = swap(whole, "fsdp", 1)
    first = lax.axis_index("fsdp") == 0
    out, start = [], 0
    for value in values:
        size = value.shape[axis]
        theirs = lax.slice_in_dim(other, start, start + size, axis=axis)
        start += size
        pair = [jnp.where(first, value, theirs), jnp.where(first, theirs, value)]
        out.append(jnp.concatenate(pair, axis=axis))
    return out


def scatter_fsdp(value):
    if lax.axis_size("fsdp") != 2:
        return lax.psum_scatter(value, "fsdp", scatter_dimension=0, tiled=False)
    rank = lax.axis_index("fsdp")
    mine = lax.dynamic_index_in_dim(value, rank, 0, keepdims=False)
    theirs = lax.dynamic_index_in_dim(value, 1 - rank, 0, keepdims=False)
    return (mine.astype(F32) + swap(theirs, "fsdp", 1).astype(F32)).astype(value.dtype)


def scatter_pair(value, split):
    size = lax.axis_size("fsdp")
    pieces = [part.reshape((size, -1) + part.shape[1:]) for part in (value[:split], value[split:])]
    if size != 2:
        return jnp.concatenate([scatter_fsdp(piece) for piece in pieces], axis=0)
    rank = lax.axis_index("fsdp")

    def cut(index):
        both = [lax.dynamic_index_in_dim(piece, index, 0, keepdims=False) for piece in pieces]
        return jnp.concatenate(both, axis=0)

    return (cut(rank).astype(F32) + swap(cut(1 - rank), "fsdp", 1).astype(F32)).astype(value.dtype)


def ctx_plan(rows):
    size = lax.axis_size("ctx")
    return size == 4 and rows % (8 * size) == 0


def ctx_reduce(value):
    if not ctx_plan(value.shape[0]):
        return lax.psum(value, "ctx")
    rank = lax.axis_index("ctx")

    def halve(array, axis, bit, side):
        mine = lax.dynamic_index_in_dim(array, side, axis, keepdims=False)
        theirs = lax.dynamic_index_in_dim(array, 1 - side, axis, keepdims=False)
        return (mine.astype(F32) + swap(theirs, "ctx", bit).astype(F32)).astype(value.dtype)

    parts = value.reshape((2, 2, value.shape[0] // 4) + value.shape[1:])
    return halve(halve(parts, 1, 1, rank % 2), 0, 2, rank // 2)


def ctx_double(array, axis, bit, side):
    other = swap(array, "ctx", bit)
    first = side == 0
    return jnp.stack([jnp.where(first, array, other), jnp.where(first, other, array)], axis=axis)


def ctx_spread_far(total, rows):
    if not ctx_plan(rows):
        return total
    return ctx_double(total, 0, 2, lax.axis_index("ctx") // 2)


def ctx_spread(total, rows):
    if not ctx_plan(rows):
        return total.astype(F32)
    total = ctx_double(total, 1, 1, lax.axis_index("ctx") % 2)
    return total.reshape((rows,) + total.shape[3:]).astype(F32)


def gather_tp(value):
    far = swap(value, "tp", 2)
    return [value, swap(value, "tp", 1), far, swap(far, "tp", 1)]


def add_low(left, right):
    return (left.astype(F32) + right.astype(F32)).astype(BF)


def near_sums(slots):
    return [add_low(slots[n], swap(slots[n + 1], "tp", 1)) for n in (0, 2)]


def far_sum(near, far):
    return near.astype(F32) + swap(far, "tp", 2).astype(F32)


def seq_steps(seqs):
    size = lax.axis_size("ctx")
    groups = size // seqs
    return [
        [(src, ((src % seqs + step) % seqs) * groups + src // seqs) for src in range(size)]
        for step in range(seqs)
    ]


def send(value, pairs):
    if all(src == dst for src, dst in pairs):
        return value
    return lax.ppermute(value, "ctx", pairs)


def to_sequence(value):
    seqs = value.shape[0]
    size = lax.axis_size("ctx")
    base = lax.axis_index("ctx") % seqs
    owner = lax.axis_index("ctx") // (size // seqs)
    out = jnp.zeros_like(value)
    for step, pairs in enumerate(seq_steps(seqs)):
        block = lax.dynamic_index_in_dim(value, (base + step) % seqs, 0, keepdims=True)
        place = (owner - step + seqs) % seqs
        out = lax.dynamic_update_slice_in_dim(out, send(block, pairs), place, 0)
    return out


def from_sequence(value):
    seqs = value.shape[0]
    size = lax.axis_size("ctx")
    base = lax.axis_index("ctx") % seqs
    owner = lax.axis_index("ctx") // (size // seqs)
    out = jnp.zeros_like(value)
    for step, pairs in enumerate(seq_steps(seqs)):
        block = lax.dynamic_index_in_dim(value, (owner - step + seqs) % seqs, 0, keepdims=True)
        block = send(block, [(dst, src) for src, dst in pairs])
        out = lax.dynamic_update_slice_in_dim(out, block, (base + step) % seqs, 0)
    return out


def lane_is_low(rows):
    return lax.broadcasted_iota(jnp.int32, (rows, LANES), 1) < LANES // 2


def pieces(dims):
    ranks, steps = dims
    return [(j * ranks + rank, j, rank) for j in range(steps) for rank in range(ranks)]


def allowed_block(seg_row, seg_col, q_axis, q_start, k_start, shape):
    q_at = q_start + lax.broadcasted_iota(jnp.int32, shape, q_axis)
    k_at = k_start + lax.broadcasted_iota(jnp.int32, shape, 1 - q_axis)
    return (seg_row == seg_col) & (k_at <= q_at)


def split_heads(tile, target, rows, low):
    head_pair = tile[:, :LANES]
    zero = jnp.zeros_like(head_pair)
    target[rows, 0:128] = jnp.where(low, head_pair, zero)
    target[rows, 128:256] = jnp.where(low, zero, head_pair)
    target[rows, 256:384] = tile[:, LANES:]


def attend_kernel(gathered, where_ref, low_ref, full_ref, seg_q_ref, seg_k_ref, proj_ref, *refs):
    kv_ref = refs[0] if gathered else None
    o_ref, lse_ref, qs, ks, vs = refs[1:] if gathered else refs
    ranks, steps, sub, _ = proj_ref.shape
    parts = kv_ref.shape[0] if gathered else 1
    tp_rank, part = where_ref[0], where_ref[1]
    q_len = ranks * steps * sub
    scale = 64 ** (-0.5)
    low = lane_is_low(sub)
    for block, j, rank in pieces((ranks, steps)):
        slot = tp_rank ^ rank
        rows = slice(block * sub, (block + 1) * sub)
        tile = (proj_ref[slot, j, :, :HEAD_PAD].astype(F32) * scale).astype(BF)
        split_heads(tile, qs, rows, low)
        for p in range(parts):
            at = slice(p * q_len + block * sub, p * q_len + (block + 1) * sub)
            both = kv_ref[p, slot, j] if gathered else proj_ref[slot, j, :, HEAD_PAD:]
            ks[at, :] = both[:, :HEAD_PAD]
            vs[at, :] = both[:, HEAD_PAD:]

    def q_block(i, _):
        q_row = pl.multiple_of(i * BQ, BQ)
        q_first = part * q_len + q_row
        seg_q = seg_q_ref[pl.ds(q_row, BQ), :]

        def step(masked, kk, carry):
            k_row = pl.multiple_of(kk * BK, BK)
            keys = ks[pl.ds(k_row, BK), :]
            vals = vs[pl.ds(k_row, BK), :]
            if masked:
                ok = allowed_block(seg_q, seg_k_ref[:, pl.ds(k_row, BK)], 0, q_first, k_row, (BQ, BK))
            out = []
            for h in range(3):
                top, total, acc = carry[h]
                lanes = slice((h // 2) * LANES, (h // 2 + 1) * LANES)
                scores = dot_nt(qs[pl.ds(q_row, BQ), h * LANES : (h + 1) * LANES], keys[:, lanes])
                if masked:
                    scores = jnp.where(ok, scores, NEG)
                new_top = jnp.maximum(top, jnp.max(scores, axis=1, keepdims=True))
                probs = jnp.exp(scores - new_top)
                shrink = jnp.exp(top - new_top)
                total = total * shrink + jnp.sum(probs, axis=1, keepdims=True)
                acc = acc * shrink + dot_nn(probs.astype(BF), vals[:, lanes])
                out.append((new_top, total, acc))
            return tuple(out)

        start = tuple(
            (jnp.full((BQ, 1), NEG, F32), jnp.zeros((BQ, 1), F32), jnp.zeros((BQ, LANES), F32))
            for _ in range(3)
        )
        first, full = low_ref[i], full_ref[i]
        last = q_first // BK
        carry = lax.fori_loop(first, full, functools.partial(step, True), start)
        carry = lax.fori_loop(full, last, functools.partial(step, False), carry)
        carry = lax.fori_loop(last, last + BQ // BK, functools.partial(step, True), carry)
        heads = [acc / total for _, total, acc in carry]
        pair = jnp.where(lane_is_low(BQ), heads[0], heads[1]).astype(BF)
        third = heads[2].astype(BF)
        for n in range(BQ // sub):
            block = i * (BQ // sub) + n
            slot, j = tp_rank ^ lax.rem(block, ranks), block // ranks
            o_ref[slot, j, :, 0:128] = pair[n * sub : (n + 1) * sub]
            o_ref[slot, j, :, 128:256] = third[n * sub : (n + 1) * sub]
        for h in range(3):
            top, total, _ = carry[h]
            column = jnp.broadcast_to(top + jnp.log(total), (BQ, LANES))
            lse_ref[i, h] = column.T[0:8]
        return 0

    lax.fori_loop(0, q_len // BQ, q_block, 0)


def attend_back_kernel(
    gathered, q_range, k_range, k_done, more, where_ref, full_ref, high_ref, seg_q_ref, seg_k_ref, o_ref, do_ref, lse_ref, proj_ref, *refs
):
    refs = list(refs)
    kv_ref = refs.pop(0) if gathered else None
    sum_ref = refs.pop(0) if more else None
    dproj_ref = refs.pop(0)
    dkv_ref = refs.pop(0) if gathered else None
    rest_ref = refs.pop(0) if k_done > k_range[0] else None
    qs, ks, vs, kt, dos, dqs, delta = refs
    ranks, steps, sub, _ = proj_ref.shape
    parts = kv_ref.shape[0] if gathered else 1
    tp_rank, part = where_ref[0], where_ref[1]
    q_len = ranks * steps * sub
    scale = 64 ** (-0.5)
    low = lane_is_low(sub)
    q_first, q_end = q_range
    per_q = BQ // sub

    for block, j, rank in pieces((ranks, steps)):
        slot = tp_rank ^ rank
        rows = slice(block * sub, (block + 1) * sub)
        if q_first * per_q <= block < q_end * per_q:
            split_heads((proj_ref[slot, j, :, :HEAD_PAD].astype(F32) * scale).astype(BF), qs, rows, low)
            grad = do_ref[slot, j]
            split_heads(grad, dos, rows, low)
            product = grad.astype(F32) * o_ref[slot, j].astype(F32)
            pair, third = product[:, :LANES].T, product[:, LANES:].T
            lanes = slice(rows.start % BQ, rows.start % BQ + sub)
            for h, part_of in enumerate((pair[:64], pair[64:], third[:64])):
                delta[block // per_q, h : h + 1, lanes] = jnp.sum(part_of, axis=0, keepdims=True)
        for p in range(parts):
            if not k_range[0] * BK <= p * q_len + block * sub < k_range[1] * BK:
                continue
            at = slice(p * q_len + block * sub, p * q_len + (block + 1) * sub)
            both = kv_ref[p, slot, j] if gathered else proj_ref[slot, j, :, HEAD_PAD:]
            ks[at, :] = both[:, :HEAD_PAD]
            vs[at, :] = both[:, HEAD_PAD:]
            kt[at.start // BK, :, at.start % BK : at.start % BK + sub] = both[:, :HEAD_PAD].T
    dqs[...] = jnp.zeros_like(dqs)

    def k_block(kk, _):
        k_row = pl.multiple_of(kk * BK, BK)
        keys = ks[pl.ds(k_row, BK), :]
        vals = vs[pl.ds(k_row, BK), :]
        seg_k = seg_k_ref[pl.ds(k_row, BK), :]

        def step(masked, i, carry):
            q_row = pl.multiple_of(i * BQ, BQ)
            at = pl.ds(q_row, BQ)
            if masked:
                ok = allowed_block(seg_q_ref[i], seg_k, 1, part * q_len + q_row, k_row, (BK, BQ))
            dk, dv = list(carry[0]), list(carry[1])
            for h in range(3):
                t = h // 2
                lanes = slice(t * LANES, (t + 1) * LANES)
                mine = slice(h * LANES, (h + 1) * LANES)
                q_head, do_head = qs[at, mine], dos[at, mine]
                scores = dot_nt(keys[:, lanes], q_head)
                probs = jnp.exp(scores - lse_ref[i, h, 0:1, :])
                if masked:
                    probs = jnp.where(ok, probs, 0.0)
                grad_probs = dot_nt(vals[:, lanes], do_head)
                grad_scores = (probs * (grad_probs - delta[i, h : h + 1, :])).astype(BF)
                dv[t] = dv[t] + dot_nn(probs.astype(BF), do_head)
                dk[t] = dk[t] + dot_nn(grad_scores, q_head)
                rows = slice(h * 64, (h + 1) * 64)
                dqs[i, rows, :] += dot_nn(kt[kk, rows, :], grad_scores)
            return tuple(dk), tuple(dv)

        zero = jnp.zeros((BK, LANES), F32)
        carry = ((zero, zero), (zero, zero))
        if more:
            pieces_in = [sum_ref[pl.ds(k_row, BK), t * LANES : (t + 1) * LANES] for t in range(4)]
            carry = (tuple(pieces_in[:2]), tuple(pieces_in[2:]))
        ahead = kk - part * (q_len // BQ)
        inside = lambda value: jnp.clip(value, q_first, q_end)
        first = inside(ahead)
        diagonal = jnp.where(ahead >= 0, inside(ahead + 1), first)
        full = jnp.maximum(inside(full_ref[kk]), diagonal)
        high = jnp.maximum(inside(high_ref[kk]), full)
        carry = lax.fori_loop(first, diagonal, functools.partial(step, True), carry)
        carry = lax.fori_loop(diagonal, full, functools.partial(step, False), carry)
        carry = lax.fori_loop(full, high, functools.partial(step, True), carry)
        return carry[0] + carry[1]

    def finish(kk, _):
        sums = k_block(kk, 0)
        for n in range(BK // sub):
            block = lax.rem(kk, q_len // BK) * (BK // sub) + n
            slot, j = tp_rank ^ lax.rem(block, ranks), block // ranks
            for t in range(4):
                piece = sums[t][n * sub : (n + 1) * sub].astype(BF)
                lanes = slice(t * LANES, (t + 1) * LANES)
                if gathered:
                    dkv_ref[kk // (q_len // BK), slot, j, :, lanes] = piece
                else:
                    start = HEAD_PAD + t * LANES
                    dproj_ref[slot, j - k_done * BK // (ranks * sub), :, start : start + LANES] = piece
        return 0

    def keep(kk, _):
        sums = k_block(kk, 0)
        for t in range(4):
            rest_ref[pl.ds(pl.multiple_of(kk * BK, BK), BK), t * LANES : (t + 1) * LANES] = sums[t]
        return 0

    if rest_ref is not None:
        lax.fori_loop(k_range[0], k_done, keep, 0)
    lax.fori_loop(k_done, k_range[1], finish, 0)
    for block, j, rank in pieces((ranks, steps)):
        if q_first * per_q <= block < q_end * per_q:
            lanes = slice(block % per_q * sub, (block % per_q + 1) * sub)
            grad = (dqs[block // per_q, :, lanes] * scale).T.astype(BF)
            dproj_ref[tp_rank ^ rank, j - q_first * per_q // ranks, :, :HEAD_PAD] = grad


SMEM = pl.BlockSpec(memory_space=pltpu.SMEM)
VMEM = pl.BlockSpec(memory_space=pltpu.VMEM)
PARAMS = pltpu.CompilerParams(vmem_limit_bytes=VMEM_BYTES)


def attend(where, seg_q, seg_k, proj, keyvals):
    ranks, steps, sub, _ = proj.shape
    gathered = keyvals is not None
    q_len = ranks * steps * sub
    k_len = q_len * (keyvals.shape[0] if gathered else 1)
    q_first, q_last = seg_q[::BQ], seg_q[BQ - 1 :: BQ]
    k_first, k_last = seg_k[::BK], seg_k[BK - 1 :: BK]
    k_index = jnp.arange(k_len // BK)
    bound = where[1] * (q_len // BK) + jnp.arange(q_len // BQ) * (BQ // BK)
    before = k_index[None, :] < bound[:, None]
    first = jnp.sum(before & (k_last[None, :] < q_first[:, None]), axis=1).astype(jnp.int32)
    full = jnp.sum(before & (k_first[None, :] != q_last[:, None]), axis=1).astype(jnp.int32)
    inputs = (proj, keyvals) if gathered else (proj,)
    return pl.pallas_call(
        functools.partial(attend_kernel, gathered),
        out_shape=(
            jax.ShapeDtypeStruct((ranks, steps, sub, HEAD_PAD), BF),
            jax.ShapeDtypeStruct((q_len // BQ, 3, 8, BQ), F32),
        ),
        in_specs=[SMEM] * 3 + [VMEM] * (2 + len(inputs)),
        out_specs=(VMEM, VMEM),
        scratch_shapes=[
            pltpu.VMEM((q_len, 3 * LANES), BF),
            pltpu.VMEM((k_len, HEAD_PAD), BF),
            pltpu.VMEM((k_len, HEAD_PAD), BF),
        ],
        compiler_params=PARAMS,
        cost_estimate=pl.CostEstimate(
            flops=16 * q_len * k_len * 256, bytes_accessed=8 * q_len * 1024, transcendentals=3 * q_len * k_len // 2
        ),
        name="attend",
    )(where, first, jnp.maximum(full, first), seg_q[:, None], seg_k[None, :], *inputs)


def attend_back(where, seg_q, seg_k, proj, keyvals, attended, grad, lse, q_range, k_range, k_done, before=None):
    ranks, steps, sub, _ = proj.shape
    gathered = keyvals is not None
    q_len = ranks * steps * sub
    k_len = q_len * (keyvals.shape[0] if gathered else 1)
    q_first, q_last = seg_q[::BQ], seg_q[BQ - 1 :: BQ]
    k_first, k_last = seg_k[::BK], seg_k[BK - 1 :: BK]
    full = jnp.sum(q_last[None, :] <= k_first[:, None], axis=1).astype(jnp.int32)
    high = jnp.sum(q_first[None, :] <= k_last[:, None], axis=1).astype(jnp.int32)
    inputs = [attended, grad, lse, proj] + ([keyvals] if gathered else []) + ([before] if before is not None else [])
    part_steps = (q_range[1] - q_range[0]) * BQ // (ranks * sub)
    outs = [jax.ShapeDtypeStruct((ranks, part_steps, sub, proj.shape[3] if not gathered else HEAD_PAD), BF)]
    if gathered:
        outs.append(jax.ShapeDtypeStruct(keyvals.shape, BF))
    if k_done > k_range[0]:
        outs.append(jax.ShapeDtypeStruct((k_done * BK, 2 * HEAD_PAD), F32))
    return pl.pallas_call(
        functools.partial(attend_back_kernel, gathered, q_range, k_range, k_done, before is not None),
        out_shape=outs,
        in_specs=[SMEM] * 3 + [VMEM] * (2 + len(inputs)),
        out_specs=[VMEM] * len(outs),
        scratch_shapes=[
            pltpu.VMEM((q_len, 3 * LANES), BF),
            pltpu.VMEM((k_len, HEAD_PAD), BF),
            pltpu.VMEM((k_len, HEAD_PAD), BF),
            pltpu.VMEM((k_len // BK, HEAD_PAD, BK), BF),
            pltpu.VMEM((q_len, 3 * LANES), BF),
            pltpu.VMEM((q_len // BQ, HEAD_PAD, BQ), F32),
            pltpu.VMEM((q_len // BQ, 8, BQ), F32),
        ],
        compiler_params=PARAMS,
        cost_estimate=pl.CostEstimate(
            flops=12 * q_len * k_len * 256, bytes_accessed=16 * q_len * 1024, transcendentals=3 * q_len * k_len // 2
        ),
        name=f"attend_back_{q_range[0]}_{q_range[1]}",
    )(where, full, high, seg_q.reshape(-1, 1, BQ), seg_k[:, None], *inputs)


GELU_A, GELU_B = 0.7978845608028654, 0.044715
ORDER = (0, 2, 1, 3)


def row_mean(values):
    return jnp.mean(values, axis=-1, keepdims=True)


def middle_kernel(
    head_width, x_ref, m0, m1, m2, m3, cot_ref, vec_ref, up0, up1, up2, up3, down_even, down_odd,
    out_ref, gh_ref, do_ref, up_even_ref, up_odd_ref, down_even_ref, down_odd_ref, wout_even_ref, wout_odd_ref, small_ref,
    wu, wd, xhat, rstd, n2, act, gpre, mlp, dn2,
):
    at = pl.program_id(0)
    tokens, width = x_ref.shape
    units = wd.shape[0]
    chunk, wide = tokens, 256
    merged = (m0, m1, m2, m3)
    ups = (up0, up1, up2, up3)
    downs = ((down_even, 0), (down_odd, 0), (down_even, 1), (down_odd, 1))
    bias_row = up0.shape[0] - 16

    @pl.when(at == 0)
    def _():
        gain, shift = vec_ref[0:1, :], vec_ref[1:2, :]
        for t in range(tokens // chunk):
            rows = slice(t * chunk, (t + 1) * chunk)
            hidden = x_ref[rows, :].astype(F32) + vec_ref[2:3, :]
            for s in range(4):
                hidden = hidden + dot_nn(merged[s][rows, :head_width], ups[s][units : units + head_width, :])
            center = hidden - row_mean(hidden)
            scale = lax.rsqrt(row_mean(center * center) + EPS)
            norm = center * scale
            xhat[rows, :] = norm
            rstd[rows, :] = jnp.broadcast_to(scale, (chunk, LANES))
            n2[rows, :] = (norm * gain + shift).astype(BF)
            mlp[rows, :] = hidden + vec_ref[3:4, :]
        dn2[...] = jnp.zeros_like(dn2)
        small_ref[...] = jnp.zeros_like(small_ref)

    for n, s in enumerate(ORDER):

        @pl.when(at == n)
        def _():
            wu[...] = ups[s][...]
            wd[...] = downs[s][0][downs[s][1]]

    slot = (at % 2) * 2 + at // 2
    bias = wu[bias_row : bias_row + 16, :][0:1].astype(F32)

    def tokens_step(t, total):
        rows = pl.ds(pl.multiple_of(t * chunk, chunk), chunk)
        pre = dot_nn(n2[rows, :], wu[:units, :]) + bias
        square = pre * pre
        tanh = jnp.tanh(GELU_A * pre * (1.0 + GELU_B * square))
        half = 0.5 * (1.0 + tanh)
        activ = (pre * half).astype(BF)
        act[rows, :] = activ
        mlp[rows, :] += dot_nn(activ, wd[...])
        slope = half + (0.5 * GELU_A) * pre * (1.0 - tanh * tanh) * (1.0 + (3.0 * GELU_B) * square)
        grad = (dot_nt(cot_ref[rows, :], wd[...]) * slope).astype(BF)
        gpre[rows, :] = grad
        dn2[rows, :] += dot_nt(grad, wu[:units, :])
        return total + jnp.sum(grad.astype(F32), axis=0, keepdims=True)

    total = lax.fori_loop(0, tokens // chunk, tokens_step, jnp.zeros((1, units), F32))
    for s in range(4):

        @pl.when(slot == s)
        def _():
            small_ref[4 + s : 5 + s, :] = total

    def weight_grads(up_out, down_out):
        for c in range(units // wide):
            rows = slice(c * wide, (c + 1) * wide)
            down_out[0, rows, :] = dot_tn(act[:, rows], cot_ref[...]).astype(BF)
        for c in range(width // wide):
            rows = slice(c * wide, (c + 1) * wide)
            up_out[0, rows, :] = dot_tn(n2[:, rows], gpre[...]).astype(BF)

    @pl.when(at < 2)
    def _():
        weight_grads(up_even_ref, down_even_ref)

    @pl.when(at >= 2)
    def _():
        weight_grads(up_odd_ref, down_odd_ref)

    @pl.when(at == 3)
    def _():
        gain = vec_ref[0:1, :]
        for t in range(tokens // chunk):
            rows = slice(t * chunk, (t + 1) * chunk)
            out_ref[rows, :] = mlp[rows, :].astype(BF)
            grad, norm, cot = dn2[rows, :], xhat[rows, :], cot_ref[rows, :].astype(F32)
            gg = grad * gain
            inner = gg - row_mean(gg) - norm * row_mean(gg * norm)
            hidden = cot + rstd[rows, 0:1] * inner
            gh_ref[rows, :] = hidden
            small_ref[0:1, :] += jnp.sum(grad * norm, axis=0, keepdims=True)
            small_ref[1:2, :] += jnp.sum(grad, axis=0, keepdims=True)
            small_ref[2:3, :] += jnp.sum(hidden, axis=0, keepdims=True)
            small_ref[3:4, :] += jnp.sum(cot, axis=0, keepdims=True)
            branch = hidden.astype(BF)
            gpre[rows, :width] = branch
            for s in range(4):
                back = dot_nt(branch, ups[s][units : units + head_width, :]).astype(BF)
                do_ref[s, rows, :head_width] = back
                do_ref[s, rows, head_width:] = jnp.zeros((chunk, HEAD_PAD - head_width), BF)
        for s in range(4):
            target = (wout_even_ref, wout_odd_ref)[s % 2]
            target[s // 2] = dot_tn(merged[s][...], gpre[:, :width])[:head_width].astype(BF)


def middle(head_width, x_rows, merged, cot_rows, vectors, ups, down_even, down_odd):
    tokens, width = x_rows.shape
    units = down_even.shape[1]
    whole = lambda shape: pl.BlockSpec(shape, lambda at: (0,) * len(shape))
    early = lambda at: (jnp.minimum(at, 1), 0, 0)
    late = lambda at: (jnp.maximum(at - 2, 0), 0, 0)
    once = lambda value: pl.BlockSpec(value.shape, lambda at: (0,) * value.ndim, pipeline_mode=pl.Buffered(1))
    struct = jax.ShapeDtypeStruct
    return pl.pallas_call(
        functools.partial(middle_kernel, head_width),
        grid=(4,),
        out_shape=(
            struct((tokens, width), BF),
            struct((tokens, width), F32),
            struct((4, tokens, HEAD_PAD), BF),
            struct((2, width, units), BF),
            struct((2, width, units), BF),
            struct((2, units, width), BF),
            struct((2, units, width), BF),
            struct((2, head_width, width), BF),
            struct((2, head_width, width), BF),
            struct((8, width), F32),
        ),
        in_specs=[whole((tokens, width))]
        + [whole((tokens, HEAD_PAD))] * 4
        + [whole((tokens, width)), whole(vectors.shape)]
        + [once(value) for value in (*ups, down_even, down_odd)],
        out_specs=(
            whole((tokens, width)),
            whole((tokens, width)),
            whole((4, tokens, HEAD_PAD)),
            pl.BlockSpec((1, width, units), early),
            pl.BlockSpec((1, width, units), late),
            pl.BlockSpec((1, units, width), early),
            pl.BlockSpec((1, units, width), late),
            whole((2, head_width, width)),
            whole((2, head_width, width)),
            whole((8, width)),
        ),
        scratch_shapes=[
            pltpu.VMEM(ups[0].shape, BF),
            pltpu.VMEM((units, width), BF),
            pltpu.VMEM((tokens, width), F32),
            pltpu.VMEM((tokens, LANES), F32),
            pltpu.VMEM((tokens, width), BF),
            pltpu.VMEM((tokens, units), BF),
            pltpu.VMEM((tokens, units), BF),
            pltpu.VMEM((tokens, width), F32),
            pltpu.VMEM((tokens, width), F32),
        ],
        compiler_params=PARAMS,
        cost_estimate=pl.CostEstimate(
            flops=60 * tokens * width * units, bytes_accessed=12 * units * width, transcendentals=4 * tokens * units
        ),
        name="middle",
    )(x_rows, *merged, cot_rows, vectors, *ups, down_even, down_odd)


def norm_parts(values):
    center = values - row_mean(values)
    rstd = lax.rsqrt(row_mean(center * center) + EPS)
    return center * rstd, rstd


def norm_back(xhat, rstd, gain, grad):
    gg = grad * gain
    return rstd * (gg - row_mean(gg) - xhat * row_mean(gg * xhat))


def pick(array, index, axis):
    return lax.dynamic_index_in_dim(array, index, axis, keepdims=False)


def on_device(
    block_in, segments, ln1_gain, ln1_shift, w_qkv, b_qv, w_out, b_out, ln2_gain, ln2_shift, w_up, b_up, w_down, b_down, cotangent
):
    seqs, sub, width = block_in.shape
    ranks, fsdp, ctx_size = lax.axis_size("tp"), lax.axis_size("fsdp"), lax.axis_size("ctx")
    parts = ctx_size // seqs
    tp_rank, ctx_rank, fsdp_rank = lax.axis_index("tp"), lax.axis_index("ctx"), lax.axis_index("fsdp")
    heads = b_qv.shape[0]
    head_width = heads * 64
    own = seqs * sub
    tokens = ranks * own
    shard = ln1_gain.shape[0]

    x_blocks = to_sequence(block_in)
    down_far = swap(w_down, "tp", 2)
    x_blocks, down_far = lax.optimization_barrier((x_blocks, down_far))
    x_own = x_blocks.reshape(own, width)

    vectors = [ln1_gain, ln1_shift, b_out, ln2_gain, ln2_shift, b_down, b_qv.reshape(-1), b_up.reshape(-1)]
    rows = jnp.stack([jnp.pad(v, (0, shard - v.shape[0])) for v in vectors])
    (small,) = gather_fsdp([rows[None]], 0)
    (qkv_mat,) = gather_fsdp([w_qkv], 1)
    gain_one, shift_one, out_bias, gain_two, shift_two, down_bias = (
        small[:, n].reshape(-1).astype(F32) for n in range(6)
    )
    qv_bias = small[:, 6, : b_qv.size].reshape((fsdp,) + b_qv.shape)
    qv_bias = qv_bias.transpose(1, 0, 2).reshape(heads, -1).astype(F32)
    up_bias = small[:, 7, : b_up.size].reshape((fsdp,) + b_up.shape).transpose(1, 0, 2).reshape(1, -1)
    extra = HEAD_PAD - head_width
    qkv_pad = jnp.pad(qkv_mat, ((0, 0), (0, extra), (0, 0))).reshape(3 * HEAD_PAD, width)
    bias_rows = jnp.stack(
        [qv_bias[:, :64].reshape(-1), jnp.zeros((head_width,), F32), qv_bias[:, 64:].reshape(-1)]
    )
    qkv_bias = jnp.pad(bias_rows, ((0, 0), (0, extra))).reshape(-1)

    up_rows, out_rows = gather_fsdp([w_up, w_out], 0)
    up_own = jnp.concatenate([up_rows, out_rows, jnp.pad(up_bias, ((0, 15), (0, 0)))], axis=0)
    down_pair = jnp.stack([w_down, down_far])

    x_float = x_own.astype(F32)
    xhat_one, rstd_one = norm_parts(x_float)
    normed_own = (xhat_one * gain_one + shift_one).astype(BF)
    normed_own, cotangent = lax.optimization_barrier((normed_own, cotangent))
    cot_rows = to_sequence(cotangent)
    normed_one = jnp.concatenate(gather_tp(normed_own), axis=0)
    normed_one, up_own, down_pair, cot_rows = lax.optimization_barrier(
        (normed_one, up_own, down_pair, cot_rows)
    )
    cot_rows = cot_rows.reshape(own, width)
    proj = (dot_nt(normed_one, qkv_pad) + qkv_bias).astype(BF).reshape(ranks, seqs, sub, 3 * HEAD_PAD)
    up_side = swap(up_own, "tp", 1)
    keyvals = None
    groups = [[g * parts + p for p in range(parts)] for g in range(ctx_size // parts)]
    if parts > 1:
        keyvals = lax.all_gather(
            proj[None, ..., HEAD_PAD:], "ctx", axis=0, tiled=True, axis_index_groups=groups
        )
    seq_rank, part = ctx_rank // parts, ctx_rank % parts
    where = jnp.stack([tp_rank, part]).astype(jnp.int32)
    seg_k = pick(segments, seq_rank, 0)
    seg_q = lax.dynamic_slice_in_dim(seg_k, part * tokens, tokens, 0)
    attended, lse = attend(where, seg_q, seg_k, proj, keyvals)

    up_far = swap(up_own, "tp", 2)
    (down_even,) = gather_fsdp([down_pair], 1)
    attended, up_far, up_side, down_even = lax.optimization_barrier(
        (attended, up_far, up_side, down_even)
    )
    ups = [up_own, up_side, up_far, swap(up_far, "tp", 1)]
    down_odd = swap(down_even, "tp", 1)

    slots = attended.reshape(ranks, own, HEAD_PAD)
    merged = [slots[0]] + [swap(slots[s], "tp", s) for s in range(1, ranks)]
    vecs = jnp.stack([gain_two, shift_two, out_bias, down_bias])
    vecs = jnp.pad(vecs, ((0, 4), (0, 0)))
    (
        block_out, grad_hidden, grad_slots, up_even, up_odd, down_even_g, down_odd_g, out_even, out_odd, sums,
    ) = middle(head_width, x_own, merged, cot_rows, vecs, ups, down_even, down_odd)

    up_got, out_got = swap(up_odd, "tp", 1), swap(out_odd, "tp", 1)
    up_near = [
        jnp.concatenate([add_low(up_even[n], up_got[n]), add_low(out_even[n], out_got[n])])
        for n in range(2)
    ]
    down_near = add_low(down_even_g, swap(down_odd_g, "tp", 1))
    grad_slots = [grad_slots[s] for s in range(ranks)]
    grad_slots[1], up_near, down_near = lax.optimization_barrier((grad_slots[1], up_near, down_near))
    grad_slots = [grad_slots[0]] + [swap(grad_slots[s], "tp", s) for s in range(1, ranks)]
    grad_attended = jnp.stack(grad_slots).reshape(ranks, seqs, sub, HEAD_PAD)
    grad_attended, up_near, down_near, block_out = lax.optimization_barrier(
        (grad_attended, up_near, down_near, block_out)
    )
    out_blocks = from_sequence(block_out.reshape(seqs, sub, width))

    up_mid = add_low(up_near[0], swap(up_near[1], "tp", 2))
    down_mid = scatter_fsdp(down_near.reshape(2, fsdp, -1, width).transpose(1, 0, 2, 3))

    def project_back(half):
        return dot_nn(half.reshape(-1, 3 * HEAD_PAD), qkv_pad).astype(BF).reshape(ranks, -1, width)

    q_blocks = tokens // BQ
    back = functools.partial(attend_back, where, seg_q, seg_k, proj, keyvals, attended)
    if parts > 1:
        dq, dkv = back(grad_attended, lse, (0, q_blocks), (0, parts * q_blocks), 0)
        dkv = lax.psum_scatter(
            dkv, "ctx", scatter_dimension=0, tiled=True, axis_index_groups=groups
        )
        halves = [jnp.concatenate([dq, dkv.reshape(ranks, seqs, sub, 2 * HEAD_PAD)], axis=-1)]
        edges = [0, seqs]
    else:
        mid = q_blocks // 2
        high, rest = back(grad_attended, lse, (mid, q_blocks), (0, q_blocks), mid)
        rest, high, up_mid, down_mid, out_blocks = lax.optimization_barrier(
            (rest, high, up_mid, down_mid, out_blocks)
        )
        high_rows = project_back(high)
        rest, high_rows = lax.optimization_barrier((rest, high_rows))
        (low,) = back(grad_attended, lse, (0, mid), (0, mid), 0, rest)
        halves = [low, high]
        edges = [0, mid * BQ // (ranks * sub), seqs]

    up_last = scatter_pair(up_mid, width)
    down_last = add_low(down_mid[0], swap(down_mid[1], "tp", 2))
    if parts == 1:
        halves[0], high_rows, up_last, down_last = lax.optimization_barrier(
            (halves[0], high_rows, up_last, down_last)
        )
        slots = [project_back(halves[0]), high_rows]
    else:
        slots = [project_back(halves[0])]
    grad_rows = [near_sums([rows[s] for s in range(ranks)]) for rows in reversed(slots)][::-1]
    quarter = ctx_reduce(jnp.concatenate([up_last, down_last], axis=0))
    cuts = [0, w_up.shape[0], w_up.shape[0] + w_out.shape[0], w_up.shape[0] + w_out.shape[0] + w_down.shape[0]]
    halves, grad_rows = lax.optimization_barrier((halves, grad_rows))

    normed_all = normed_one.reshape(ranks, seqs, sub, width)
    grad_qkv, grad_normed, bias_sum = 0.0, [], 0.0
    for n in reversed(range(len(halves))):
        rows = halves[n].reshape(-1, 3 * HEAD_PAD)
        grad_normed.insert(0, far_sum(*grad_rows[n]))
        seen = normed_all[:, edges[n] : edges[n + 1]].reshape(-1, width)
        grad_qkv = grad_qkv + dot_tn(rows, seen)
        bias_sum = bias_sum + jnp.sum(rows.astype(F32), axis=0)
    grad_normed_one = jnp.concatenate(grad_normed, axis=0)
    grad_x = grad_hidden + norm_back(xhat_one, rstd_one, gain_one, grad_normed_one)
    grad_x = grad_x.astype(BF)
    ln1_sums = jnp.stack([jnp.sum(grad_normed_one * xhat_one, axis=0), jnp.sum(grad_normed_one, axis=0)])
    grad_qkv = grad_qkv.reshape(3, HEAD_PAD, width)[:, :head_width].astype(BF)
    qkv_shard = scatter_fsdp(grad_qkv.reshape(3, fsdp, -1, width).transpose(1, 0, 2, 3))
    qkv_rows, quarter = lax.optimization_barrier((qkv_shard.reshape(-1, width), quarter))
    quarter = ctx_spread_far(quarter, cuts[3])
    grad_x, quarter = lax.optimization_barrier((grad_x, quarter))
    grad_blocks = from_sequence(grad_x.reshape(seqs, sub, width))
    total = ctx_spread(quarter, cuts[3])
    sum_up, sum_out, sum_down = (total[cuts[n] : cuts[n + 1]] for n in range(3))
    sum_qkv = ctx_spread_far(ctx_reduce(qkv_rows), qkv_rows.shape[0])
    sum_qkv = ctx_spread(sum_qkv, qkv_rows.shape[0]).reshape(w_qkv.shape)

    bias_sum = bias_sum.reshape(3, HEAD_PAD)[:, :head_width].reshape(3, heads, 64)
    bias_rows = jnp.concatenate([bias_sum[0], bias_sum[2]], axis=1)
    bias_all = lax.dynamic_update_slice(
        jnp.zeros((ranks * heads, 128), F32), bias_rows, (tp_rank * heads, 0)
    )
    up_bias_all = jnp.zeros((ranks, width), F32)
    for s in range(ranks):
        up_bias_all = lax.dynamic_update_slice(up_bias_all, sums[4 + s : 5 + s], (tp_rank ^ s, 0))
    late = jnp.concatenate(
        [sums[:4].reshape(-1, LANES), up_bias_all.reshape(-1, LANES), ln1_sums.reshape(-1, LANES), bias_all]
    )
    late = butterfly(butterfly(late, "tp"), "fsdp")
    late, grad_blocks = lax.optimization_barrier((late, grad_blocks))
    late = butterfly(late, "ctx")
    late_rows = late[: 10 * width // LANES].reshape(10, fsdp, shard)

    def mine_bias(rows, like):
        rows = lax.dynamic_slice_in_dim(rows, tp_rank * like.shape[0], like.shape[0], 0)
        return lax.dynamic_slice_in_dim(rows, fsdp_rank * like.shape[1], like.shape[1], 1)

    vector_sums = pick(late_rows, fsdp_rank, 1)
    sum_qv_bias = mine_bias(late[10 * width // LANES :], b_qv)
    up_bias_rows = late[4 * width // LANES : 8 * width // LANES]
    sum_up_bias = mine_bias(up_bias_rows.reshape(ranks * b_up.shape[0], -1), b_up)
    return (
        out_blocks, grad_blocks, vector_sums[8], vector_sums[9], sum_qkv, sum_qv_bias, sum_out, vector_sums[2],
        vector_sums[0], vector_sums[1], sum_up, sum_up_bias, sum_down, vector_sums[3],
    )


def solution(mesh):
    rows = P("fsdp", ("ctx", "tp"), None)
    vector = P("fsdp")
    out_rows = P(("tp", "fsdp"), None)
    qkv_rows = P(None, ("tp", "fsdp"), None)
    bias = P("tp", "fsdp")
    weights = (
        vector, vector, qkv_rows, bias, out_rows, vector, vector, vector, P("fsdp", "tp"), bias, out_rows, vector,
    )
    return jax.shard_map(
        on_device,
        mesh=mesh,
        in_specs=(rows, P("fsdp", None)) + weights + (rows,),
        out_specs=(rows, rows) + weights,
        check_vma=False,
    )
```

```python
import functools

import jax
import jax.numpy as jnp
from jax import lax
from jax.experimental import pallas as pl
from jax.experimental.pallas import tpu as pltpu
from jax.sharding import PartitionSpec as P

EPS = 1e-05
NEG = -1e30
BF = jnp.bfloat16
F32 = jnp.float32
LANES = 128
HEAD_PAD = 256
BQ = 512
BK = 512
VMEM_BYTES = 48 * 1024 * 1024


def dot_nn(left, right):
    return lax.dot_general(left, right, (((1,), (0,)), ((), ())), preferred_element_type=F32)


def dot_nt(left, right):
    return lax.dot_general(left, right, (((1,), (1,)), ((), ())), preferred_element_type=F32)


def dot_tn(left, right):
    return lax.dot_general(left, right, (((0,), (0,)), ((), ())), preferred_element_type=F32)


def swap(value, axis, bit):
    size = lax.axis_size(axis)
    return lax.ppermute(value, axis, [(i, i ^ bit) for i in range(size)])


def tree_sum(items):
    items = [item.astype(F32) for item in items]
    while len(items) > 1:
        items = [items[i] + items[i + 1] for i in range(0, len(items), 2)]
    return items[0]


def butterfly(value, axis):
    size = lax.axis_size(axis)
    if size & (size - 1):
        return lax.psum(value, axis)
    return tree_sum([value] + [swap(value, axis, bit) for bit in range(1, size)])


def gather_fsdp(values, axis):
    if lax.axis_size("fsdp") != 2:
        return [lax.all_gather(value, "fsdp", axis=axis, tiled=True) for value in values]
    whole = values[0] if len(values) == 1 else jnp.concatenate(values, axis=axis)
    other = swap(whole, "fsdp", 1)
    first = lax.axis_index("fsdp") == 0
    out, start = [], 0
    for value in values:
        size = value.shape[axis]
        theirs = lax.slice_in_dim(other, start, start + size, axis=axis)
        start += size
        pair = [jnp.where(first, value, theirs), jnp.where(first, theirs, value)]
        out.append(jnp.concatenate(pair, axis=axis))
    return out


def scatter_fsdp(value):
    if lax.axis_size("fsdp") != 2:
        return lax.psum_scatter(value, "fsdp", scatter_dimension=0, tiled=False)
    rank = lax.axis_index("fsdp")
    mine = lax.dynamic_index_in_dim(value, rank, 0, keepdims=False)
    theirs = lax.dynamic_index_in_dim(value, 1 - rank, 0, keepdims=False)
    return (mine.astype(F32) + swap(theirs, "fsdp", 1).astype(F32)).astype(value.dtype)


def scatter_pair(value, split):
    size = lax.axis_size("fsdp")
    pieces = [part.reshape((size, -1) + part.shape[1:]) for part in (value[:split], value[split:])]
    if size != 2:
        return jnp.concatenate([scatter_fsdp(piece) for piece in pieces], axis=0)
    rank = lax.axis_index("fsdp")

    def cut(index):
        both = [lax.dynamic_index_in_dim(piece, index, 0, keepdims=False) for piece in pieces]
        return jnp.concatenate(both, axis=0)

    return (cut(rank).astype(F32) + swap(cut(1 - rank), "fsdp", 1).astype(F32)).astype(value.dtype)


def ctx_plan(rows):
    size = lax.axis_size("ctx")
    return size == 4 and rows % (8 * size) == 0


def ctx_reduce(value):
    if not ctx_plan(value.shape[0]):
        return lax.psum(value, "ctx")
    rank = lax.axis_index("ctx")

    def halve(array, axis, bit, side):
        mine = lax.dynamic_index_in_dim(array, side, axis, keepdims=False)
        theirs = lax.dynamic_index_in_dim(array, 1 - side, axis, keepdims=False)
        return (mine.astype(F32) + swap(theirs, "ctx", bit).astype(F32)).astype(value.dtype)

    parts = value.reshape((2, 2, value.shape[0] // 4) + value.shape[1:])
    return halve(halve(parts, 1, 1, rank % 2), 0, 2, rank // 2)


def ctx_double(array, axis, bit, side):
    other = swap(array, "ctx", bit)
    first = side == 0
    return jnp.stack([jnp.where(first, array, other), jnp.where(first, other, array)], axis=axis)


def ctx_spread_far(total, rows):
    if not ctx_plan(rows):
        return total
    return ctx_double(total, 0, 2, lax.axis_index("ctx") // 2)


def ctx_spread(total, rows):
    if not ctx_plan(rows):
        return total.astype(F32)
    total = ctx_double(total, 1, 1, lax.axis_index("ctx") % 2)
    return total.reshape((rows,) + total.shape[3:]).astype(F32)


def gather_tp(value):
    far = swap(value, "tp", 2)
    return [value, swap(value, "tp", 1), far, swap(far, "tp", 1)]


def add_low(left, right):
    return (left.astype(F32) + right.astype(F32)).astype(BF)


def near_sums(slots):
    return [add_low(slots[n], swap(slots[n + 1], "tp", 1)) for n in (0, 2)]


def far_sum(near, far):
    return near.astype(F32) + swap(far, "tp", 2).astype(F32)


def seq_steps(seqs):
    size = lax.axis_size("ctx")
    groups = size // seqs
    return [
        [(src, ((src % seqs + step) % seqs) * groups + src // seqs) for src in range(size)]
        for step in range(seqs)
    ]


def send(value, pairs):
    if all(src == dst for src, dst in pairs):
        return value
    return lax.ppermute(value, "ctx", pairs)


def to_sequence(value, later=()):
    seqs = value.shape[0]
    size = lax.axis_size("ctx")
    base = lax.axis_index("ctx") % seqs
    owner = lax.axis_index("ctx") // (size // seqs)
    out = jnp.zeros_like(value)
    blocks = [
        lax.dynamic_index_in_dim(value, (base + step) % seqs, 0, keepdims=True)
        for step in range(seqs)
    ]
    blocks, later = lax.optimization_barrier((blocks, later))
    for step, pairs in enumerate(seq_steps(seqs)):
        place = (owner - step + seqs) % seqs
        out = lax.dynamic_update_slice_in_dim(out, send(blocks[step], pairs), place, 0)
    return out, later


def from_sequence(value):
    seqs = value.shape[0]
    size = lax.axis_size("ctx")
    base = lax.axis_index("ctx") % seqs
    owner = lax.axis_index("ctx") // (size // seqs)
    out = jnp.zeros_like(value)
    for step, pairs in enumerate(seq_steps(seqs)):
        block = lax.dynamic_index_in_dim(value, (owner - step + seqs) % seqs, 0, keepdims=True)
        block = send(block, [(dst, src) for src, dst in pairs])
        out = lax.dynamic_update_slice_in_dim(out, block, (base + step) % seqs, 0)
    return out


def lane_is_low(rows):
    return lax.broadcasted_iota(jnp.int32, (rows, LANES), 1) < LANES // 2


def pieces(dims):
    ranks, steps = dims
    return [(j * ranks + rank, j, rank) for j in range(steps) for rank in range(ranks)]


def allowed_block(seg_row, seg_col, q_axis, q_start, k_start, shape):
    q_at = q_start + lax.broadcasted_iota(jnp.int32, shape, q_axis)
    k_at = k_start + lax.broadcasted_iota(jnp.int32, shape, 1 - q_axis)
    return (seg_row == seg_col) & (k_at <= q_at)


def split_heads(tile, target, rows, low):
    head_pair = tile[:, :LANES]
    zero = jnp.zeros_like(head_pair)
    target[rows, 0:128] = jnp.where(low, head_pair, zero)
    target[rows, 128:256] = jnp.where(low, zero, head_pair)
    target[rows, 256:384] = tile[:, LANES:]


def attend_kernel(gathered, where_ref, low_ref, full_ref, seg_q_ref, seg_k_ref, proj_ref, *refs):
    kv_ref = refs[0] if gathered else None
    o_ref, lse_ref, qs, ks, vs = refs[1:] if gathered else refs
    ranks, steps, sub, _ = proj_ref.shape
    parts = kv_ref.shape[0] if gathered else 1
    tp_rank, part = where_ref[0], where_ref[1]
    q_len = ranks * steps * sub
    scale = 64 ** (-0.5)
    low = lane_is_low(sub)
    for block, j, rank in pieces((ranks, steps)):
        slot = tp_rank ^ rank
        rows = slice(block * sub, (block + 1) * sub)
        tile = (proj_ref[slot, j, :, :HEAD_PAD].astype(F32) * scale).astype(BF)
        split_heads(tile, qs, rows, low)
        for p in range(parts):
            at = slice(p * q_len + block * sub, p * q_len + (block + 1) * sub)
            both = kv_ref[p, slot, j] if gathered else proj_ref[slot, j, :, HEAD_PAD:]
            ks[at, :] = both[:, :HEAD_PAD]
            vs[at, :] = both[:, HEAD_PAD:]

    def q_block(i, _):
        q_row = pl.multiple_of(i * BQ, BQ)
        q_first = part * q_len + q_row
        seg_q = seg_q_ref[pl.ds(q_row, BQ), :]

        def step(masked, kk, carry):
            k_row = pl.multiple_of(kk * BK, BK)
            keys = ks[pl.ds(k_row, BK), :]
            vals = vs[pl.ds(k_row, BK), :]
            if masked:
                ok = allowed_block(seg_q, seg_k_ref[:, pl.ds(k_row, BK)], 0, q_first, k_row, (BQ, BK))
            out = []
            for h in range(3):
                top, total, acc = carry[h]
                lanes = slice((h // 2) * LANES, (h // 2 + 1) * LANES)
                scores = dot_nt(qs[pl.ds(q_row, BQ), h * LANES : (h + 1) * LANES], keys[:, lanes])
                if masked:
                    scores = jnp.where(ok, scores, NEG)
                new_top = jnp.maximum(top, jnp.max(scores, axis=1, keepdims=True))
                probs = jnp.exp(scores - new_top)
                shrink = jnp.exp(top - new_top)
                total = total * shrink + jnp.sum(probs, axis=1, keepdims=True)
                acc = acc * shrink + dot_nn(probs.astype(BF), vals[:, lanes])
                out.append((new_top, total, acc))
            return tuple(out)

        start = tuple(
            (jnp.full((BQ, 1), NEG, F32), jnp.zeros((BQ, 1), F32), jnp.zeros((BQ, LANES), F32))
            for _ in range(3)
        )
        first, full = low_ref[i], full_ref[i]
        last = q_first // BK
        carry = lax.fori_loop(first, full, functools.partial(step, True), start)
        carry = lax.fori_loop(full, last, functools.partial(step, False), carry)
        carry = lax.fori_loop(last, last + BQ // BK, functools.partial(step, True), carry)
        heads = [acc / total for _, total, acc in carry]
        pair = jnp.where(lane_is_low(BQ), heads[0], heads[1]).astype(BF)
        third = heads[2].astype(BF)
        for n in range(BQ // sub):
            block = i * (BQ // sub) + n
            slot, j = tp_rank ^ lax.rem(block, ranks), block // ranks
            o_ref[slot, j, :, 0:128] = pair[n * sub : (n + 1) * sub]
            o_ref[slot, j, :, 128:256] = third[n * sub : (n + 1) * sub]
        for h in range(3):
            top, total, _ = carry[h]
            column = jnp.broadcast_to(top + jnp.log(total), (BQ, LANES))
            lse_ref[i, h] = column.T[0:8]
        return 0

    lax.fori_loop(0, q_len // BQ, q_block, 0)


def attend_back_kernel(
    gathered, q_range, k_range, k_done, more, where_ref, full_ref, high_ref, seg_q_ref, seg_k_ref, o_ref, do_ref, lse_ref, proj_ref, *refs
):
    refs = list(refs)
    kv_ref = refs.pop(0) if gathered else None
    sum_ref = refs.pop(0) if more else None
    dproj_ref = refs.pop(0)
    dkv_ref = refs.pop(0) if gathered else None
    rest_ref = refs.pop(0) if k_done > k_range[0] else None
    qs, ks, vs, kt, dos, dqs, delta = refs
    ranks, steps, sub, _ = proj_ref.shape
    parts = kv_ref.shape[0] if gathered else 1
    tp_rank, part = where_ref[0], where_ref[1]
    q_len = ranks * steps * sub
    scale = 64 ** (-0.5)
    low = lane_is_low(sub)
    q_first, q_end = q_range
    per_q = BQ // sub

    for block, j, rank in pieces((ranks, steps)):
        slot = tp_rank ^ rank
        rows = slice(block * sub, (block + 1) * sub)
        if q_first * per_q <= block < q_end * per_q:
            split_heads((proj_ref[slot, j, :, :HEAD_PAD].astype(F32) * scale).astype(BF), qs, rows, low)
            grad = do_ref[slot, j]
            split_heads(grad, dos, rows, low)
            product = grad.astype(F32) * o_ref[slot, j].astype(F32)
            pair, third = product[:, :LANES].T, product[:, LANES:].T
            lanes = slice(rows.start % BQ, rows.start % BQ + sub)
            for h, part_of in enumerate((pair[:64], pair[64:], third[:64])):
                delta[block // per_q, h : h + 1, lanes] = jnp.sum(part_of, axis=0, keepdims=True)
        for p in range(parts):
            if not k_range[0] * BK <= p * q_len + block * sub < k_range[1] * BK:
                continue
            at = slice(p * q_len + block * sub, p * q_len + (block + 1) * sub)
            both = kv_ref[p, slot, j] if gathered else proj_ref[slot, j, :, HEAD_PAD:]
            ks[at, :] = both[:, :HEAD_PAD]
            vs[at, :] = both[:, HEAD_PAD:]
            kt[at.start // BK, :, at.start % BK : at.start % BK + sub] = both[:, :HEAD_PAD].T
    dqs[...] = jnp.zeros_like(dqs)

    def k_block(kk, _):
        k_row = pl.multiple_of(kk * BK, BK)
        keys = ks[pl.ds(k_row, BK), :]
        vals = vs[pl.ds(k_row, BK), :]
        seg_k = seg_k_ref[pl.ds(k_row, BK), :]

        def step(masked, i, carry):
            q_row = pl.multiple_of(i * BQ, BQ)
            at = pl.ds(q_row, BQ)
            if masked:
                ok = allowed_block(seg_q_ref[i], seg_k, 1, part * q_len + q_row, k_row, (BK, BQ))
            dk, dv = list(carry[0]), list(carry[1])
            for h in range(3):
                t = h // 2
                lanes = slice(t * LANES, (t + 1) * LANES)
                mine = slice(h * LANES, (h + 1) * LANES)
                q_head, do_head = qs[at, mine], dos[at, mine]
                scores = dot_nt(keys[:, lanes], q_head)
                probs = jnp.exp(scores - lse_ref[i, h, 0:1, :])
                if masked:
                    probs = jnp.where(ok, probs, 0.0)
                grad_probs = dot_nt(vals[:, lanes], do_head)
                grad_scores = (probs * (grad_probs - delta[i, h : h + 1, :])).astype(BF)
                dv[t] = dv[t] + dot_nn(probs.astype(BF), do_head)
                dk[t] = dk[t] + dot_nn(grad_scores, q_head)
                rows = slice(h * 64, (h + 1) * 64)
                dqs[i, rows, :] += dot_nn(kt[kk, rows, :], grad_scores)
            return tuple(dk), tuple(dv)

        zero = jnp.zeros((BK, LANES), F32)
        carry = ((zero, zero), (zero, zero))
        if more:
            pieces_in = [sum_ref[pl.ds(k_row, BK), t * LANES : (t + 1) * LANES] for t in range(4)]
            carry = (tuple(pieces_in[:2]), tuple(pieces_in[2:]))
        ahead = kk - part * (q_len // BQ)
        inside = lambda value: jnp.clip(value, q_first, q_end)
        first = inside(ahead)
        diagonal = jnp.where(ahead >= 0, inside(ahead + 1), first)
        full = jnp.maximum(inside(full_ref[kk]), diagonal)
        high = jnp.maximum(inside(high_ref[kk]), full)
        carry = lax.fori_loop(first, diagonal, functools.partial(step, True), carry)
        carry = lax.fori_loop(diagonal, full, functools.partial(step, False), carry)
        carry = lax.fori_loop(full, high, functools.partial(step, True), carry)
        return carry[0] + carry[1]

    def finish(kk, _):
        sums = k_block(kk, 0)
        for n in range(BK // sub):
            block = lax.rem(kk, q_len // BK) * (BK // sub) + n
            slot, j = tp_rank ^ lax.rem(block, ranks), block // ranks
            for t in range(4):
                piece = sums[t][n * sub : (n + 1) * sub].astype(BF)
                lanes = slice(t * LANES, (t + 1) * LANES)
                if gathered:
                    dkv_ref[kk // (q_len // BK), slot, j, :, lanes] = piece
                else:
                    start = HEAD_PAD + t * LANES
                    dproj_ref[slot, j - k_done * BK // (ranks * sub), :, start : start + LANES] = piece
        return 0

    def keep(kk, _):
        sums = k_block(kk, 0)
        for t in range(4):
            rest_ref[pl.ds(pl.multiple_of(kk * BK, BK), BK), t * LANES : (t + 1) * LANES] = sums[t]
        return 0

    if rest_ref is not None:
        lax.fori_loop(k_range[0], k_done, keep, 0)
    lax.fori_loop(k_done, k_range[1], finish, 0)
    for block, j, rank in pieces((ranks, steps)):
        if q_first * per_q <= block < q_end * per_q:
            lanes = slice(block % per_q * sub, (block % per_q + 1) * sub)
            grad = (dqs[block // per_q, :, lanes] * scale).T.astype(BF)
            dproj_ref[tp_rank ^ rank, j - q_first * per_q // ranks, :, :HEAD_PAD] = grad


SMEM = pl.BlockSpec(memory_space=pltpu.SMEM)
VMEM = pl.BlockSpec(memory_space=pltpu.VMEM)
PARAMS = pltpu.CompilerParams(vmem_limit_bytes=VMEM_BYTES)


def attend(where, seg_q, seg_k, proj, keyvals):
    ranks, steps, sub, _ = proj.shape
    gathered = keyvals is not None
    q_len = ranks * steps * sub
    k_len = q_len * (keyvals.shape[0] if gathered else 1)
    q_first, q_last = seg_q[::BQ], seg_q[BQ - 1 :: BQ]
    k_first, k_last = seg_k[::BK], seg_k[BK - 1 :: BK]
    k_index = jnp.arange(k_len // BK)
    bound = where[1] * (q_len // BK) + jnp.arange(q_len // BQ) * (BQ // BK)
    before = k_index[None, :] < bound[:, None]
    first = jnp.sum(before & (k_last[None, :] < q_first[:, None]), axis=1).astype(jnp.int32)
    full = jnp.sum(before & (k_first[None, :] != q_last[:, None]), axis=1).astype(jnp.int32)
    inputs = (proj, keyvals) if gathered else (proj,)
    return pl.pallas_call(
        functools.partial(attend_kernel, gathered),
        out_shape=(
            jax.ShapeDtypeStruct((ranks, steps, sub, HEAD_PAD), BF),
            jax.ShapeDtypeStruct((q_len // BQ, 3, 8, BQ), F32),
        ),
        in_specs=[SMEM] * 3 + [VMEM] * (2 + len(inputs)),
        out_specs=(VMEM, VMEM),
        scratch_shapes=[
            pltpu.VMEM((q_len, 3 * LANES), BF),
            pltpu.VMEM((k_len, HEAD_PAD), BF),
            pltpu.VMEM((k_len, HEAD_PAD), BF),
        ],
        compiler_params=PARAMS,
        cost_estimate=pl.CostEstimate(
            flops=16 * q_len * k_len * 256, bytes_accessed=8 * q_len * 1024, transcendentals=3 * q_len * k_len // 2
        ),
        name="attend",
    )(where, first, jnp.maximum(full, first), seg_q[:, None], seg_k[None, :], *inputs)


def attend_back(where, seg_q, seg_k, proj, keyvals, attended, grad, lse, q_range, k_range, k_done, before=None):
    ranks, steps, sub, _ = proj.shape
    gathered = keyvals is not None
    q_len = ranks * steps * sub
    k_len = q_len * (keyvals.shape[0] if gathered else 1)
    q_first, q_last = seg_q[::BQ], seg_q[BQ - 1 :: BQ]
    k_first, k_last = seg_k[::BK], seg_k[BK - 1 :: BK]
    full = jnp.sum(q_last[None, :] <= k_first[:, None], axis=1).astype(jnp.int32)
    high = jnp.sum(q_first[None, :] <= k_last[:, None], axis=1).astype(jnp.int32)
    inputs = [attended, grad, lse, proj] + ([keyvals] if gathered else []) + ([before] if before is not None else [])
    part_steps = (q_range[1] - q_range[0]) * BQ // (ranks * sub)
    outs = [jax.ShapeDtypeStruct((ranks, part_steps, sub, proj.shape[3] if not gathered else HEAD_PAD), BF)]
    if gathered:
        outs.append(jax.ShapeDtypeStruct(keyvals.shape, BF))
    if k_done > k_range[0]:
        outs.append(jax.ShapeDtypeStruct((k_done * BK, 2 * HEAD_PAD), F32))
    return pl.pallas_call(
        functools.partial(attend_back_kernel, gathered, q_range, k_range, k_done, before is not None),
        out_shape=outs,
        in_specs=[SMEM] * 3 + [VMEM] * (2 + len(inputs)),
        out_specs=[VMEM] * len(outs),
        scratch_shapes=[
            pltpu.VMEM((q_len, 3 * LANES), BF),
            pltpu.VMEM((k_len, HEAD_PAD), BF),
            pltpu.VMEM((k_len, HEAD_PAD), BF),
            pltpu.VMEM((k_len // BK, HEAD_PAD, BK), BF),
            pltpu.VMEM((q_len, 3 * LANES), BF),
            pltpu.VMEM((q_len // BQ, HEAD_PAD, BQ), F32),
            pltpu.VMEM((q_len // BQ, 8, BQ), F32),
        ],
        compiler_params=PARAMS,
        cost_estimate=pl.CostEstimate(
            flops=12 * q_len * k_len * 256, bytes_accessed=16 * q_len * 1024, transcendentals=3 * q_len * k_len // 2
        ),
        name=f"attend_back_{q_range[0]}_{q_range[1]}",
    )(where, full, high, seg_q.reshape(-1, 1, BQ), seg_k[:, None], *inputs)


GELU_A, GELU_B = 0.7978845608028654, 0.044715
ORDER = (0, 2, 1, 3)


def row_mean(values):
    return jnp.mean(values, axis=-1, keepdims=True)


def middle_kernel(
    head_width, x_ref, m0, m1, m2, m3, cot_ref, vec_ref, up0, up1, up2, up3, down_even, down_odd,
    out_ref, gh_ref, do_ref, up_even_ref, up_odd_ref, down_even_ref, down_odd_ref, wout_even_ref, wout_odd_ref, small_ref,
    wu, wd, xhat, rstd, n2, act, gpre, mlp, dn2,
):
    at = pl.program_id(0)
    tokens, width = x_ref.shape
    units = wd.shape[0]
    chunk, wide = tokens, 256
    merged = (m0, m1, m2, m3)
    ups = (up0, up1, up2, up3)
    downs = ((down_even, 0), (down_odd, 0), (down_even, 1), (down_odd, 1))
    bias_row = up0.shape[0] - 16

    @pl.when(at == 0)
    def _():
        gain, shift = vec_ref[0:1, :], vec_ref[1:2, :]
        for t in range(tokens // chunk):
            rows = slice(t * chunk, (t + 1) * chunk)
            hidden = x_ref[rows, :].astype(F32) + vec_ref[2:3, :]
            for s in range(4):
                hidden = hidden + dot_nn(merged[s][rows, :head_width], ups[s][units : units + head_width, :])
            center = hidden - row_mean(hidden)
            scale = lax.rsqrt(row_mean(center * center) + EPS)
            norm = center * scale
            xhat[rows, :] = norm
            rstd[rows, :] = jnp.broadcast_to(scale, (chunk, LANES))
            n2[rows, :] = (norm * gain + shift).astype(BF)
            mlp[rows, :] = hidden + vec_ref[3:4, :]
        dn2[...] = jnp.zeros_like(dn2)
        small_ref[...] = jnp.zeros_like(small_ref)

    for n, s in enumerate(ORDER):

        @pl.when(at == n)
        def _():
            wu[...] = ups[s][...]
            wd[...] = downs[s][0][downs[s][1]]

    slot = (at % 2) * 2 + at // 2
    bias = wu[bias_row : bias_row + 16, :][0:1].astype(F32)

    def tokens_step(t, total):
        rows = pl.ds(pl.multiple_of(t * chunk, chunk), chunk)
        pre = dot_nn(n2[rows, :], wu[:units, :]) + bias
        square = pre * pre
        tanh = jnp.tanh(GELU_A * pre * (1.0 + GELU_B * square))
        half = 0.5 * (1.0 + tanh)
        activ = (pre * half).astype(BF)
        act[rows, :] = activ
        mlp[rows, :] += dot_nn(activ, wd[...])
        slope = half + (0.5 * GELU_A) * pre * (1.0 - tanh * tanh) * (1.0 + (3.0 * GELU_B) * square)
        grad = (dot_nt(cot_ref[rows, :], wd[...]) * slope).astype(BF)
        gpre[rows, :] = grad
        dn2[rows, :] += dot_nt(grad, wu[:units, :])
        return total + jnp.sum(grad.astype(F32), axis=0, keepdims=True)

    total = lax.fori_loop(0, tokens // chunk, tokens_step, jnp.zeros((1, units), F32))
    for s in range(4):

        @pl.when(slot == s)
        def _():
            small_ref[4 + s : 5 + s, :] = total

    def weight_grads(up_out, down_out):
        for c in range(units // wide):
            rows = slice(c * wide, (c + 1) * wide)
            down_out[0, rows, :] = dot_tn(act[:, rows], cot_ref[...]).astype(BF)
        for c in range(width // wide):
            rows = slice(c * wide, (c + 1) * wide)
            up_out[0, rows, :] = dot_tn(n2[:, rows], gpre[...]).astype(BF)

    @pl.when(at < 2)
    def _():
        weight_grads(up_even_ref, down_even_ref)

    @pl.when(at >= 2)
    def _():
        weight_grads(up_odd_ref, down_odd_ref)

    @pl.when(at == 3)
    def _():
        gain = vec_ref[0:1, :]
        for t in range(tokens // chunk):
            rows = slice(t * chunk, (t + 1) * chunk)
            out_ref[rows, :] = mlp[rows, :].astype(BF)
            grad, norm, cot = dn2[rows, :], xhat[rows, :], cot_ref[rows, :].astype(F32)
            gg = grad * gain
            inner = gg - row_mean(gg) - norm * row_mean(gg * norm)
            hidden = cot + rstd[rows, 0:1] * inner
            gh_ref[rows, :] = hidden
            small_ref[0:1, :] += jnp.sum(grad * norm, axis=0, keepdims=True)
            small_ref[1:2, :] += jnp.sum(grad, axis=0, keepdims=True)
            small_ref[2:3, :] += jnp.sum(hidden, axis=0, keepdims=True)
            small_ref[3:4, :] += jnp.sum(cot, axis=0, keepdims=True)
            branch = hidden.astype(BF)
            gpre[rows, :width] = branch
            for s in range(4):
                back = dot_nt(branch, ups[s][units : units + head_width, :]).astype(BF)
                do_ref[s, rows, :head_width] = back
                do_ref[s, rows, head_width:] = jnp.zeros((chunk, HEAD_PAD - head_width), BF)
        for s in range(4):
            target = (wout_even_ref, wout_odd_ref)[s % 2]
            target[s // 2] = dot_tn(merged[s][...], gpre[:, :width])[:head_width].astype(BF)


def middle(head_width, x_rows, merged, cot_rows, vectors, ups, down_even, down_odd):
    tokens, width = x_rows.shape
    units = down_even.shape[1]
    whole = lambda shape: pl.BlockSpec(shape, lambda at: (0,) * len(shape))
    early = lambda at: (jnp.minimum(at, 1), 0, 0)
    late = lambda at: (jnp.maximum(at - 2, 0), 0, 0)
    once = lambda value: pl.BlockSpec(value.shape, lambda at: (0,) * value.ndim, pipeline_mode=pl.Buffered(1))
    struct = jax.ShapeDtypeStruct
    return pl.pallas_call(
        functools.partial(middle_kernel, head_width),
        grid=(4,),
        out_shape=(
            struct((tokens, width), BF),
            struct((tokens, width), F32),
            struct((4, tokens, HEAD_PAD), BF),
            struct((2, width, units), BF),
            struct((2, width, units), BF),
            struct((2, units, width), BF),
            struct((2, units, width), BF),
            struct((2, head_width, width), BF),
            struct((2, head_width, width), BF),
            struct((8, width), F32),
        ),
        in_specs=[whole((tokens, width))]
        + [whole((tokens, HEAD_PAD))] * 4
        + [whole((tokens, width)), whole(vectors.shape)]
        + [once(value) for value in (*ups, down_even, down_odd)],
        out_specs=(
            whole((tokens, width)),
            whole((tokens, width)),
            whole((4, tokens, HEAD_PAD)),
            pl.BlockSpec((1, width, units), early),
            pl.BlockSpec((1, width, units), late),
            pl.BlockSpec((1, units, width), early),
            pl.BlockSpec((1, units, width), late),
            whole((2, head_width, width)),
            whole((2, head_width, width)),
            whole((8, width)),
        ),
        scratch_shapes=[
            pltpu.VMEM(ups[0].shape, BF),
            pltpu.VMEM((units, width), BF),
            pltpu.VMEM((tokens, width), F32),
            pltpu.VMEM((tokens, LANES), F32),
            pltpu.VMEM((tokens, width), BF),
            pltpu.VMEM((tokens, units), BF),
            pltpu.VMEM((tokens, units), BF),
            pltpu.VMEM((tokens, width), F32),
            pltpu.VMEM((tokens, width), F32),
        ],
        compiler_params=PARAMS,
        cost_estimate=pl.CostEstimate(
            flops=60 * tokens * width * units, bytes_accessed=12 * units * width, transcendentals=4 * tokens * units
        ),
        name="middle",
    )(x_rows, *merged, cot_rows, vectors, *ups, down_even, down_odd)


def norm_parts(values):
    center = values - row_mean(values)
    rstd = lax.rsqrt(row_mean(center * center) + EPS)
    return center * rstd, rstd


def norm_back(xhat, rstd, gain, grad):
    gg = grad * gain
    return rstd * (gg - row_mean(gg) - xhat * row_mean(gg * xhat))


def pick(array, index, axis):
    return lax.dynamic_index_in_dim(array, index, axis, keepdims=False)


def on_device(
    block_in, segments, ln1_gain, ln1_shift, w_qkv, b_qv, w_out, b_out, ln2_gain, ln2_shift, w_up, b_up, w_down, b_down, cotangent
):
    seqs, sub, width = block_in.shape
    ranks, fsdp, ctx_size = lax.axis_size("tp"), lax.axis_size("fsdp"), lax.axis_size("ctx")
    parts = ctx_size // seqs
    tp_rank, ctx_rank, fsdp_rank = lax.axis_index("tp"), lax.axis_index("ctx"), lax.axis_index("fsdp")
    heads = b_qv.shape[0]
    head_width = heads * 64
    own = seqs * sub
    tokens = ranks * own
    shard = ln1_gain.shape[0]

    vectors = [ln1_gain, ln1_shift, b_out, ln2_gain, ln2_shift, b_down, b_qv.reshape(-1), b_up.reshape(-1)]
    x_blocks, vectors = to_sequence(block_in, vectors)
    down_far = swap(w_down, "tp", 2)
    x_blocks, down_far = lax.optimization_barrier((x_blocks, down_far))
    x_own = x_blocks.reshape(own, width)

    rows = jnp.stack([jnp.pad(v, (0, shard - v.shape[0])) for v in vectors])
    (small,) = gather_fsdp([rows[None]], 0)
    (qkv_mat,) = gather_fsdp([w_qkv], 1)
    gain_one, shift_one, out_bias, gain_two, shift_two, down_bias = (
        small[:, n].reshape(-1).astype(F32) for n in range(6)
    )
    qv_bias = small[:, 6, : b_qv.size].reshape((fsdp,) + b_qv.shape)
    qv_bias = qv_bias.transpose(1, 0, 2).reshape(heads, -1).astype(F32)
    up_bias = small[:, 7, : b_up.size].reshape((fsdp,) + b_up.shape).transpose(1, 0, 2).reshape(1, -1)
    extra = HEAD_PAD - head_width
    qkv_pad = jnp.pad(qkv_mat, ((0, 0), (0, extra), (0, 0))).reshape(3 * HEAD_PAD, width)
    bias_rows = jnp.stack(
        [qv_bias[:, :64].reshape(-1), jnp.zeros((head_width,), F32), qv_bias[:, 64:].reshape(-1)]
    )
    qkv_bias = jnp.pad(bias_rows, ((0, 0), (0, extra))).reshape(-1)

    up_rows, out_rows = gather_fsdp([w_up, w_out], 0)
    up_own = jnp.concatenate([up_rows, out_rows, jnp.pad(up_bias, ((0, 15), (0, 0)))], axis=0)
    down_pair = jnp.stack([w_down, down_far])

    x_float = x_own.astype(F32)
    xhat_one, rstd_one = norm_parts(x_float)
    normed_own = (xhat_one * gain_one + shift_one).astype(BF)
    normed_own, cotangent = lax.optimization_barrier((normed_own, cotangent))
    cot_rows, _ = to_sequence(cotangent)
    normed_one = jnp.concatenate(gather_tp(normed_own), axis=0)
    normed_one, up_own, down_pair, cot_rows = lax.optimization_barrier(
        (normed_one, up_own, down_pair, cot_rows)
    )
    cot_rows = cot_rows.reshape(own, width)
    proj = (dot_nt(normed_one, qkv_pad) + qkv_bias).astype(BF).reshape(ranks, seqs, sub, 3 * HEAD_PAD)
    up_side = swap(up_own, "tp", 1)
    keyvals = None
    groups = [[g * parts + p for p in range(parts)] for g in range(ctx_size // parts)]
    if parts > 1:
        keyvals = lax.all_gather(
            proj[None, ..., HEAD_PAD:], "ctx", axis=0, tiled=True, axis_index_groups=groups
        )
    seq_rank, part = ctx_rank // parts, ctx_rank % parts
    where = jnp.stack([tp_rank, part]).astype(jnp.int32)
    seg_k = pick(segments, seq_rank, 0)
    seg_q = lax.dynamic_slice_in_dim(seg_k, part * tokens, tokens, 0)
    attended, lse = attend(where, seg_q, seg_k, proj, keyvals)

    up_far = swap(up_own, "tp", 2)
    (down_even,) = gather_fsdp([down_pair], 1)
    attended, up_far, up_side, down_even = lax.optimization_barrier(
        (attended, up_far, up_side, down_even)
    )
    ups = [up_own, up_side, up_far, swap(up_far, "tp", 1)]
    down_odd = swap(down_even, "tp", 1)

    slots = attended.reshape(ranks, own, HEAD_PAD)
    merged = [slots[0]] + [swap(slots[s], "tp", s) for s in range(1, ranks)]
    vecs = jnp.stack([gain_two, shift_two, out_bias, down_bias])
    vecs = jnp.pad(vecs, ((0, 4), (0, 0)))
    (
        block_out, grad_hidden, grad_slots, up_even, up_odd, down_even_g, down_odd_g, out_even, out_odd, sums,
    ) = middle(head_width, x_own, merged, cot_rows, vecs, ups, down_even, down_odd)

    up_got, out_got = swap(up_odd, "tp", 1), swap(out_odd, "tp", 1)
    up_near = [
        jnp.concatenate([add_low(up_even[n], up_got[n]), add_low(out_even[n], out_got[n])])
        for n in range(2)
    ]
    down_near = add_low(down_even_g, swap(down_odd_g, "tp", 1))
    grad_slots = [grad_slots[s] for s in range(ranks)]
    grad_slots[1], up_near, down_near = lax.optimization_barrier((grad_slots[1], up_near, down_near))
    grad_slots = [grad_slots[0]] + [swap(grad_slots[s], "tp", s) for s in range(1, ranks)]
    grad_attended = jnp.stack(grad_slots).reshape(ranks, seqs, sub, HEAD_PAD)
    grad_attended, up_near, down_near, block_out = lax.optimization_barrier(
        (grad_attended, up_near, down_near, block_out)
    )
    out_blocks = from_sequence(block_out.reshape(seqs, sub, width))

    up_mid = add_low(up_near[0], swap(up_near[1], "tp", 2))
    down_mid = scatter_fsdp(down_near.reshape(2, fsdp, -1, width).transpose(1, 0, 2, 3))

    def project_back(half):
        return dot_nn(half.reshape(-1, 3 * HEAD_PAD), qkv_pad).astype(BF).reshape(ranks, -1, width)

    q_blocks = tokens // BQ
    back = functools.partial(attend_back, where, seg_q, seg_k, proj, keyvals, attended)
    if parts > 1:
        dq, dkv = back(grad_attended, lse, (0, q_blocks), (0, parts * q_blocks), 0)
        dkv = lax.psum_scatter(
            dkv, "ctx", scatter_dimension=0, tiled=True, axis_index_groups=groups
        )
        halves = [jnp.concatenate([dq, dkv.reshape(ranks, seqs, sub, 2 * HEAD_PAD)], axis=-1)]
        edges = [0, seqs]
    else:
        mid = q_blocks // 2
        high, rest = back(grad_attended, lse, (mid, q_blocks), (0, q_blocks), mid)
        rest, high, up_mid, down_mid, out_blocks = lax.optimization_barrier(
            (rest, high, up_mid, down_mid, out_blocks)
        )
        high_rows = project_back(high)
        rest, high_rows = lax.optimization_barrier((rest, high_rows))
        (low,) = back(grad_attended, lse, (0, mid), (0, mid), 0, rest)
        halves = [low, high]
        edges = [0, mid * BQ // (ranks * sub), seqs]

    up_last = scatter_pair(up_mid, width)
    down_last = add_low(down_mid[0], swap(down_mid[1], "tp", 2))
    if parts == 1:
        halves[0], high_rows, up_last, down_last = lax.optimization_barrier(
            (halves[0], high_rows, up_last, down_last)
        )
        slots = [project_back(halves[0]), high_rows]
    else:
        slots = [project_back(halves[0])]
    grad_rows = [near_sums([rows[s] for s in range(ranks)]) for rows in reversed(slots)][::-1]
    quarter = ctx_reduce(jnp.concatenate([up_last, down_last], axis=0))
    cuts = [0, w_up.shape[0], w_up.shape[0] + w_out.shape[0], w_up.shape[0] + w_out.shape[0] + w_down.shape[0]]
    halves, grad_rows = lax.optimization_barrier((halves, grad_rows))

    normed_all = normed_one.reshape(ranks, seqs, sub, width)
    grad_qkv, grad_normed, bias_sum = 0.0, [], 0.0
    for n in reversed(range(len(halves))):
        rows = halves[n].reshape(-1, 3 * HEAD_PAD)
        grad_normed.insert(0, far_sum(*grad_rows[n]))
        seen = normed_all[:, edges[n] : edges[n + 1]].reshape(-1, width)
        grad_qkv = grad_qkv + dot_tn(rows, seen)
        bias_sum = bias_sum + jnp.sum(rows.astype(F32), axis=0)
    grad_normed_one = jnp.concatenate(grad_normed, axis=0)
    grad_x = grad_hidden + norm_back(xhat_one, rstd_one, gain_one, grad_normed_one)
    grad_x = grad_x.astype(BF)
    ln1_sums = jnp.stack([jnp.sum(grad_normed_one * xhat_one, axis=0), jnp.sum(grad_normed_one, axis=0)])
    grad_qkv = grad_qkv.reshape(3, HEAD_PAD, width)[:, :head_width].astype(BF)
    qkv_shard = scatter_fsdp(grad_qkv.reshape(3, fsdp, -1, width).transpose(1, 0, 2, 3))
    qkv_rows, quarter = lax.optimization_barrier((qkv_shard.reshape(-1, width), quarter))
    quarter = ctx_spread_far(quarter, cuts[3])
    grad_x, quarter = lax.optimization_barrier((grad_x, quarter))
    grad_blocks = from_sequence(grad_x.reshape(seqs, sub, width))
    total = ctx_spread(quarter, cuts[3])
    sum_up, sum_out, sum_down = (total[cuts[n] : cuts[n + 1]] for n in range(3))
    sum_qkv = ctx_spread_far(ctx_reduce(qkv_rows), qkv_rows.shape[0])
    sum_qkv = ctx_spread(sum_qkv, qkv_rows.shape[0]).reshape(w_qkv.shape)

    bias_sum = bias_sum.reshape(3, HEAD_PAD)[:, :head_width].reshape(3, heads, 64)
    bias_rows = jnp.concatenate([bias_sum[0], bias_sum[2]], axis=1)
    bias_all = lax.dynamic_update_slice(
        jnp.zeros((ranks * heads, 128), F32), bias_rows, (tp_rank * heads, 0)
    )
    up_bias_all = jnp.zeros((ranks, width), F32)
    for s in range(ranks):
        up_bias_all = lax.dynamic_update_slice(up_bias_all, sums[4 + s : 5 + s], (tp_rank ^ s, 0))
    late = jnp.concatenate(
        [sums[:4].reshape(-1, LANES), up_bias_all.reshape(-1, LANES), ln1_sums.reshape(-1, LANES), bias_all]
    )
    late = butterfly(butterfly(late, "tp"), "fsdp")
    late, grad_blocks = lax.optimization_barrier((late, grad_blocks))
    late = butterfly(late, "ctx")
    late_rows = late[: 10 * width // LANES].reshape(10, fsdp, shard)

    def mine_bias(rows, like):
        rows = lax.dynamic_slice_in_dim(rows, tp_rank * like.shape[0], like.shape[0], 0)
        return lax.dynamic_slice_in_dim(rows, fsdp_rank * like.shape[1], like.shape[1], 1)

    vector_sums = pick(late_rows, fsdp_rank, 1)
    sum_qv_bias = mine_bias(late[10 * width // LANES :], b_qv)
    up_bias_rows = late[4 * width // LANES : 8 * width // LANES]
    sum_up_bias = mine_bias(up_bias_rows.reshape(ranks * b_up.shape[0], -1), b_up)
    return (
        out_blocks, grad_blocks, vector_sums[8], vector_sums[9], sum_qkv, sum_qv_bias, sum_out, vector_sums[2],
        vector_sums[0], vector_sums[1], sum_up, sum_up_bias, sum_down, vector_sums[3],
    )


def solution(mesh):
    rows = P("fsdp", ("ctx", "tp"), None)
    vector = P("fsdp")
    out_rows = P(("tp", "fsdp"), None)
    qkv_rows = P(None, ("tp", "fsdp"), None)
    bias = P("tp", "fsdp")
    weights = (
        vector, vector, qkv_rows, bias, out_rows, vector, vector, vector, P("fsdp", "tp"), bias, out_rows, vector,
    )
    return jax.shard_map(
        on_device,
        mesh=mesh,
        in_specs=(rows, P("fsdp", None)) + weights + (rows,),
        out_specs=(rows, rows) + weights,
        check_vma=False,
    )
```
